32 devices in a mesh: grp: 2 (over y), tgt: 4 (over z), qry: 2 (over x), rep: 2 (over core).
Axes of the slice: x: 2, y: 2, z: 4, core: 2. Of those that a mesh axis runs over, the one named last changes fastest.
Arguments:
- query_res: bfloat16 [16, 256, 1280], P(('grp', 'tgt', 'qry'), None, 'rep'), parts along dimension 0, may hold values from -100 to 100
- target_res: bfloat16 [16, 128, 1280], P(('grp', 'tgt'), None, 'rep'), parts along dimension 0, may hold values from -50 to 50
- target_len: int32 [16], P('grp'), parts along dimension 0, may hold values from 64 to 128
- hits: int32 [16, 28], P(('grp', 'tgt', 'qry')), parts along dimension 0, may hold values from 0 to 7, as said below
- sharpness: float32 [16], P(('grp', 'tgt', 'qry')), parts along dimension 0, may hold values from 0.4 to 30
- query_pool: float32 [16, 1280], P(('grp', 'tgt', 'qry')), parts along dimension 0, may hold values from -41 to 41
- target_pool: float32 [16, 1280], P(('grp', 'tgt')), parts along dimension 0, may hold values from -5.1 to 5.1
Outputs:
- profile: bfloat16 [16, 256, 1280], P(('grp', 'tgt', 'qry'), None, 'rep'), parts along dimension 0
- posterior: float32 [16, 8], P(('grp', 'tgt', 'qry')), parts along dimension 0
The draws below stay inside these ranges and needn't reach their ends.
There are 2 independent parts, one for each index of `grp`. The reference program is written for one: setup_inputs(seed, part) draws one part's arguments, and reference() takes and returns one part's arrays. A program takes and returns all parts, laid end to end along the dimension named above; each array names one. Nothing has to cross between parts.
Inputs may be any that keep to these rules, and one draw needn't show every extreme that they name: Each row lists 28 ids of targets hit by that query; ids may repeat. Target t is held by index t // 2 of tgt. In each aligned block of 1 row (the queries of one device), at most 14 hits name targets held by one index of tgt, and in every block some index is named exactly 14 times.
All inputs are finite; a program needn't handle non-finite values.
Results may differ from the reference program's by a relative error of at most 0.0051.
Values may be sent and summed in bfloat16 or wider, within the bound.
No kernel may reach another device: no remote copies, remote signals or barrier semaphores. Data moves between devices by JAX's collectives and lax.ppermute only.
A program may use at most 64 MiB of HBM per device.

```python
import math
import jax
import jax.numpy as jnp
from jax import lax

D = 1280
LQ = 256
LT = 128
TDEV = 2
QDEV = 1
HQ = 28
NQ = 8
NT = 8
CAP = 14
N_TGT = 4
N_QRY = 2


def hit_block(block_key):
    slot_count = N_TGT * CAP
    key_busy, key_order, key_local, key_shuffle = jax.random.split(block_key, 4)
    busiest = jax.random.randint(key_busy, (), 0, N_TGT)
    owner_of = jnp.arange(slot_count, dtype=jnp.int32) // CAP
    priority = jax.random.permutation(key_order, slot_count).astype(jnp.int32)
    ranking = priority + jnp.where(owner_of == busiest, slot_count, 0)
    picked = jnp.argsort(-ranking)[:QDEV * HQ]
    owners = owner_of[picked]
    local_ids = jax.random.randint(key_local, (QDEV * HQ,), 0, TDEV)
    return jax.random.permutation(key_shuffle, owners * TDEV + local_ids)


def common_parts(key):
    query_count = QDEV * N_TGT * N_QRY
    target_count = TDEV * N_TGT
    block_keys = jax.random.split(jax.random.fold_in(key, 11), N_TGT * N_QRY)
    hit_ids = jax.vmap(hit_block)(block_keys).reshape(query_count, HQ)
    base_targets = jnp.clip(jax.random.normal(jax.random.fold_in(key, 12), (target_count, LT, D)), -5.0, 5.0)
    aligned = jax.random.randint(jax.random.fold_in(key, 13), (query_count,), 0, 4) == 0
    base_library = jnp.clip(jax.random.normal(jax.random.fold_in(key, 14), (target_count, D)), -5.0, 5.0)
    return (hit_ids, base_targets, aligned, base_library)


def shaped_targets(key, base_targets, spread):
    target_count = base_targets.shape[0]
    block_scale = jnp.exp(jax.random.uniform(jax.random.fold_in(key, 22), (target_count, 1, 1), minval=-math.log(10.0), maxval=math.log(10.0)))
    row_scale = jnp.exp(spread * jax.random.uniform(jax.random.fold_in(key, 21), (target_count, base_targets.shape[1], 1)))
    scaled = base_targets * (block_scale * row_scale)
    second = scaled[:, 1, :]
    return scaled.at[:, 1, :].set(second)


def shaped_library(key, base_library):
    evens = base_library[0::2]
    odds = base_library[1::2]
    return jnp.stack([evens, odds], axis=1).reshape(base_library.shape)


def draw_hits(key, part):
    hit_ids, base_targets, aligned, base_library = common_parts(key)
    return hit_ids


def draw_target_res(key, part):
    hit_ids, base_targets, aligned, base_library = common_parts(key)
    targets = shaped_targets(key, base_targets, 0.0)
    return targets.astype(jnp.bfloat16)


def shaped_queries(own_key, targets, hit_ids, aligned, pull):
    query_count = hit_ids.shape[0]
    base_rows = jnp.clip(jax.random.normal(jax.random.fold_in(own_key, 1), (query_count, LQ, D)), -5.0, 5.0)
    queries = base_rows
    anchor = targets[hit_ids[:, 0], 0]
    factor = jax.random.uniform(jax.random.fold_in(own_key, 3), (query_count, LQ, 1), minval=1.0, maxval=2.0)
    chosen_rows = (jnp.arange(LQ) < 4)[None, :, None] & aligned[:, None, None] & (pull > 0.5)
    return jnp.where(chosen_rows, factor * anchor[:, None, :], queries)


def draw_query_res(key, part):
    hit_ids, base_targets, aligned, base_library = common_parts(key)
    own_key = jax.random.fold_in(key, 4)
    queries = shaped_queries(own_key, base_targets, hit_ids, aligned, 0.0)
    return queries.astype(jnp.bfloat16)


def draw_sharpness(key, part):
    own_key = jax.random.fold_in(key, 5)
    spread = jax.random.uniform(own_key, (NQ,))
    high_end = jnp.log(30.0)
    low_end = jnp.log(0.4) + jnp.zeros((NQ,))
    return jnp.exp(low_end + (high_end - low_end) * spread).astype(jnp.float32)


def draw_target_pool(key, part):
    hit_ids, base_targets, aligned, base_library = common_parts(key)
    library = shaped_library(key, base_library)
    return library.astype(jnp.float32)


def hit_lift(library, hit_ids, strength):
    named = jnp.any(hit_ids[:, :, None] == jnp.arange(NT)[None, None, :], axis=1)
    coarse = jnp.floor(library * 1024.0) / 1024.0
    summed = jnp.sum(jnp.where(named[:, :, None], coarse[None, :, :], 0.0), axis=1)
    return strength / math.sqrt(HQ) * summed


def draw_query_pool(key, part):
    hit_ids, base_targets, aligned, base_library = common_parts(key)
    own_key = jax.random.fold_in(key, 6)
    noise_rows = 0.5 * jnp.clip(jax.random.normal(jax.random.fold_in(own_key, 1), (NQ, D)), -5.0, 5.0)
    library = shaped_library(key, base_library)
    rows_out = noise_rows + hit_lift(library, hit_ids, 0.9)
    return rows_out.astype(jnp.float32)


def place_ends(drawn, key, low, largest):
    dims = drawn.shape
    index_at = [jax.random.randint(jax.random.fold_in(key, axis), (), 0, dims[axis]) for axis in range(len(dims))]
    drawn = drawn.at[tuple(index_at)].set(low)
    longest = dims.index(max(dims))
    index_at[longest] = (index_at[longest] + 1) % dims[longest]
    return drawn.at[tuple(index_at)].set(largest)


def setup_inputs(seed: int = 0, part: int = 0) -> dict:
    splits = jax.random.split(jax.random.key(seed), 8)
    part_keys = jax.random.split(jax.random.fold_in(splits[7], part), 8)
    query_res = draw_query_res(jax.random.fold_in(jax.random.fold_in(splits[7], part), 71), part)
    target_res = draw_target_res(jax.random.fold_in(jax.random.fold_in(splits[7], part), 71), part)
    target_len = place_ends(jax.random.randint(part_keys[2], (NT,), LT // 2, LT + 1), jax.random.fold_in(part_keys[2], 1), LT // 2, LT).astype(jnp.int32)
    hits = draw_hits(jax.random.fold_in(jax.random.fold_in(splits[7], part), 71), part)
    sharpness = draw_sharpness(jax.random.fold_in(jax.random.fold_in(splits[7], part), 71), part)
    query_pool = draw_query_pool(jax.random.fold_in(jax.random.fold_in(splits[7], part), 71), part)
    target_pool = draw_target_pool(jax.random.fold_in(jax.random.fold_in(splits[7], part), 71), part)
    return {"query_res": query_res, "target_res": target_res, "target_len": target_len, "hits": hits, "sharpness": sharpness, "query_pool": query_pool, "target_pool": target_pool}


def softmax_rows(logits):
    highest = lax.optimization_barrier(jnp.max(logits, axis=-1, keepdims=True))
    raised = jnp.exp(logits - highest)
    return raised / lax.optimization_barrier(jnp.sum(raised, axis=-1, keepdims=True))

def weigh_alignment(similar, lengths, sharpness, hit_weight):
    target_rows = similar.shape[-1]
    inside = jnp.arange(target_rows)[None, None, None, :] < lengths[:, :, None, None]
    counted = lengths[:, :, None, None].astype(jnp.float32)
    row_mean = lax.optimization_barrier(jnp.sum(jnp.where(inside, similar, 0.0), axis=-1, keepdims=True)) / counted
    row_diff = similar - row_mean
    row_var = lax.optimization_barrier(jnp.sum(jnp.where(inside, row_diff * row_diff, 0.0), axis=-1, keepdims=True)) / counted
    row_score = row_diff / jnp.sqrt(row_var + 1e-05)
    column_mean = lax.optimization_barrier(jnp.mean(similar, axis=2, keepdims=True))
    column_diff = similar - column_mean
    column_var = lax.optimization_barrier(jnp.mean(column_diff * column_diff, axis=2, keepdims=True))
    column_score = column_diff / jnp.sqrt(column_var + 1e-05)
    scores = sharpness[:, None, None, None] * (0.5 * (row_score + column_score))
    scores = jnp.where(inside, scores, -jnp.inf)
    alignment = softmax_rows(scores)
    return (hit_weight[:, :, None, None] * alignment).astype(jnp.bfloat16)

def reference(query_res, target_res, target_len, hits, sharpness, query_pool, target_pool):
    model_width = query_pool.shape[1]
    logits = jnp.dot(query_pool, target_pool.T, precision=lax.Precision.HIGHEST) / math.sqrt(model_width)
    posterior = softmax_rows(logits)
    matches = hits[:, :, None] == jnp.arange(target_pool.shape[0])[None, None, :]
    hit_weight = softmax_rows(lax.optimization_barrier(jnp.sum(jnp.where(matches, logits[:, None, :], 0.0), axis=-1)))
    lengths = lax.optimization_barrier(jnp.sum(jnp.where(matches, target_len[None, None, :], 0), axis=-1))

    def per_query(position):
        chosen = jnp.take(target_res, hits[position], axis=0).astype(jnp.float32)
        query_rows = query_res[position].astype(jnp.float32)
        similar = jnp.einsum('id,hjd->hij', query_rows, chosen) / math.sqrt(model_width)
        weighted = weigh_alignment(similar[None], lengths[position][None], sharpness[position][None], hit_weight[position][None])[0]
        return jnp.einsum('hij,hjd->id', weighted.astype(jnp.float32), chosen).astype(jnp.bfloat16)
    profile = lax.map(per_query, jnp.arange(hits.shape[0]))
    return (profile, posterior)
```

```python
import functools
import math

import jax
import jax.numpy as jnp
from jax import lax
from jax.experimental import pallas as pl
from jax.experimental.pallas import tpu as pltpu
from jax.sharding import PartitionSpec as P

VMEM_BYTES = 48 * 1024 * 1024


def softmax_rows(logits):
    highest = jnp.max(logits, axis=-1, keepdims=True)
    raised = jnp.exp(logits - highest)
    return raised / jnp.sum(raised, axis=-1, keepdims=True)


def weigh_alignment(similar, lengths, sharpness, hit_weight):
    target_rows = similar.shape[-1]
    inside = jnp.arange(target_rows)[None, None, None, :] < lengths[:, :, None, None]
    counted = lengths[:, :, None, None].astype(jnp.float32)
    row_mean = jnp.sum(jnp.where(inside, similar, 0.0), axis=-1, keepdims=True) / counted
    row_diff = similar - row_mean
    row_var = jnp.sum(jnp.where(inside, row_diff * row_diff, 0.0), axis=-1, keepdims=True) / counted
    row_score = row_diff / jnp.sqrt(row_var + 1e-05)
    column_mean = jnp.mean(similar, axis=2, keepdims=True)
    column_diff = similar - column_mean
    column_var = jnp.mean(column_diff * column_diff, axis=2, keepdims=True)
    column_score = column_diff / jnp.sqrt(column_var + 1e-05)
    scores = sharpness[:, None, None, None] * (0.5 * (row_score + column_score))
    scores = jnp.where(inside, scores, -jnp.inf)
    alignment = softmax_rows(scores)
    return (hit_weight[:, :, None, None] * alignment).astype(jnp.bfloat16)


def plan_slots(flat_hits, owned_targets, tgt_count, capacity):
    owners = flat_hits // owned_targets
    local_ids = flat_hits % owned_targets
    matched = owners[:, None] == jnp.arange(tgt_count)[None, :]
    earlier = jnp.cumsum(matched.astype(jnp.int32), axis=0) - 1
    rank_in = jnp.sum(jnp.where(matched, earlier, 0), axis=1)
    slot_of = owners * capacity + rank_in
    placed = slot_of[:, None] == jnp.arange(tgt_count * capacity)[None, :]
    wanted = jnp.sum(jnp.where(placed, local_ids[:, None], 0), axis=0).reshape(tgt_count, capacity)
    return (wanted, slot_of)


def fetch_shares(target_res, flat_hits, capacity):
    tgt_count = lax.axis_size("tgt")
    owned_targets, target_rows, width = target_res.shape
    wanted, slot_of = plan_slots(flat_hits, owned_targets, tgt_count, capacity)
    requested = lax.all_to_all(wanted, "tgt", split_axis=0, concat_axis=0, tiled=True)
    outgoing = jnp.take(target_res, requested.reshape(tgt_count * capacity), axis=0)
    outgoing = outgoing.reshape(tgt_count, capacity, target_rows, width)
    arrived = lax.all_to_all(outgoing, "tgt", split_axis=0, concat_axis=0, tiled=True)
    return jnp.take(arrived.reshape(tgt_count * capacity, target_rows, width), slot_of, axis=0)


def per_device_by_hit(query_res, target_res, target_len, hits, sharpness, query_pool, target_pool):
    tgt_count = lax.axis_size("tgt")
    query_count = query_res.shape[0]
    target_rows = target_res.shape[1]
    hit_count = hits.shape[1]
    pair_count = query_count * hit_count
    model_width = query_pool.shape[1]
    capacity = max(2, (2 * pair_count + tgt_count - 1) // tgt_count)
    library = lax.all_gather(target_pool, "tgt", axis=0, tiled=True)
    logits = jnp.dot(query_pool, library.T, precision=lax.Precision.HIGHEST) / math.sqrt(
        model_width
    )
    posterior = softmax_rows(logits)
    matches = hits[:, :, None] == jnp.arange(library.shape[0])[None, None, :]
    hit_weight = softmax_rows(jnp.sum(jnp.where(matches, logits[:, None, :], 0.0), axis=-1))
    lengths = jnp.sum(jnp.where(matches, target_len[None, None, :], 0), axis=-1)
    half_width = query_res.shape[2]
    chosen = fetch_shares(target_res, hits.reshape(pair_count), capacity)
    chosen = chosen.reshape(query_count, hit_count, target_rows, half_width)
    partial_sim = jnp.einsum(
        "qid,qhjd->qhij", query_res, chosen, preferred_element_type=jnp.float32
    ) / math.sqrt(model_width)
    similar = lax.psum(partial_sim, "rep")
    weighted = weigh_alignment(similar, lengths, sharpness, hit_weight)
    profile = jnp.einsum("qhij,qhjd->qid", weighted, chosen, preferred_element_type=jnp.float32)
    return (profile.astype(jnp.bfloat16), posterior)


def partial_kernel(*refs):
    query, blocks, out = refs[0], refs[1:-1], refs[-1]
    rows = 0
    for block in blocks:
        out[:, rows : rows + block.shape[0]] = lax.dot_general(
            query[...], block[...], (((1,), (1,)), ((), ())), preferred_element_type=jnp.float32
        )
        rows += block.shape[0]


def partial_similar(query, blocks):
    rows = sum(block.shape[0] for block in blocks)
    cost = pl.CostEstimate(
        flops=2 * query.shape[0] * rows * query.shape[1],
        bytes_accessed=2 * (query.size + rows * query.shape[1]) + 4 * query.shape[0] * rows,
        transcendentals=0,
    )
    return pl.pallas_call(
        partial_kernel,
        out_shape=jax.ShapeDtypeStruct((query.shape[0], rows), jnp.float32),
        cost_estimate=cost,
        compiler_params=pltpu.CompilerParams(vmem_limit_bytes=VMEM_BYTES),
    )(query, *blocks)


def align_kernel(groups, target_rows, target_count, *refs):
    slot_ref, len_ref, sharp_ref, hits_ref, pool_ref = refs[:5]
    libs = refs[5 : 5 + groups]
    mine = refs[5 + groups : 5 + 2 * groups]
    other = refs[5 + 2 * groups : 5 + 3 * groups]
    blocks = refs[5 + 3 * groups : 5 + 3 * groups + target_count]
    profile_ref, posterior_ref, weight_ref = refs[5 + 3 * groups + target_count :]
    width = pool_ref.shape[1]
    scale = 1.0 / math.sqrt(width)
    owned = target_count // groups

    pool = pool_ref[...]
    logits = []
    for group in range(groups):
        products = jnp.sum(libs[group][...] * pool, axis=1, keepdims=True) * scale
        logits += [products[a : a + 1, :] for a in range(owned)]
    lane = lax.broadcasted_iota(jnp.int32, (1, target_count), 1)
    ordered = jnp.zeros((1, target_count), jnp.float32)
    for s in range(target_count):
        ordered = jnp.where(lane == slot_ref[s], logits[s], ordered)
    raised = jnp.exp(ordered - jnp.max(ordered, axis=1, keepdims=True))
    posterior_ref[...] = raised / jnp.sum(raised, axis=1, keepdims=True)

    hits = hits_ref[...]
    counts = [
        jnp.sum(jnp.where(hits == slot_ref[s], 1.0, 0.0), axis=1, keepdims=True)
        for s in range(target_count)
    ]
    shown = [jnp.where(c > 0.0, l, -jnp.inf) for c, l in zip(counts, logits)]
    highest = functools.reduce(jnp.maximum, shown)
    parts = [c * jnp.exp(l - highest) for c, l in zip(counts, shown)]
    total = functools.reduce(jnp.add, parts)

    half_sharp = 0.5 * sharp_ref[0]
    column = lax.broadcasted_iota(jnp.int32, (1, target_rows), 1)
    for s in range(target_count):
        at = pl.ds((s % owned) * target_rows, target_rows)
        similar = (mine[s // owned][:, at] + other[s // owned][:, at]) * scale
        length = len_ref[slot_ref[s]]
        inside = column < length
        fraction = 1.0 / length.astype(jnp.float32)
        row_mean = jnp.sum(jnp.where(inside, similar, 0.0), axis=1, keepdims=True) * fraction
        row_diff = similar - row_mean
        row_var = (
            jnp.sum(jnp.where(inside, row_diff * row_diff, 0.0), axis=1, keepdims=True) * fraction
        )
        column_mean = jnp.mean(similar, axis=0, keepdims=True)
        column_diff = similar - column_mean
        column_var = jnp.mean(column_diff * column_diff, axis=0, keepdims=True)
        scores = row_diff * (half_sharp * lax.rsqrt(row_var + 1e-05)) + column_diff * (
            half_sharp * lax.rsqrt(column_var + 1e-05)
        )
        scores = jnp.where(inside, scores, -jnp.inf)
        raised = jnp.exp(scores - jnp.max(scores, axis=1, keepdims=True))
        weight = (parts[s] / total) / jnp.sum(raised, axis=1, keepdims=True)
        weight_ref[:, pl.ds(s * target_rows, target_rows)] = (raised * weight).astype(jnp.bfloat16)

    acc = None
    for s in range(target_count):
        term = jnp.dot(
            weight_ref[:, pl.ds(s * target_rows, target_rows)],
            blocks[s][...],
            preferred_element_type=jnp.float32,
        )
        acc = term if acc is None else acc + term
    profile_ref[...] = acc.astype(jnp.bfloat16)


def per_device_by_target(
    query_res, target_res, target_len, hits, sharpness, query_pool, target_pool
):
    groups = lax.axis_size("tgt")
    owned, target_rows, width = target_res.shape
    target_count = groups * owned
    query = query_res[0]
    at_tgt, at_qry = lax.axis_index("tgt"), lax.axis_index("qry")
    swap = [(0, 1), (1, 0)]

    def from_peer(array, k):
        return lax.ppermute(array, "tgt", [(i, i ^ k) for i in range(groups)])

    share = lax.dynamic_index_in_dim(target_res, at_qry, 0, keepdims=False)
    direct = [from_peer(share, k) for k in range(1, groups)]
    libs = [target_pool] + [from_peer(target_pool, k) for k in range(1, groups)]
    libs = [libs[0]] + [jnp.where(at_qry == 0, lib, lib[::-1]) for lib in libs[1:]]
    blocks = [[target_res[0], target_res[1]]]
    slots = [at_tgt * owned, at_tgt * owned + 1]
    for k in range(1, groups):
        blocks.append([direct[k - 1], lax.ppermute(direct[k - 1], "qry", swap)])
        base = (at_tgt ^ k) * owned
        slots += [base + at_qry, base + 1 - at_qry]
    mine = [partial_similar(query, pair) for pair in blocks]
    other = [lax.ppermute(m, "rep", swap) for m in mine]
    slots = jnp.stack(slots).astype(jnp.int32)

    flat_blocks = [block for pair in blocks for block in pair]
    smem = pl.BlockSpec(memory_space=pltpu.SMEM)
    vmem = pl.BlockSpec(memory_space=pltpu.VMEM)
    operands = [slots, target_len, sharpness, hits, query_pool, *libs, *mine, *other, *flat_blocks]
    rows = query.shape[0]
    profile, posterior = pl.pallas_call(
        functools.partial(align_kernel, groups, target_rows, target_count),
        out_shape=(
            jax.ShapeDtypeStruct((rows, width), jnp.bfloat16),
            jax.ShapeDtypeStruct((1, target_count), jnp.float32),
        ),
        in_specs=[smem] * 3 + [vmem] * (len(operands) - 3),
        out_specs=(vmem, vmem),
        scratch_shapes=[pltpu.VMEM((rows, target_count * target_rows), jnp.bfloat16)],
        cost_estimate=pl.CostEstimate(
            flops=2 * rows * width * target_count * target_rows,
            bytes_accessed=4 * 1024 * 1024,
            transcendentals=rows * target_count * target_rows,
        ),
        compiler_params=pltpu.CompilerParams(vmem_limit_bytes=VMEM_BYTES),
    )(*operands)
    return (profile[None], posterior)


def solution(mesh):
    placed = (
        P(("grp", "tgt", "qry"), None, "rep"),
        P(("grp", "tgt"), None, "rep"),
        P("grp"),
        P(("grp", "tgt", "qry"), None),
        P(("grp", "tgt", "qry")),
        P(("grp", "tgt", "qry"), None),
        P(("grp", "tgt"), None),
    )
    groups = mesh.shape["tgt"]

    def per_device(*arrays):
        query_res, target_res, _, hits = arrays[:4]
        few = (
            query_res.shape[0] == 1
            and groups * target_res.shape[0] <= hits.shape[1]
            and target_res.shape[0] == mesh.shape["qry"] == 2
            and mesh.shape["rep"] == 2
            and groups & (groups - 1) == 0
        )
        return (per_device_by_target if few else per_device_by_hit)(*arrays)

    return jax.shard_map(
        per_device,
        mesh=mesh,
        in_specs=placed,
        out_specs=(P(("grp", "tgt", "qry"), None, "rep"), P(("grp", "tgt", "qry"), None)),
        check_vma=False,
    )
```

```python
import functools
import math

import jax
import jax.numpy as jnp
from jax import lax
from jax.experimental import pallas as pl
from jax.experimental.pallas import tpu as pltpu
from jax.sharding import PartitionSpec as P

VMEM_BYTES = 48 * 1024 * 1024


def softmax_rows(logits):
    highest = jnp.max(logits, axis=-1, keepdims=True)
    raised = jnp.exp(logits - highest)
    return raised / jnp.sum(raised, axis=-1, keepdims=True)


def weigh_alignment(similar, lengths, sharpness, hit_weight):
    target_rows = similar.shape[-1]
    inside = jnp.arange(target_rows)[None, None, None, :] < lengths[:, :, None, None]
    counted = lengths[:, :, None, None].astype(jnp.float32)
    row_mean = jnp.sum(jnp.where(inside, similar, 0.0), axis=-1, keepdims=True) / counted
    row_diff = similar - row_mean
    row_var = jnp.sum(jnp.where(inside, row_diff * row_diff, 0.0), axis=-1, keepdims=True) / counted
    row_score = row_diff / jnp.sqrt(row_var + 1e-05)
    column_mean = jnp.mean(similar, axis=2, keepdims=True)
    column_diff = similar - column_mean
    column_var = jnp.mean(column_diff * column_diff, axis=2, keepdims=True)
    column_score = column_diff / jnp.sqrt(column_var + 1e-05)
    scores = sharpness[:, None, None, None] * (0.5 * (row_score + column_score))
    scores = jnp.where(inside, scores, -jnp.inf)
    alignment = softmax_rows(scores)
    return (hit_weight[:, :, None, None] * alignment).astype(jnp.bfloat16)


def plan_slots(flat_hits, owned_targets, tgt_count, capacity):
    owners = flat_hits // owned_targets
    local_ids = flat_hits % owned_targets
    matched = owners[:, None] == jnp.arange(tgt_count)[None, :]
    earlier = jnp.cumsum(matched.astype(jnp.int32), axis=0) - 1
    rank_in = jnp.sum(jnp.where(matched, earlier, 0), axis=1)
    slot_of = owners * capacity + rank_in
    placed = slot_of[:, None] == jnp.arange(tgt_count * capacity)[None, :]
    wanted = jnp.sum(jnp.where(placed, local_ids[:, None], 0), axis=0).reshape(tgt_count, capacity)
    return (wanted, slot_of)


def fetch_shares(target_res, flat_hits, capacity):
    tgt_count = lax.axis_size("tgt")
    owned_targets, target_rows, width = target_res.shape
    wanted, slot_of = plan_slots(flat_hits, owned_targets, tgt_count, capacity)
    requested = lax.all_to_all(wanted, "tgt", split_axis=0, concat_axis=0, tiled=True)
    outgoing = jnp.take(target_res, requested.reshape(tgt_count * capacity), axis=0)
    outgoing = outgoing.reshape(tgt_count, capacity, target_rows, width)
    arrived = lax.all_to_all(outgoing, "tgt", split_axis=0, concat_axis=0, tiled=True)
    return jnp.take(arrived.reshape(tgt_count * capacity, target_rows, width), slot_of, axis=0)


def per_device_by_hit(query_res, target_res, target_len, hits, sharpness, query_pool, target_pool):
    tgt_count = lax.axis_size("tgt")
    query_count = query_res.shape[0]
    target_rows = target_res.shape[1]
    hit_count = hits.shape[1]
    pair_count = query_count * hit_count
    model_width = query_pool.shape[1]
    capacity = max(2, (2 * pair_count + tgt_count - 1) // tgt_count)
    library = lax.all_gather(target_pool, "tgt", axis=0, tiled=True)
    logits = jnp.dot(query_pool, library.T, precision=lax.Precision.HIGHEST) / math.sqrt(
        model_width
    )
    posterior = softmax_rows(logits)
    matches = hits[:, :, None] == jnp.arange(library.shape[0])[None, None, :]
    hit_weight = softmax_rows(jnp.sum(jnp.where(matches, logits[:, None, :], 0.0), axis=-1))
    lengths = jnp.sum(jnp.where(matches, target_len[None, None, :], 0), axis=-1)
    half_width = query_res.shape[2]
    chosen = fetch_shares(target_res, hits.reshape(pair_count), capacity)
    chosen = chosen.reshape(query_count, hit_count, target_rows, half_width)
    partial_sim = jnp.einsum(
        "qid,qhjd->qhij", query_res, chosen, preferred_element_type=jnp.float32
    ) / math.sqrt(model_width)
    similar = lax.psum(partial_sim, "rep")
    weighted = weigh_alignment(similar, lengths, sharpness, hit_weight)
    profile = jnp.einsum("qhij,qhjd->qid", weighted, chosen, preferred_element_type=jnp.float32)
    return (profile.astype(jnp.bfloat16), posterior)


VMEM = pl.BlockSpec(memory_space=pltpu.VMEM)
SMEM = pl.BlockSpec(memory_space=pltpu.SMEM)
PARAMS = pltpu.CompilerParams(vmem_limit_bytes=VMEM_BYTES)


def weigh_kernel(groups, slot_ref, hits_ref, pool_ref, *refs):
    libs, (posterior_ref, weight_ref) = refs[:groups], refs[groups:]
    owned, width = libs[0].shape
    target_count = groups * owned
    lane = lax.broadcasted_iota(jnp.int32, (1, target_count), 1)
    pool, hits = pool_ref[...], hits_ref[...]
    logits = jnp.zeros((1, target_count), jnp.float32)
    counts = jnp.zeros((1, target_count), jnp.float32)
    for group in range(groups):
        products = jnp.sum(libs[group][...] * pool, axis=1, keepdims=True) / math.sqrt(width)
        for a in range(owned):
            logits = jnp.where(lane == slot_ref[group] * owned + a, products[a : a + 1, :], logits)
    for t in range(target_count):
        named = jnp.sum(jnp.where(hits == t, 1.0, 0.0), axis=1, keepdims=True)
        counts = jnp.where(lane == t, named, counts)
    raised = jnp.exp(logits - jnp.max(logits, axis=1, keepdims=True))
    posterior_ref[...] = raised / jnp.sum(raised, axis=1, keepdims=True)
    shown = jnp.where(counts > 0.0, logits, -jnp.inf)
    parts = counts * jnp.exp(shown - jnp.max(shown, axis=1, keepdims=True))
    weight_ref[...] = parts / jnp.sum(parts, axis=1, keepdims=True)


def weigh_targets(slots, hits, pool, libs):
    count = len(libs) * libs[0].shape[0]
    shape = jax.ShapeDtypeStruct((1, count), jnp.float32)
    return pl.pallas_call(
        functools.partial(weigh_kernel, len(libs)),
        out_shape=(shape, shape),
        in_specs=[SMEM] + [VMEM] * (2 + len(libs)),
        out_specs=(VMEM, VMEM),
        cost_estimate=pl.CostEstimate(flops=65536, bytes_accessed=65536, transcendentals=64),
        compiler_params=PARAMS,
    )(slots, hits, pool, *libs)


def partial_kernel(*refs):
    query, blocks, out = refs[0], refs[1:-1], refs[-1]
    rows = 0
    for block in blocks:
        out[:, rows : rows + block.shape[0]] = lax.dot_general(
            query[...], block[...], (((1,), (1,)), ((), ())), preferred_element_type=jnp.float32
        )
        rows += block.shape[0]


def partial_similar(query, blocks):
    rows = sum(block.shape[0] for block in blocks)
    cost = pl.CostEstimate(
        flops=2 * query.shape[0] * rows * query.shape[1],
        bytes_accessed=2 * (query.size + rows * query.shape[1]) + 4 * query.shape[0] * rows,
        transcendentals=0,
    )
    return pl.pallas_call(
        partial_kernel,
        out_shape=jax.ShapeDtypeStruct((query.shape[0], rows), jnp.float32),
        in_specs=[VMEM] * (1 + len(blocks)),
        out_specs=VMEM,
        cost_estimate=cost,
        compiler_params=PARAMS,
    )(query, *blocks)


def align_kernel(model_width, parts, first, *refs):
    slot_ref, len_ref, sharp_ref, weight_ref = refs[:4]
    mine, other = refs[4 : 4 + parts], refs[4 + parts : 4 + 2 * parts]
    blocks = refs[4 + 2 * parts : -2 if first else -3]
    out_ref, align_ref = refs[-2:]
    target_rows = blocks[0].shape[0]
    scale = 1.0 / math.sqrt(model_width)
    half_sharp = 0.5 * sharp_ref[0]
    column = lax.broadcasted_iota(jnp.int32, (1, target_rows), 1)
    weights = weight_ref[...]
    lane = lax.broadcasted_iota(jnp.int32, weights.shape, 1)
    acc = None if first else refs[-3][...]
    places = [
        (part, pl.ds(at, target_rows))
        for part in range(parts)
        for at in range(0, mine[part].shape[1], target_rows)
    ]
    for s, (part, at) in enumerate(places):
        similar = (mine[part][:, at] + other[part][:, at]) * scale
        length = len_ref[slot_ref[s]]
        inside = column < length
        fraction = 1.0 / length.astype(jnp.float32)
        row_mean = jnp.sum(jnp.where(inside, similar, 0.0), axis=1, keepdims=True) * fraction
        row_diff = similar - row_mean
        row_var = (
            jnp.sum(jnp.where(inside, row_diff * row_diff, 0.0), axis=1, keepdims=True) * fraction
        )
        column_mean = jnp.mean(similar, axis=0, keepdims=True)
        column_diff = similar - column_mean
        column_var = jnp.mean(column_diff * column_diff, axis=0, keepdims=True)
        scores = row_diff * (half_sharp * lax.rsqrt(row_var + 1e-05)) + column_diff * (
            half_sharp * lax.rsqrt(column_var + 1e-05)
        )
        scores = jnp.where(inside, scores, -jnp.inf)
        raised = jnp.exp(scores - jnp.max(scores, axis=1, keepdims=True))
        weight = jnp.sum(jnp.where(lane == slot_ref[s], weights, 0.0), axis=1, keepdims=True)
        weight = weight / jnp.sum(raised, axis=1, keepdims=True)
        align_ref[:, pl.ds(s * target_rows, target_rows)] = (raised * weight).astype(jnp.bfloat16)
    for s, block in enumerate(blocks):
        term = jnp.dot(
            align_ref[:, pl.ds(s * target_rows, target_rows)],
            block[...],
            preferred_element_type=jnp.float32,
        )
        acc = term if acc is None else acc + term
    out_ref[...] = acc.astype(out_ref.dtype)


def add_aligned(common, weights, slots, mine, other, blocks, acc, dtype, model_width):
    rows, width = mine[0].shape[0], blocks[0].shape[1]
    target_rows = blocks[0].shape[0]
    slots = jnp.stack(slots).astype(jnp.int32)
    operands = [slots, *common, weights, *mine, *other, *blocks]
    operands += [] if acc is None else [acc]
    return pl.pallas_call(
        functools.partial(align_kernel, model_width, len(mine), acc is None),
        out_shape=jax.ShapeDtypeStruct((rows, width), dtype),
        in_specs=[SMEM] * 3 + [VMEM] * (len(operands) - 3),
        out_specs=VMEM,
        scratch_shapes=[pltpu.VMEM((rows, len(blocks) * target_rows), jnp.bfloat16)],
        cost_estimate=pl.CostEstimate(
            flops=2 * rows * width * len(blocks) * target_rows,
            bytes_accessed=len(blocks) * (8 * rows * target_rows + 2 * width * target_rows),
            transcendentals=rows * len(blocks) * target_rows,
        ),
        compiler_params=PARAMS,
    )(*operands)


def per_device_by_target(
    query_res, target_res, target_len, hits, sharpness, query_pool, target_pool
):
    model_width = query_pool.shape[1]
    query = query_res[0]
    at_tgt, at_qry = lax.axis_index("tgt"), lax.axis_index("qry")
    swap = [(0, 1), (1, 0)]

    def from_peer(array, k):
        return lax.ppermute(array, "tgt", [(i, i ^ k) for i in range(4)])

    def across(array, axis):
        return lax.ppermute(array, axis, swap)

    def after(array, *done):
        return lax.optimization_barrier((array, *done))[0]

    share = lax.dynamic_index_in_dim(target_res, at_qry, 0, keepdims=False)
    far = from_peer(share, 2)
    near = from_peer(target_res, 1)
    own_blocks = [target_res[0], target_res[1]]
    own = partial_similar(query, own_blocks)
    own_other = across(own, "rep")
    pool = after(target_pool, share)
    libs = [pool, from_peer(pool, 1), from_peer(pool, 2), from_peer(after(pool, own_other), 3)]
    far_rest = across(far, "qry")
    last = from_peer(far, 1)
    last_rest = across(last, "qry")

    peers = jnp.stack([at_tgt ^ k for k in range(4)]).astype(jnp.int32)
    posterior, weights = weigh_targets(peers, after(hits, far), query_pool, libs)
    own_id, near_id, far_id, last_id = (2 * (at_tgt ^ k) for k in range(4))
    common = (target_len, sharpness)

    def aligned(slots, mine, other, blocks, acc, dtype=jnp.float32):
        return add_aligned(
            common, weights, slots, [mine], [other], blocks, acc, dtype, model_width
        )

    acc = aligned([own_id, own_id + 1], own, own_other, own_blocks, None)
    one_blocks = [near[0], near[1], far, far_rest]
    one = partial_similar(after(query, acc, last), one_blocks)
    one_other = across(one, "rep")
    two_blocks = [last]
    two = partial_similar(query, two_blocks)
    two_other = across(two, "rep")
    slots = [near_id, near_id + 1, far_id + at_qry, far_id + 1 - at_qry]
    acc = aligned(slots, after(one, two), one_other, one_blocks, acc)
    three = partial_similar(after(query, acc), [last_rest])
    three_other = across(three, "rep")
    slots = [last_id + at_qry]
    acc = aligned(slots, after(two, three), two_other, two_blocks, acc)
    slots = [last_id + 1 - at_qry]
    acc = aligned(slots, three, three_other, [last_rest], acc, jnp.bfloat16)
    return (acc[None], posterior)


def solution(mesh):
    placed = (
        P(("grp", "tgt", "qry"), None, "rep"),
        P(("grp", "tgt"), None, "rep"),
        P("grp"),
        P(("grp", "tgt", "qry"), None),
        P(("grp", "tgt", "qry")),
        P(("grp", "tgt", "qry"), None),
        P(("grp", "tgt"), None),
    )
    groups = mesh.shape["tgt"]

    def per_device(*arrays):
        query_res, target_res, _, hits = arrays[:4]
        few = (
            query_res.shape[0] == 1
            and groups == 4 <= hits.shape[1] // target_res.shape[0]
            and target_res.shape[0] == mesh.shape["qry"] == 2
            and mesh.shape["rep"] == 2
        )
        return (per_device_by_target if few else per_device_by_hit)(*arrays)

    return jax.shard_map(
        per_device,
        mesh=mesh,
        in_specs=placed,
        out_specs=(P(("grp", "tgt", "qry"), None, "rep"), P(("grp", "tgt", "qry"), None)),
        check_vma=False,
    )
```

```python
import functools
import math

import jax
import jax.numpy as jnp
from jax import lax
from jax.experimental import pallas as pl
from jax.experimental.pallas import tpu as pltpu
from jax.sharding import PartitionSpec as P

VMEM_BYTES = 16 * 1024 * 1024


def softmax_rows(logits):
    highest = jnp.max(logits, axis=-1, keepdims=True)
    raised = jnp.exp(logits - highest)
    return raised / jnp.sum(raised, axis=-1, keepdims=True)


def weigh_alignment(similar, lengths, sharpness, hit_weight):
    target_rows = similar.shape[-1]
    inside = jnp.arange(target_rows)[None, None, None, :] < lengths[:, :, None, None]
    counted = lengths[:, :, None, None].astype(jnp.float32)
    row_mean = jnp.sum(jnp.where(inside, similar, 0.0), axis=-1, keepdims=True) / counted
    row_diff = similar - row_mean
    row_var = jnp.sum(jnp.where(inside, row_diff * row_diff, 0.0), axis=-1, keepdims=True) / counted
    row_score = row_diff / jnp.sqrt(row_var + 1e-05)
    column_mean = jnp.mean(similar, axis=2, keepdims=True)
    column_diff = similar - column_mean
    column_var = jnp.mean(column_diff * column_diff, axis=2, keepdims=True)
    column_score = column_diff / jnp.sqrt(column_var + 1e-05)
    scores = sharpness[:, None, None, None] * (0.5 * (row_score + column_score))
    scores = jnp.where(inside, scores, -jnp.inf)
    alignment = softmax_rows(scores)
    return (hit_weight[:, :, None, None] * alignment).astype(jnp.bfloat16)


def plan_slots(flat_hits, owned_targets, tgt_count, capacity):
    owners = flat_hits // owned_targets
    local_ids = flat_hits % owned_targets
    matched = owners[:, None] == jnp.arange(tgt_count)[None, :]
    earlier = jnp.cumsum(matched.astype(jnp.int32), axis=0) - 1
    rank_in = jnp.sum(jnp.where(matched, earlier, 0), axis=1)
    slot_of = owners * capacity + rank_in
    placed = slot_of[:, None] == jnp.arange(tgt_count * capacity)[None, :]
    wanted = jnp.sum(jnp.where(placed, local_ids[:, None], 0), axis=0).reshape(tgt_count, capacity)
    return (wanted, slot_of)


def fetch_shares(target_res, flat_hits, capacity):
    tgt_count = lax.axis_size("tgt")
    owned_targets, target_rows, width = target_res.shape
    wanted, slot_of = plan_slots(flat_hits, owned_targets, tgt_count, capacity)
    requested = lax.all_to_all(wanted, "tgt", split_axis=0, concat_axis=0, tiled=True)
    outgoing = jnp.take(target_res, requested.reshape(tgt_count * capacity), axis=0)
    outgoing = outgoing.reshape(tgt_count, capacity, target_rows, width)
    arrived = lax.all_to_all(outgoing, "tgt", split_axis=0, concat_axis=0, tiled=True)
    return jnp.take(arrived.reshape(tgt_count * capacity, target_rows, width), slot_of, axis=0)


def per_device_by_hit(query_res, target_res, target_len, hits, sharpness, query_pool, target_pool):
    tgt_count = lax.axis_size("tgt")
    query_count = query_res.shape[0]
    target_rows = target_res.shape[1]
    hit_count = hits.shape[1]
    pair_count = query_count * hit_count
    model_width = query_pool.shape[1]
    capacity = max(2, (2 * pair_count + tgt_count - 1) // tgt_count)
    library = lax.all_gather(target_pool, "tgt", axis=0, tiled=True)
    logits = jnp.dot(query_pool, library.T, precision=lax.Precision.HIGHEST) / math.sqrt(
        model_width
    )
    posterior = softmax_rows(logits)
    matches = hits[:, :, None] == jnp.arange(library.shape[0])[None, None, :]
    hit_weight = softmax_rows(jnp.sum(jnp.where(matches, logits[:, None, :], 0.0), axis=-1))
    lengths = jnp.sum(jnp.where(matches, target_len[None, None, :], 0), axis=-1)
    half_width = query_res.shape[2]
    chosen = fetch_shares(target_res, hits.reshape(pair_count), capacity)
    chosen = chosen.reshape(query_count, hit_count, target_rows, half_width)
    partial_sim = jnp.einsum(
        "qid,qhjd->qhij", query_res, chosen, preferred_element_type=jnp.float32
    ) / math.sqrt(model_width)
    similar = lax.psum(partial_sim, "rep")
    weighted = weigh_alignment(similar, lengths, sharpness, hit_weight)
    profile = jnp.einsum("qhij,qhjd->qid", weighted, chosen, preferred_element_type=jnp.float32)
    return (profile.astype(jnp.bfloat16), posterior)


VMEM = pl.BlockSpec(memory_space=pltpu.VMEM)
SMEM = pl.BlockSpec(memory_space=pltpu.SMEM)
PARAMS = pltpu.CompilerParams(vmem_limit_bytes=VMEM_BYTES)


def weigh_kernel(groups, slot_ref, hits_ref, pool_ref, *refs):
    libs, (posterior_ref, weight_ref) = refs[:groups], refs[groups:]
    owned, width = libs[0].shape
    target_count = groups * owned
    lane = lax.broadcasted_iota(jnp.int32, (1, target_count), 1)
    pool, hits = pool_ref[...], hits_ref[...]
    logits = jnp.zeros((1, target_count), jnp.float32)
    counts = jnp.zeros((1, target_count), jnp.float32)
    for group in range(groups):
        products = jnp.sum(libs[group][...] * pool, axis=1, keepdims=True) / math.sqrt(width)
        for a in range(owned):
            logits = jnp.where(lane == slot_ref[group] * owned + a, products[a : a + 1, :], logits)
    for t in range(target_count):
        named = jnp.sum(jnp.where(hits == t, 1.0, 0.0), axis=1, keepdims=True)
        counts = jnp.where(lane == t, named, counts)
    raised = jnp.exp(logits - jnp.max(logits, axis=1, keepdims=True))
    posterior_ref[...] = raised / jnp.sum(raised, axis=1, keepdims=True)
    shown = jnp.where(counts > 0.0, logits, -jnp.inf)
    parts = counts * jnp.exp(shown - jnp.max(shown, axis=1, keepdims=True))
    weight_ref[...] = parts / jnp.sum(parts, axis=1, keepdims=True)


def weigh_targets(slots, hits, pool, libs):
    count = len(libs) * libs[0].shape[0]
    shape = jax.ShapeDtypeStruct((1, count), jnp.float32)
    return pl.pallas_call(
        functools.partial(weigh_kernel, len(libs)),
        out_shape=(shape, shape),
        in_specs=[SMEM] + [VMEM] * (2 + len(libs)),
        out_specs=(VMEM, VMEM),
        cost_estimate=pl.CostEstimate(flops=65536, bytes_accessed=65536, transcendentals=64),
        compiler_params=PARAMS,
    )(slots, hits, pool, *libs)


def partial_kernel(*refs):
    query, blocks, out = refs[0], refs[1:-1], refs[-1]
    rows = 0
    for block in blocks:
        out[:, rows : rows + block.shape[0]] = lax.dot_general(
            query[...], block[...], (((1,), (1,)), ((), ())), preferred_element_type=jnp.float32
        )
        rows += block.shape[0]


def partial_similar(query, blocks):
    rows = sum(block.shape[0] for block in blocks)
    cost = pl.CostEstimate(
        flops=2 * query.shape[0] * rows * query.shape[1],
        bytes_accessed=2 * (query.size + rows * query.shape[1]) + 4 * query.shape[0] * rows,
        transcendentals=0,
    )
    return pl.pallas_call(
        partial_kernel,
        out_shape=jax.ShapeDtypeStruct((query.shape[0], rows), jnp.float32),
        in_specs=[VMEM] * (1 + len(blocks)),
        out_specs=VMEM,
        cost_estimate=cost,
        compiler_params=PARAMS,
    )(query, *blocks)


def align_kernel(model_width, parts, first, *refs):
    slot_ref, len_ref, sharp_ref, weight_ref = refs[:4]
    mine, other = refs[4 : 4 + parts], refs[4 + parts : 4 + 2 * parts]
    blocks = refs[4 + 2 * parts : -2 if first else -3]
    out_ref, align_ref = refs[-2:]
    target_rows = blocks[0].shape[0]
    scale = 1.0 / math.sqrt(model_width)
    half_sharp = 0.5 * sharp_ref[0]
    column = lax.broadcasted_iota(jnp.int32, (1, target_rows), 1)
    weights = weight_ref[...]
    lane = lax.broadcasted_iota(jnp.int32, weights.shape, 1)
    acc = None if first else refs[-3][...]
    places = [
        (part, pl.ds(at, target_rows))
        for part in range(parts)
        for at in range(0, mine[part].shape[1], target_rows)
    ]
    for s, (part, at) in enumerate(places):
        similar = (mine[part][:, at] + other[part][:, at]) * scale
        length = len_ref[slot_ref[s]]
        inside = column < length
        fraction = 1.0 / length.astype(jnp.float32)
        row_mean = jnp.sum(jnp.where(inside, similar, 0.0), axis=1, keepdims=True) * fraction
        row_diff = similar - row_mean
        row_var = (
            jnp.sum(jnp.where(inside, row_diff * row_diff, 0.0), axis=1, keepdims=True) * fraction
        )
        column_mean = jnp.mean(similar, axis=0, keepdims=True)
        column_diff = similar - column_mean
        column_var = jnp.mean(column_diff * column_diff, axis=0, keepdims=True)
        scores = row_diff * (half_sharp * lax.rsqrt(row_var + 1e-05)) + column_diff * (
            half_sharp * lax.rsqrt(column_var + 1e-05)
        )
        scores = jnp.where(inside, scores, -jnp.inf)
        raised = jnp.exp(scores - jnp.max(scores, axis=1, keepdims=True))
        weight = jnp.sum(jnp.where(lane == slot_ref[s], weights, 0.0), axis=1, keepdims=True)
        weight = weight / jnp.sum(raised, axis=1, keepdims=True)
        align_ref[:, pl.ds(s * target_rows, target_rows)] = (raised * weight).astype(jnp.bfloat16)
    for s, block in enumerate(blocks):
        term = jnp.dot(
            align_ref[:, pl.ds(s * target_rows, target_rows)],
            block[...],
            preferred_element_type=jnp.float32,
        )
        acc = term if acc is None else acc + term
    out_ref[...] = acc.astype(out_ref.dtype)


def add_aligned(common, weights, slots, mine, other, blocks, acc, dtype, model_width):
    rows, width = mine[0].shape[0], blocks[0].shape[1]
    target_rows = blocks[0].shape[0]
    slots = jnp.stack(slots).astype(jnp.int32)
    operands = [slots, *common, weights, *mine, *other, *blocks]
    operands += [] if acc is None else [acc]
    return pl.pallas_call(
        functools.partial(align_kernel, model_width, len(mine), acc is None),
        out_shape=jax.ShapeDtypeStruct((rows, width), dtype),
        in_specs=[SMEM] * 3 + [VMEM] * (len(operands) - 3),
        out_specs=VMEM,
        scratch_shapes=[pltpu.VMEM((rows, len(blocks) * target_rows), jnp.bfloat16)],
        cost_estimate=pl.CostEstimate(
            flops=2 * rows * width * len(blocks) * target_rows,
            bytes_accessed=len(blocks) * (8 * rows * target_rows + 2 * width * target_rows),
            transcendentals=rows * len(blocks) * target_rows,
        ),
        compiler_params=PARAMS,
    )(*operands)


def per_device_by_target(
    query_res, target_res, target_len, hits, sharpness, query_pool, target_pool
):
    model_width = query_pool.shape[1]
    query = query_res[0]
    at_tgt, at_qry = lax.axis_index("tgt"), lax.axis_index("qry")
    swap = [(0, 1), (1, 0)]

    def from_peer(array, k):
        return lax.ppermute(array, "tgt", [(i, i ^ k) for i in range(4)])

    def across(array, axis):
        return lax.ppermute(array, axis, swap)

    def after(array, *done):
        return lax.optimization_barrier((array, *done))[0]

    share = lax.dynamic_index_in_dim(target_res, at_qry, 0, keepdims=True)
    library = lax.all_gather(share, ("tgt", "qry"), axis=0, tiled=True)
    pool = after(target_pool, share)
    libs = [pool] + [from_peer(pool, k) for k in range(1, 4)]
    peers = jnp.stack([at_tgt ^ k for k in range(4)]).astype(jnp.int32)
    posterior, weights = weigh_targets(peers, hits, query_pool, libs)
    common = (target_len, sharpness)
    library, weights = lax.optimization_barrier((library, weights))

    pairs = [[library[2 * g], library[2 * g + 1]] for g in range(4)]
    mine = [partial_similar(query, pair) for pair in pairs]
    other = [across(m, "rep") for m in mine]
    acc = None
    for cut in ((0, 1), (2, 3)):
        acc = add_aligned(
            common,
            weights,
            [jnp.int32(t) for g in cut for t in (2 * g, 2 * g + 1)],
            [mine[g] for g in cut],
            [other[g] for g in cut],
            [block for g in cut for block in pairs[g]],
            acc,
            jnp.bfloat16 if cut[-1] == 3 else jnp.float32,
            model_width,
        )
    return (acc[None], posterior)


def solution(mesh):
    placed = (
        P(("grp", "tgt", "qry"), None, "rep"),
        P(("grp", "tgt"), None, "rep"),
        P("grp"),
        P(("grp", "tgt", "qry"), None),
        P(("grp", "tgt", "qry")),
        P(("grp", "tgt", "qry"), None),
        P(("grp", "tgt"), None),
    )
    groups = mesh.shape["tgt"]

    def per_device(*arrays):
        query_res, target_res, _, hits = arrays[:4]
        few = (
            query_res.shape[0] == 1
            and groups == 4 <= hits.shape[1] // target_res.shape[0]
            and target_res.shape[0] == mesh.shape["qry"] == 2
            and mesh.shape["rep"] == 2
        )
        return (per_device_by_target if few else per_device_by_hit)(*arrays)

    return jax.shard_map(
        per_device,
        mesh=mesh,
        in_specs=placed,
        out_specs=(P(("grp", "tgt", "qry"), None, "rep"), P(("grp", "tgt", "qry"), None)),
        check_vma=False,
    )
```

```python
import functools
import math

import jax
import jax.numpy as jnp
from jax import lax
from jax.experimental import pallas as pl
from jax.experimental.pallas import tpu as pltpu
from jax.sharding import PartitionSpec as P

VMEM_BYTES = 16 * 1024 * 1024


def softmax_rows(logits):
    highest = jnp.max(logits, axis=-1, keepdims=True)
    raised = jnp.exp(logits - highest)
    return raised / jnp.sum(raised, axis=-1, keepdims=True)


def weigh_alignment(similar, lengths, sharpness, hit_weight):
    target_rows = similar.shape[-1]
    inside = jnp.arange(target_rows)[None, None, None, :] < lengths[:, :, None, None]
    counted = lengths[:, :, None, None].astype(jnp.float32)
    row_mean = jnp.sum(jnp.where(inside, similar, 0.0), axis=-1, keepdims=True) / counted
    row_diff = similar - row_mean
    row_var = jnp.sum(jnp.where(inside, row_diff * row_diff, 0.0), axis=-1, keepdims=True) / counted
    row_score = row_diff / jnp.sqrt(row_var + 1e-05)
    column_mean = jnp.mean(similar, axis=2, keepdims=True)
    column_diff = similar - column_mean
    column_var = jnp.mean(column_diff * column_diff, axis=2, keepdims=True)
    column_score = column_diff / jnp.sqrt(column_var + 1e-05)
    scores = sharpness[:, None, None, None] * (0.5 * (row_score + column_score))
    scores = jnp.where(inside, scores, -jnp.inf)
    alignment = softmax_rows(scores)
    return (hit_weight[:, :, None, None] * alignment).astype(jnp.bfloat16)


def plan_slots(flat_hits, owned_targets, tgt_count, capacity):
    owners = flat_hits // owned_targets
    local_ids = flat_hits % owned_targets
    matched = owners[:, None] == jnp.arange(tgt_count)[None, :]
    earlier = jnp.cumsum(matched.astype(jnp.int32), axis=0) - 1
    rank_in = jnp.sum(jnp.where(matched, earlier, 0), axis=1)
    slot_of = owners * capacity + rank_in
    placed = slot_of[:, None] == jnp.arange(tgt_count * capacity)[None, :]
    wanted = jnp.sum(jnp.where(placed, local_ids[:, None], 0), axis=0).reshape(tgt_count, capacity)
    return (wanted, slot_of)


def fetch_shares(target_res, flat_hits, capacity):
    tgt_count = lax.axis_size("tgt")
    owned_targets, target_rows, width = target_res.shape
    wanted, slot_of = plan_slots(flat_hits, owned_targets, tgt_count, capacity)
    requested = lax.all_to_all(wanted, "tgt", split_axis=0, concat_axis=0, tiled=True)
    outgoing = jnp.take(target_res, requested.reshape(tgt_count * capacity), axis=0)
    outgoing = outgoing.reshape(tgt_count, capacity, target_rows, width)
    arrived = lax.all_to_all(outgoing, "tgt", split_axis=0, concat_axis=0, tiled=True)
    return jnp.take(arrived.reshape(tgt_count * capacity, target_rows, width), slot_of, axis=0)


def per_device_by_hit(query_res, target_res, target_len, hits, sharpness, query_pool, target_pool):
    tgt_count = lax.axis_size("tgt")
    query_count = query_res.shape[0]
    target_rows = target_res.shape[1]
    hit_count = hits.shape[1]
    pair_count = query_count * hit_count
    model_width = query_pool.shape[1]
    capacity = max(2, (2 * pair_count + tgt_count - 1) // tgt_count)
    library = lax.all_gather(target_pool, "tgt", axis=0, tiled=True)
    logits = jnp.dot(query_pool, library.T, precision=lax.Precision.HIGHEST) / math.sqrt(
        model_width
    )
    posterior = softmax_rows(logits)
    matches = hits[:, :, None] == jnp.arange(library.shape[0])[None, None, :]
    hit_weight = softmax_rows(jnp.sum(jnp.where(matches, logits[:, None, :], 0.0), axis=-1))
    lengths = jnp.sum(jnp.where(matches, target_len[None, None, :], 0), axis=-1)
    half_width = query_res.shape[2]
    chosen = fetch_shares(target_res, hits.reshape(pair_count), capacity)
    chosen = chosen.reshape(query_count, hit_count, target_rows, half_width)
    partial_sim = jnp.einsum(
        "qid,qhjd->qhij", query_res, chosen, preferred_element_type=jnp.float32
    ) / math.sqrt(model_width)
    similar = lax.psum(partial_sim, "rep")
    weighted = weigh_alignment(similar, lengths, sharpness, hit_weight)
    profile = jnp.einsum("qhij,qhjd->qid", weighted, chosen, preferred_element_type=jnp.float32)
    return (profile.astype(jnp.bfloat16), posterior)


VMEM = pl.BlockSpec(memory_space=pltpu.VMEM)


def call_kernel(kernel, out_shape, *operands, scratch=(), flops=0):
    return pl.pallas_call(
        kernel,
        out_shape=out_shape,
        in_specs=[VMEM] * len(operands),
        out_specs=jax.tree.map(lambda _: VMEM, out_shape),
        scratch_shapes=scratch,
        cost_estimate=pl.CostEstimate(flops=flops, bytes_accessed=0, transcendentals=0),
        compiler_params=pltpu.CompilerParams(vmem_limit_bytes=VMEM_BYTES),
    )(*operands)


def weigh_kernel(slot_ref, len_ref, sharp_ref, hits_ref, pool_ref, owner_ref, *refs):
    libs, (posterior_ref, table_ref) = refs[:-2], refs[-2:]
    owned, width = libs[0].shape
    target_count = len_ref.shape[1]
    lane = lax.broadcasted_iota(jnp.int32, (1, target_count), 1)
    pool, hits = pool_ref[...], hits_ref[...]
    logits = jnp.zeros((1, target_count), jnp.float32)
    counts = jnp.zeros((1, target_count), jnp.float32)
    for at, lib in enumerate(libs):
        products = jnp.sum(lib[...] * pool, axis=1, keepdims=True) / math.sqrt(width)
        first = owner_ref[at : at + 1, :] * owned
        for a in range(owned):
            logits = jnp.where(lane == first + a, products[a : a + 1, :], logits)
    for t in range(target_count):
        named = jnp.sum(jnp.where(hits == t, 1.0, 0.0), axis=1, keepdims=True)
        counts = jnp.where(lane == t, named, counts)
    raised = jnp.exp(logits - jnp.max(logits, axis=1, keepdims=True))
    posterior_ref[...] = raised / jnp.sum(raised, axis=1, keepdims=True)
    shown = jnp.where(counts > 0.0, logits, -jnp.inf)
    parts = counts * jnp.exp(shown - jnp.max(shown, axis=1, keepdims=True))
    weights = parts / jnp.sum(parts, axis=1, keepdims=True)
    matches = slot_ref[...] == lane
    lengths = jnp.sum(
        jnp.where(matches, len_ref[...].astype(jnp.float32), 0.0), axis=1, keepdims=True
    )
    weights = jnp.sum(jnp.where(matches, weights, 0.0), axis=1, keepdims=True)
    rows = table_ref.shape[1:]
    table_ref[0] = jnp.broadcast_to(lengths, rows)
    table_ref[1] = jnp.broadcast_to(1.0 / lengths, rows)
    table_ref[2] = jnp.broadcast_to(weights, rows)
    table_ref[3] = jnp.broadcast_to(0.5 * sharp_ref[...], rows)


def partial_kernel(*refs):
    query, blocks, out = refs[0], refs[1:-1], refs[-1]
    rows = 0
    for block in blocks:
        out[:, rows : rows + block.shape[0]] = lax.dot_general(
            query[...], block[...], (((1,), (1,)), ((), ())), preferred_element_type=jnp.float32
        )
        rows += block.shape[0]


def partial_similar(query, blocks):
    rows = sum(block.shape[0] for block in blocks)
    shape = jax.ShapeDtypeStruct((query.shape[0], rows), jnp.float32)
    return call_kernel(partial_kernel, shape, query, *blocks)


def align_kernel(model_width, slots, first, table_ref, mine, other, *refs):
    blocks = refs[: len(slots)]
    out_ref, align_ref = refs[-2:]
    target_rows = blocks[0].shape[0]
    scale = 1.0 / math.sqrt(model_width)
    column = lax.broadcasted_iota(jnp.int32, (1, target_rows), 1).astype(jnp.float32)
    acc = None if first else refs[-3][...]
    for at, slot in enumerate(slots):
        part = pl.ds(at * target_rows, target_rows)
        similar = (mine[:, part] + other[:, part]) * scale
        inside = column < table_ref[0, slot : slot + 1, :target_rows]
        fraction = table_ref[1, slot : slot + 1, 0:1]
        weight = table_ref[2, slot : slot + 1, 0:1]
        half_sharp = table_ref[3, slot : slot + 1, 0:1]
        row_mean = jnp.sum(jnp.where(inside, similar, 0.0), axis=1, keepdims=True) * fraction
        row_diff = similar - row_mean
        row_var = (
            jnp.sum(jnp.where(inside, row_diff * row_diff, 0.0), axis=1, keepdims=True) * fraction
        )
        column_mean = jnp.mean(similar, axis=0, keepdims=True)
        column_diff = similar - column_mean
        column_var = jnp.mean(column_diff * column_diff, axis=0, keepdims=True)
        scores = row_diff * (half_sharp * lax.rsqrt(row_var + 1e-05)) + column_diff * (
            half_sharp * lax.rsqrt(column_var + 1e-05)
        )
        scores = jnp.where(inside, scores, -jnp.inf)
        raised = jnp.exp(scores - jnp.max(scores, axis=1, keepdims=True))
        weight = weight / jnp.sum(raised, axis=1, keepdims=True)
        align_ref[:, part] = (raised * weight).astype(jnp.bfloat16)
    for at, block in enumerate(blocks):
        part = pl.ds(at * target_rows, target_rows)
        term = jnp.dot(align_ref[:, part], block[...], preferred_element_type=jnp.float32)
        acc = term if acc is None else acc + term
    out_ref[...] = acc.astype(out_ref.dtype)


def add_aligned(model_width, slots, table, mine, other, blocks, acc, dtype=jnp.float32):
    rows, width = mine.shape[0], blocks[0].shape[1]
    return call_kernel(
        functools.partial(align_kernel, model_width, slots, acc is None),
        jax.ShapeDtypeStruct((rows, width), dtype),
        table,
        mine,
        other,
        *blocks,
        *([] if acc is None else [acc]),
        scratch=[pltpu.VMEM(mine.shape, jnp.bfloat16)],
    )


def per_device_by_target(
    query_res, target_res, target_len, hits, sharpness, query_pool, target_pool
):
    model_width = query_pool.shape[1]
    target_rows = target_res.shape[1]
    query = query_res[0]
    at_tgt, at_qry, at_rep = (lax.axis_index(name) for name in ("tgt", "qry", "rep"))

    def from_peer(array, k):
        return lax.ppermute(array, "tgt", [(i, i ^ k) for i in range(4)])

    def across(array, axis):
        return lax.ppermute(array, axis, [(0, 1), (1, 0)])

    def after(array, *done):
        return lax.optimization_barrier((array, *done))[0]

    split = [(2 * i + c, 2 * (i ^ (1 + c)) + c) for i in range(4) for c in range(2)]
    pool_split = lax.ppermute(target_pool, ("tgt", "rep"), split)
    pool_last = from_peer(target_pool, 3)
    pool_other = across(pool_split, "rep")
    owners = jnp.stack([at_tgt, at_tgt ^ (1 + at_rep), at_tgt ^ (2 - at_rep), at_tgt ^ 3])
    libs = [target_pool, pool_split, pool_other, pool_last]

    share = lax.dynamic_index_in_dim(target_res, at_qry, 0, keepdims=False)
    rest = lax.dynamic_index_in_dim(target_res, 1 - at_qry, 0, keepdims=False)
    share = after(share, pool_split, pool_last)
    far = from_peer(share, 2)
    near = from_peer(share, 1)

    bases = [2 * (at_tgt ^ k) for k in range(4)]
    slots = [bases[0], bases[0] + 1]
    for base in bases[1:]:
        slots += [base + at_qry, base + 1 - at_qry]
    posterior, table = call_kernel(
        weigh_kernel,
        (
            jax.ShapeDtypeStruct((1, len(slots)), jnp.float32),
            jax.ShapeDtypeStruct((4, len(slots), target_rows), jnp.float32),
        ),
        jnp.stack(slots).astype(jnp.int32)[:, None],
        target_len[None],
        sharpness[None],
        hits,
        query_pool,
        owners.astype(jnp.int32)[:, None],
        *libs,
    )

    own_blocks = [target_res[0], target_res[1]]
    own = partial_similar(after(query, share), own_blocks)
    own_other = across(own, "rep")
    acc = add_aligned(model_width, (0, 1), table, own, own_other, own_blocks, None)

    far = after(far, acc)
    near = after(near, far)
    far_rest = across(far, "qry")
    near_rest = across(near, "qry")
    last = from_peer(far, 1)
    last_rest = from_peer(after(rest, far), 3)

    one = partial_similar(query, [far])
    one_other = across(one, "rep")
    acc = add_aligned(model_width, (4,), table, one, one_other, [far], acc)

    blocks = [near, far_rest, near_rest]
    two = partial_similar(after(query, acc), blocks)
    two_other = across(two, "rep")
    three = partial_similar(after(query, two), [last, last_rest])
    three_other = across(three, "rep")
    acc = add_aligned(model_width, (2, 5, 3), table, after(two, three), two_other, blocks, acc)
    profile = add_aligned(
        model_width, (6, 7), table, three, three_other, [last, last_rest], acc, jnp.bfloat16
    )
    return (profile[None], posterior)


def solution(mesh):
    placed = (
        P(("grp", "tgt", "qry"), None, "rep"),
        P(("grp", "tgt"), None, "rep"),
        P("grp"),
        P(("grp", "tgt", "qry"), None),
        P(("grp", "tgt", "qry")),
        P(("grp", "tgt", "qry"), None),
        P(("grp", "tgt"), None),
    )
    groups = mesh.shape["tgt"]

    def per_device(*arrays):
        query_res, target_res, _, hits = arrays[:4]
        few = (
            query_res.shape[0] == 1
            and groups == 4 <= hits.shape[1] // target_res.shape[0]
            and target_res.shape[0] == mesh.shape["qry"] == 2
            and mesh.shape["rep"] == 2
        )
        return (per_device_by_target if few else per_device_by_hit)(*arrays)

    return jax.shard_map(
        per_device,
        mesh=mesh,
        in_specs=placed,
        out_specs=(P(("grp", "tgt", "qry"), None, "rep"), P(("grp", "tgt", "qry"), None)),
        check_vma=False,
    )
```

```python
import functools
import math

import jax
import jax.numpy as jnp
from jax import lax
from jax.experimental import pallas as pl
from jax.experimental.pallas import tpu as pltpu
from jax.sharding import PartitionSpec as P

VMEM_BYTES = 16 * 1024 * 1024


def softmax_rows(logits):
    highest = jnp.max(logits, axis=-1, keepdims=True)
    raised = jnp.exp(logits - highest)
    return raised / jnp.sum(raised, axis=-1, keepdims=True)


def weigh_alignment(similar, lengths, sharpness, hit_weight):
    target_rows = similar.shape[-1]
    inside = jnp.arange(target_rows)[None, None, None, :] < lengths[:, :, None, None]
    counted = lengths[:, :, None, None].astype(jnp.float32)
    row_mean = jnp.sum(jnp.where(inside, similar, 0.0), axis=-1, keepdims=True) / counted
    row_diff = similar - row_mean
    row_var = jnp.sum(jnp.where(inside, row_diff * row_diff, 0.0), axis=-1, keepdims=True) / counted
    row_score = row_diff / jnp.sqrt(row_var + 1e-05)
    column_mean = jnp.mean(similar, axis=2, keepdims=True)
    column_diff = similar - column_mean
    column_var = jnp.mean(column_diff * column_diff, axis=2, keepdims=True)
    column_score = column_diff / jnp.sqrt(column_var + 1e-05)
    scores = sharpness[:, None, None, None] * (0.5 * (row_score + column_score))
    scores = jnp.where(inside, scores, -jnp.inf)
    alignment = softmax_rows(scores)
    return (hit_weight[:, :, None, None] * alignment).astype(jnp.bfloat16)


def plan_slots(flat_hits, owned_targets, tgt_count, capacity):
    owners = flat_hits // owned_targets
    local_ids = flat_hits % owned_targets
    matched = owners[:, None] == jnp.arange(tgt_count)[None, :]
    earlier = jnp.cumsum(matched.astype(jnp.int32), axis=0) - 1
    rank_in = jnp.sum(jnp.where(matched, earlier, 0), axis=1)
    slot_of = owners * capacity + rank_in
    placed = slot_of[:, None] == jnp.arange(tgt_count * capacity)[None, :]
    wanted = jnp.sum(jnp.where(placed, local_ids[:, None], 0), axis=0).reshape(tgt_count, capacity)
    return (wanted, slot_of)


def fetch_shares(target_res, flat_hits, capacity):
    tgt_count = lax.axis_size("tgt")
    owned_targets, target_rows, width = target_res.shape
    wanted, slot_of = plan_slots(flat_hits, owned_targets, tgt_count, capacity)
    requested = lax.all_to_all(wanted, "tgt", split_axis=0, concat_axis=0, tiled=True)
    outgoing = jnp.take(target_res, requested.reshape(tgt_count * capacity), axis=0)
    outgoing = outgoing.reshape(tgt_count, capacity, target_rows, width)
    arrived = lax.all_to_all(outgoing, "tgt", split_axis=0, concat_axis=0, tiled=True)
    return jnp.take(arrived.reshape(tgt_count * capacity, target_rows, width), slot_of, axis=0)


def per_device_by_hit(query_res, target_res, target_len, hits, sharpness, query_pool, target_pool):
    tgt_count = lax.axis_size("tgt")
    query_count = query_res.shape[0]
    target_rows = target_res.shape[1]
    hit_count = hits.shape[1]
    pair_count = query_count * hit_count
    model_width = query_pool.shape[1]
    capacity = max(2, (2 * pair_count + tgt_count - 1) // tgt_count)
    library = lax.all_gather(target_pool, "tgt", axis=0, tiled=True)
    logits = jnp.dot(query_pool, library.T, precision=lax.Precision.HIGHEST) / math.sqrt(
        model_width
    )
    posterior = softmax_rows(logits)
    matches = hits[:, :, None] == jnp.arange(library.shape[0])[None, None, :]
    hit_weight = softmax_rows(jnp.sum(jnp.where(matches, logits[:, None, :], 0.0), axis=-1))
    lengths = jnp.sum(jnp.where(matches, target_len[None, None, :], 0), axis=-1)
    half_width = query_res.shape[2]
    chosen = fetch_shares(target_res, hits.reshape(pair_count), capacity)
    chosen = chosen.reshape(query_count, hit_count, target_rows, half_width)
    partial_sim = jnp.einsum(
        "qid,qhjd->qhij", query_res, chosen, preferred_element_type=jnp.float32
    ) / math.sqrt(model_width)
    similar = lax.psum(partial_sim, "rep")
    weighted = weigh_alignment(similar, lengths, sharpness, hit_weight)
    profile = jnp.einsum("qhij,qhjd->qid", weighted, chosen, preferred_element_type=jnp.float32)
    return (profile.astype(jnp.bfloat16), posterior)


VMEM = pl.BlockSpec(memory_space=pltpu.VMEM)


def call_kernel(kernel, out_shape, *operands, scratch=(), flops=0):
    return pl.pallas_call(
        kernel,
        out_shape=out_shape,
        in_specs=[VMEM] * len(operands),
        out_specs=jax.tree.map(lambda _: VMEM, out_shape),
        scratch_shapes=scratch,
        cost_estimate=pl.CostEstimate(flops=flops, bytes_accessed=0, transcendentals=0),
        compiler_params=pltpu.CompilerParams(vmem_limit_bytes=VMEM_BYTES),
    )(*operands)


def weigh_kernel(slot_ref, hits_ref, pool_ref, owner_ref, *refs):
    libs, (posterior_ref, weight_ref) = refs[:-2], refs[-2:]
    owned, width = libs[0].shape
    target_count = posterior_ref.shape[1]
    lane = lax.broadcasted_iota(jnp.int32, (1, target_count), 1)
    pool, hits = pool_ref[...], hits_ref[...]
    logits = jnp.zeros((1, target_count), jnp.float32)
    counts = jnp.zeros((1, target_count), jnp.float32)
    for at, lib in enumerate(libs):
        products = jnp.sum(lib[...] * pool, axis=1, keepdims=True) / math.sqrt(width)
        first = owner_ref[at : at + 1, :] * owned
        for a in range(owned):
            logits = jnp.where(lane == first + a, products[a : a + 1, :], logits)
    for t in range(target_count):
        named = jnp.sum(jnp.where(hits == t, 1.0, 0.0), axis=1, keepdims=True)
        counts = jnp.where(lane == t, named, counts)
    raised = jnp.exp(logits - jnp.max(logits, axis=1, keepdims=True))
    posterior_ref[...] = raised / jnp.sum(raised, axis=1, keepdims=True)
    shown = jnp.where(counts > 0.0, logits, -jnp.inf)
    parts = counts * jnp.exp(shown - jnp.max(shown, axis=1, keepdims=True))
    weights = parts / jnp.sum(parts, axis=1, keepdims=True)
    weights = jnp.sum(jnp.where(slot_ref[...] == lane, weights, 0.0), axis=1, keepdims=True)
    weight_ref[...] = jnp.broadcast_to(weights, weight_ref.shape)


def partial_kernel(*refs):
    query, blocks, out = refs[0], refs[1:-1], refs[-1]
    rows = 0
    for block in blocks:
        out[:, rows : rows + block.shape[0]] = lax.dot_general(
            query[...], block[...], (((1,), (1,)), ((), ())), preferred_element_type=jnp.float32
        )
        rows += block.shape[0]


def partial_similar(query, blocks):
    rows = sum(block.shape[0] for block in blocks)
    shape = jax.ShapeDtypeStruct((query.shape[0], rows), jnp.float32)
    return call_kernel(partial_kernel, shape, query, *blocks)


def align_block(similar, length, half_sharp):
    column = lax.broadcasted_iota(jnp.int32, (1, similar.shape[1]), 1).astype(jnp.float32)
    inside = column < length
    fraction = 1.0 / length[:, 0:1]
    row_mean = jnp.sum(jnp.where(inside, similar, 0.0), axis=1, keepdims=True) * fraction
    row_diff = similar - row_mean
    row_var = (
        jnp.sum(jnp.where(inside, row_diff * row_diff, 0.0), axis=1, keepdims=True) * fraction
    )
    column_mean = jnp.mean(similar, axis=0, keepdims=True)
    column_diff = similar - column_mean
    column_var = jnp.mean(column_diff * column_diff, axis=0, keepdims=True)
    scores = row_diff * (half_sharp * lax.rsqrt(row_var + 1e-05)) + column_diff * (
        half_sharp * lax.rsqrt(column_var + 1e-05)
    )
    scores = jnp.where(inside, scores, -jnp.inf)
    raised = jnp.exp(scores - jnp.max(scores, axis=1, keepdims=True))
    return raised / jnp.sum(raised, axis=1, keepdims=True)


def align_kernel(model_width, slots, len_ref, sharp_ref, mine, other, out_ref):
    scale = 1.0 / math.sqrt(model_width)
    rows = mine.shape[1] // len(slots)
    for at, slot in enumerate(slots):
        part = pl.ds(at * rows, rows)
        similar = (mine[:, part] + other[:, part]) * scale
        alignment = align_block(similar, len_ref[slot : slot + 1, :rows], sharp_ref[:, 0:1])
        out_ref[:, part] = alignment.astype(out_ref.dtype)


def align(model_width, slots, lengths, half_sharp, mine, other):
    return call_kernel(
        functools.partial(align_kernel, model_width, slots),
        jax.ShapeDtypeStruct(mine.shape, jnp.bfloat16),
        lengths,
        half_sharp,
        mine,
        other,
    )


def profile_kernel(groups, weight_ref, *refs):
    aligned, blocks, out_ref = refs[: len(groups)], refs[len(groups) : -1], refs[-1]
    rows = blocks[0].shape[0]
    acc, at = None, 0
    for group, slots in zip(aligned, groups):
        for i, slot in enumerate(slots):
            term = weight_ref[slot : slot + 1, 0:1] * jnp.dot(
                group[:, i * rows : (i + 1) * rows],
                blocks[at][...],
                preferred_element_type=jnp.float32,
            )
            acc = term if acc is None else acc + term
            at += 1
    out_ref[...] = acc


def last_kernel(model_width, slot, len_ref, sharp_ref, weight_ref, mine, other, block, acc, out_ref):
    rows = block.shape[0]
    similar = (mine[...] + other[...]) * (1.0 / math.sqrt(model_width))
    alignment = align_block(similar, len_ref[slot : slot + 1, :rows], sharp_ref[:, 0:1])
    term = weight_ref[slot : slot + 1, 0:1] * jnp.dot(
        alignment.astype(jnp.bfloat16), block[...], preferred_element_type=jnp.float32
    )
    out_ref[...] = (acc[...] + term).astype(out_ref.dtype)


def per_device_by_target(
    query_res, target_res, target_len, hits, sharpness, query_pool, target_pool
):
    model_width = query_pool.shape[1]
    target_rows = target_res.shape[1]
    query = query_res[0]
    at_tgt, at_qry, at_rep = (lax.axis_index(name) for name in ("tgt", "qry", "rep"))

    def from_peer(array, k):
        return lax.ppermute(array, "tgt", [(i, i ^ k) for i in range(4)])

    def across(array, axis):
        return lax.ppermute(array, axis, [(0, 1), (1, 0)])

    def after(array, *done):
        return lax.optimization_barrier((array, *done))[0]

    def asked(x, c):
        return 2 * c + (1 - c) * (1 + 2 * x)

    pairs = [
        ((2 * i + x) * 2 + c, (2 * (i ^ asked(x, c)) + x) * 2 + c)
        for i in range(4)
        for x in range(2)
        for c in range(2)
    ]
    pools = [lax.ppermute(target_pool, ("tgt", "qry", "rep"), pairs)]
    owners = [at_tgt] + [
        at_tgt ^ asked(x, c) for c in (at_rep, 1 - at_rep) for x in (at_qry, 1 - at_qry)
    ]
    owners = jnp.stack(owners)

    share = lax.dynamic_index_in_dim(target_res, at_qry, 0, keepdims=False)
    rest = lax.dynamic_index_in_dim(target_res, 1 - at_qry, 0, keepdims=False)
    far = from_peer(share, 2)
    near = from_peer(share, 1)

    bases = [2 * (at_tgt ^ k) for k in range(4)]
    slots = [bases[0], bases[0] + 1]
    for base in bases[1:]:
        slots += [base + at_qry, base + 1 - at_qry]
    slots = jnp.stack(slots).astype(jnp.int32)[:, None]
    named = slots == jnp.arange(len(target_len))[None]
    lengths = jnp.sum(jnp.where(named, target_len[None], 0), axis=1, keepdims=True)
    lengths = jnp.broadcast_to(lengths.astype(jnp.float32), (len(target_len), target_rows))
    half_sharp = jnp.broadcast_to(0.5 * sharpness, (1, target_rows))

    def aligned(slots, mine, other):
        return align(model_width, slots, lengths, half_sharp, mine, other)

    own_blocks = [target_res[0], target_res[1]]
    own = partial_similar(after(query, pools[0]), own_blocks)
    own_other = across(own, "rep")

    far = after(far, pools[0])
    near = after(near, far)
    far = after(far, near)
    zero = aligned((0, 1), after(own, far), own_other)
    last = from_peer(far, 1)
    far_rest = across(far, "qry")

    near_rest = from_peer(after(rest, far), 1)

    pools.append(across(pools[0], "qry"))
    pools += [across(pool, "rep") for pool in pools]
    last = after(last, *pools)
    two_blocks = [near, far, far_rest]
    two = partial_similar(after(query, zero, last), two_blocks)
    two_other = across(two, "rep")
    last = after(last, two)
    last_rest = across(last, "qry")
    two_aligned = aligned((2, 4, 5), two, two_other)

    posterior, weights = call_kernel(
        weigh_kernel,
        (
            jax.ShapeDtypeStruct((1, len(target_len)), jnp.float32),
            jax.ShapeDtypeStruct((len(target_len), target_rows), jnp.float32),
        ),
        slots,
        after(hits, two_aligned),
        query_pool,
        owners.astype(jnp.int32)[:, None],
        target_pool,
        *pools,
    )

    three_blocks = [last, near_rest]
    three = partial_similar(after(query, *pools), three_blocks)
    three_other = across(three, "rep")
    four = partial_similar(after(query, three, weights), [last_rest])
    four_other = across(four, "rep")
    three_aligned = aligned((6, 3), after(three, four), three_other)
    acc = call_kernel(
        functools.partial(profile_kernel, ((0, 1), (2, 4, 5), (6, 3))),
        jax.ShapeDtypeStruct(query.shape, jnp.float32),
        weights,
        zero,
        two_aligned,
        three_aligned,
        *own_blocks,
        *two_blocks,
        *three_blocks,
    )
    profile = call_kernel(
        functools.partial(last_kernel, model_width, 7),
        jax.ShapeDtypeStruct(query.shape, jnp.bfloat16),
        lengths,
        half_sharp,
        weights,
        four,
        four_other,
        last_rest,
        acc,
    )
    return (profile[None], posterior)


def solution(mesh):
    placed = (
        P(("grp", "tgt", "qry"), None, "rep"),
        P(("grp", "tgt"), None, "rep"),
        P("grp"),
        P(("grp", "tgt", "qry"), None),
        P(("grp", "tgt", "qry")),
        P(("grp", "tgt", "qry"), None),
        P(("grp", "tgt"), None),
    )
    groups = mesh.shape["tgt"]

    def per_device(*arrays):
        query_res, target_res, _, hits = arrays[:4]
        few = (
            query_res.shape[0] == 1
            and groups == 4 <= hits.shape[1] // target_res.shape[0]
            and target_res.shape[0] == mesh.shape["qry"] == 2
            and mesh.shape["rep"] == 2
        )
        return (per_device_by_target if few else per_device_by_hit)(*arrays)

    return jax.shard_map(
        per_device,
        mesh=mesh,
        in_specs=placed,
        out_specs=(P(("grp", "tgt", "qry"), None, "rep"), P(("grp", "tgt", "qry"), None)),
        check_vma=False,
    )
```

```python
import functools
import math

import jax
import jax.numpy as jnp
from jax import lax
from jax.experimental import pallas as pl
from jax.experimental.pallas import tpu as pltpu
from jax.sharding import PartitionSpec as P

VMEM_BYTES = 16 * 1024 * 1024


def softmax_rows(logits):
    highest = jnp.max(logits, axis=-1, keepdims=True)
    raised = jnp.exp(logits - highest)
    return raised / jnp.sum(raised, axis=-1, keepdims=True)


def weigh_alignment(similar, lengths, sharpness, hit_weight):
    target_rows = similar.shape[-1]
    inside = jnp.arange(target_rows)[None, None, None, :] < lengths[:, :, None, None]
    counted = lengths[:, :, None, None].astype(jnp.float32)
    row_mean = jnp.sum(jnp.where(inside, similar, 0.0), axis=-1, keepdims=True) / counted
    row_diff = similar - row_mean
    row_var = jnp.sum(jnp.where(inside, row_diff * row_diff, 0.0), axis=-1, keepdims=True) / counted
    row_score = row_diff / jnp.sqrt(row_var + 1e-05)
    column_mean = jnp.mean(similar, axis=2, keepdims=True)
    column_diff = similar - column_mean
    column_var = jnp.mean(column_diff * column_diff, axis=2, keepdims=True)
    column_score = column_diff / jnp.sqrt(column_var + 1e-05)
    scores = sharpness[:, None, None, None] * (0.5 * (row_score + column_score))
    scores = jnp.where(inside, scores, -jnp.inf)
    alignment = softmax_rows(scores)
    return (hit_weight[:, :, None, None] * alignment).astype(jnp.bfloat16)


def plan_slots(flat_hits, owned_targets, tgt_count, capacity):
    owners = flat_hits // owned_targets
    local_ids = flat_hits % owned_targets
    matched = owners[:, None] == jnp.arange(tgt_count)[None, :]
    earlier = jnp.cumsum(matched.astype(jnp.int32), axis=0) - 1
    rank_in = jnp.sum(jnp.where(matched, earlier, 0), axis=1)
    slot_of = owners * capacity + rank_in
    placed = slot_of[:, None] == jnp.arange(tgt_count * capacity)[None, :]
    wanted = jnp.sum(jnp.where(placed, local_ids[:, None], 0), axis=0).reshape(tgt_count, capacity)
    return (wanted, slot_of)


def fetch_shares(target_res, flat_hits, capacity):
    tgt_count = lax.axis_size("tgt")
    owned_targets, target_rows, width = target_res.shape
    wanted, slot_of = plan_slots(flat_hits, owned_targets, tgt_count, capacity)
    requested = lax.all_to_all(wanted, "tgt", split_axis=0, concat_axis=0, tiled=True)
    outgoing = jnp.take(target_res, requested.reshape(tgt_count * capacity), axis=0)
    outgoing = outgoing.reshape(tgt_count, capacity, target_rows, width)
    arrived = lax.all_to_all(outgoing, "tgt", split_axis=0, concat_axis=0, tiled=True)
    return jnp.take(arrived.reshape(tgt_count * capacity, target_rows, width), slot_of, axis=0)


def per_device_by_hit(query_res, target_res, target_len, hits, sharpness, query_pool, target_pool):
    tgt_count = lax.axis_size("tgt")
    query_count = query_res.shape[0]
    target_rows = target_res.shape[1]
    hit_count = hits.shape[1]
    pair_count = query_count * hit_count
    model_width = query_pool.shape[1]
    capacity = max(2, (2 * pair_count + tgt_count - 1) // tgt_count)
    library = lax.all_gather(target_pool, "tgt", axis=0, tiled=True)
    logits = jnp.dot(query_pool, library.T, precision=lax.Precision.HIGHEST) / math.sqrt(
        model_width
    )
    posterior = softmax_rows(logits)
    matches = hits[:, :, None] == jnp.arange(library.shape[0])[None, None, :]
    hit_weight = softmax_rows(jnp.sum(jnp.where(matches, logits[:, None, :], 0.0), axis=-1))
    lengths = jnp.sum(jnp.where(matches, target_len[None, None, :], 0), axis=-1)
    half_width = query_res.shape[2]
    chosen = fetch_shares(target_res, hits.reshape(pair_count), capacity)
    chosen = chosen.reshape(query_count, hit_count, target_rows, half_width)
    partial_sim = jnp.einsum(
        "qid,qhjd->qhij", query_res, chosen, preferred_element_type=jnp.float32
    ) / math.sqrt(model_width)
    similar = lax.psum(partial_sim, "rep")
    weighted = weigh_alignment(similar, lengths, sharpness, hit_weight)
    profile = jnp.einsum("qhij,qhjd->qid", weighted, chosen, preferred_element_type=jnp.float32)
    return (profile.astype(jnp.bfloat16), posterior)


VMEM = pl.BlockSpec(memory_space=pltpu.VMEM)


def call_kernel(kernel, out_shape, *operands, scratch=(), flops=0):
    return pl.pallas_call(
        kernel,
        out_shape=out_shape,
        in_specs=[VMEM] * len(operands),
        out_specs=jax.tree.map(lambda _: VMEM, out_shape),
        scratch_shapes=scratch,
        cost_estimate=pl.CostEstimate(flops=flops, bytes_accessed=0, transcendentals=0),
        compiler_params=pltpu.CompilerParams(vmem_limit_bytes=VMEM_BYTES),
    )(*operands)


def weigh_kernel(slot_ref, hits_ref, pool_ref, owner_ref, *refs):
    libs, (posterior_ref, weight_ref) = refs[:-2], refs[-2:]
    owned, width = libs[0].shape
    target_count = posterior_ref.shape[1]
    lane = lax.broadcasted_iota(jnp.int32, (1, target_count), 1)
    pool, hits = pool_ref[...], hits_ref[...]
    logits = jnp.zeros((1, target_count), jnp.float32)
    counts = jnp.zeros((1, target_count), jnp.float32)
    for at, lib in enumerate(libs):
        products = jnp.sum(lib[...] * pool, axis=1, keepdims=True) / math.sqrt(width)
        first = owner_ref[at : at + 1, :] * owned
        for a in range(owned):
            logits = jnp.where(lane == first + a, products[a : a + 1, :], logits)
    for t in range(target_count):
        named = jnp.sum(jnp.where(hits == t, 1.0, 0.0), axis=1, keepdims=True)
        counts = jnp.where(lane == t, named, counts)
    raised = jnp.exp(logits - jnp.max(logits, axis=1, keepdims=True))
    posterior_ref[...] = raised / jnp.sum(raised, axis=1, keepdims=True)
    shown = jnp.where(counts > 0.0, logits, -jnp.inf)
    parts = counts * jnp.exp(shown - jnp.max(shown, axis=1, keepdims=True))
    weights = parts / jnp.sum(parts, axis=1, keepdims=True)
    weights = jnp.sum(jnp.where(slot_ref[...] == lane, weights, 0.0), axis=1, keepdims=True)
    weight_ref[...] = jnp.broadcast_to(weights, weight_ref.shape)


def partial_kernel(*refs):
    query, blocks, out = refs[0], refs[1:-1], refs[-1]
    rows = 0
    for block in blocks:
        out[:, rows : rows + block.shape[0]] = lax.dot_general(
            query[...], block[...], (((1,), (1,)), ((), ())), preferred_element_type=jnp.float32
        )
        rows += block.shape[0]


def partial_similar(query, blocks):
    rows = sum(block.shape[0] for block in blocks)
    shape = jax.ShapeDtypeStruct((query.shape[0], rows), jnp.float32)
    return call_kernel(partial_kernel, shape, query, *blocks)


def align_block(similar, length, half_sharp):
    column = lax.broadcasted_iota(jnp.int32, (1, similar.shape[1]), 1).astype(jnp.float32)
    inside = column < length
    fraction = 1.0 / length[:, 0:1]
    row_mean = jnp.sum(jnp.where(inside, similar, 0.0), axis=1, keepdims=True) * fraction
    row_diff = similar - row_mean
    row_var = (
        jnp.sum(jnp.where(inside, row_diff * row_diff, 0.0), axis=1, keepdims=True) * fraction
    )
    column_mean = jnp.mean(similar, axis=0, keepdims=True)
    column_diff = similar - column_mean
    column_var = jnp.mean(column_diff * column_diff, axis=0, keepdims=True)
    scores = row_diff * (half_sharp * lax.rsqrt(row_var + 1e-05)) + column_diff * (
        half_sharp * lax.rsqrt(column_var + 1e-05)
    )
    scores = jnp.where(inside, scores, -jnp.inf)
    raised = jnp.exp(scores - jnp.max(scores, axis=1, keepdims=True))
    return raised / jnp.sum(raised, axis=1, keepdims=True)


def align_kernel(model_width, slots, len_ref, sharp_ref, mine, other, out_ref):
    scale = 1.0 / math.sqrt(model_width)
    rows = mine.shape[1] // len(slots)
    for at, slot in enumerate(slots):
        part = pl.ds(at * rows, rows)
        similar = (mine[:, part] + other[:, part]) * scale
        alignment = align_block(similar, len_ref[slot : slot + 1, :rows], sharp_ref[:, 0:1])
        out_ref[:, part] = alignment.astype(out_ref.dtype)


def align(model_width, slots, lengths, half_sharp, mine, other):
    return call_kernel(
        functools.partial(align_kernel, model_width, slots),
        jax.ShapeDtypeStruct(mine.shape, jnp.bfloat16),
        lengths,
        half_sharp,
        mine,
        other,
    )


def profile_kernel(groups, weight_ref, *refs):
    aligned, blocks, out_ref = refs[: len(groups)], refs[len(groups) : -1], refs[-1]
    rows = blocks[0].shape[0]
    acc, at = None, 0
    for group, slots in zip(aligned, groups):
        for i, slot in enumerate(slots):
            term = weight_ref[slot : slot + 1, 0:1] * jnp.dot(
                group[:, i * rows : (i + 1) * rows],
                blocks[at][...],
                preferred_element_type=jnp.float32,
            )
            acc = term if acc is None else acc + term
            at += 1
    out_ref[...] = acc


def last_kernel(model_width, slot, len_ref, sharp_ref, weight_ref, mine, other, block, acc, out_ref):
    rows = block.shape[0]
    similar = (mine[...] + other[...]) * (1.0 / math.sqrt(model_width))
    alignment = align_block(similar, len_ref[slot : slot + 1, :rows], sharp_ref[:, 0:1])
    term = weight_ref[slot : slot + 1, 0:1] * jnp.dot(
        alignment.astype(jnp.bfloat16), block[...], preferred_element_type=jnp.float32
    )
    out_ref[...] = (acc[...] + term).astype(out_ref.dtype)


def per_device_by_target(
    query_res, target_res, target_len, hits, sharpness, query_pool, target_pool
):
    model_width = query_pool.shape[1]
    target_rows = target_res.shape[1]
    query = query_res[0]
    at_tgt, at_qry, at_rep = (lax.axis_index(name) for name in ("tgt", "qry", "rep"))

    def from_peer(array, k):
        return lax.ppermute(array, "tgt", [(i, i ^ k) for i in range(4)])

    def across(array, axis):
        return lax.ppermute(array, axis, [(0, 1), (1, 0)])

    def after(array, *done):
        return lax.optimization_barrier((array, *done))[0]

    split = [(2 * i + c, 2 * (i ^ (1 + c)) + c) for i in range(4) for c in range(2)]
    pool_split = lax.ppermute(target_pool, ("tgt", "rep"), split)
    pool_last = from_peer(target_pool, 3)
    pool_other = across(pool_split, "rep")
    owners = jnp.stack([at_tgt, at_tgt ^ (1 + at_rep), at_tgt ^ (2 - at_rep), at_tgt ^ 3])

    share = lax.dynamic_index_in_dim(target_res, at_qry, 0, keepdims=False)
    rest = lax.dynamic_index_in_dim(target_res, 1 - at_qry, 0, keepdims=False)
    far = from_peer(share, 2)
    near = from_peer(share, 1)

    bases = [2 * (at_tgt ^ k) for k in range(4)]
    slots = [bases[0], bases[0] + 1]
    for base in bases[1:]:
        slots += [base + at_qry, base + 1 - at_qry]
    slots = jnp.stack(slots).astype(jnp.int32)[:, None]
    named = slots == jnp.arange(len(target_len))[None]
    lengths = jnp.sum(jnp.where(named, target_len[None], 0), axis=1, keepdims=True)
    lengths = jnp.broadcast_to(lengths.astype(jnp.float32), (len(target_len), target_rows))
    half_sharp = jnp.broadcast_to(0.5 * sharpness, (1, target_rows))

    def aligned(slots, mine, other):
        return align(model_width, slots, lengths, half_sharp, mine, other)

    far = after(far, pool_split, pool_last)
    near = after(near, far)
    far = after(far, near)
    last = from_peer(far, 1)
    far_rest = across(far, "qry")
    near_rest = from_peer(after(rest, far), 1)

    posterior, weights = call_kernel(
        weigh_kernel,
        (
            jax.ShapeDtypeStruct((1, len(target_len)), jnp.float32),
            jax.ShapeDtypeStruct((len(target_len), target_rows), jnp.float32),
        ),
        slots,
        hits,
        query_pool,
        owners.astype(jnp.int32)[:, None],
        target_pool,
        pool_split,
        pool_other,
        pool_last,
    )

    one_blocks = [target_res[0], target_res[1], near, far]
    one = partial_similar(query, one_blocks)
    one_other = across(one, "rep")
    one_aligned = aligned((0, 1, 2, 4), one, one_other)

    last = after(last, weights, one_aligned)
    last_rest = across(last, "qry")
    three = partial_similar(query, [last])
    three_other = across(three, "rep")
    three_aligned = aligned((6,), three, three_other)
    four_blocks = [far_rest, near_rest]
    four = partial_similar(after(query, three_aligned), four_blocks)
    four_other = across(four, "rep")
    five = partial_similar(after(query, four), [last_rest])
    five_other = across(five, "rep")
    four_aligned = aligned((5, 3), after(four, five), four_other)
    acc = call_kernel(
        functools.partial(profile_kernel, ((0, 1, 2, 4), (6,), (5, 3))),
        jax.ShapeDtypeStruct(query.shape, jnp.float32),
        weights,
        one_aligned,
        three_aligned,
        four_aligned,
        *one_blocks,
        last,
        *four_blocks,
    )
    profile = call_kernel(
        functools.partial(last_kernel, model_width, 7),
        jax.ShapeDtypeStruct(query.shape, jnp.bfloat16),
        lengths,
        half_sharp,
        weights,
        five,
        five_other,
        last_rest,
        acc,
    )
    return (profile[None], posterior)


def solution(mesh):
    placed = (
        P(("grp", "tgt", "qry"), None, "rep"),
        P(("grp", "tgt"), None, "rep"),
        P("grp"),
        P(("grp", "tgt", "qry"), None),
        P(("grp", "tgt", "qry")),
        P(("grp", "tgt", "qry"), None),
        P(("grp", "tgt"), None),
    )
    groups = mesh.shape["tgt"]

    def per_device(*arrays):
        query_res, target_res, _, hits = arrays[:4]
        few = (
            query_res.shape[0] == 1
            and groups == 4 <= hits.shape[1] // target_res.shape[0]
            and target_res.shape[0] == mesh.shape["qry"] == 2
            and mesh.shape["rep"] == 2
        )
        return (per_device_by_target if few else per_device_by_hit)(*arrays)

    return jax.shard_map(
        per_device,
        mesh=mesh,
        in_specs=placed,
        out_specs=(P(("grp", "tgt", "qry"), None, "rep"), P(("grp", "tgt", "qry"), None)),
        check_vma=False,
    )
```

```python
import functools
import math

import jax
import jax.numpy as jnp
from jax import lax
from jax.experimental import pallas as pl
from jax.experimental.pallas import tpu as pltpu
from jax.sharding import PartitionSpec as P

VMEM_BYTES = 16 * 1024 * 1024


def softmax_rows(logits):
    highest = jnp.max(logits, axis=-1, keepdims=True)
    raised = jnp.exp(logits - highest)
    return raised / jnp.sum(raised, axis=-1, keepdims=True)


def weigh_alignment(similar, lengths, sharpness, hit_weight):
    target_rows = similar.shape[-1]
    inside = jnp.arange(target_rows)[None, None, None, :] < lengths[:, :, None, None]
    counted = lengths[:, :, None, None].astype(jnp.float32)
    row_mean = jnp.sum(jnp.where(inside, similar, 0.0), axis=-1, keepdims=True) / counted
    row_diff = similar - row_mean
    row_var = jnp.sum(jnp.where(inside, row_diff * row_diff, 0.0), axis=-1, keepdims=True) / counted
    row_score = row_diff / jnp.sqrt(row_var + 1e-05)
    column_mean = jnp.mean(similar, axis=2, keepdims=True)
    column_diff = similar - column_mean
    column_var = jnp.mean(column_diff * column_diff, axis=2, keepdims=True)
    column_score = column_diff / jnp.sqrt(column_var + 1e-05)
    scores = sharpness[:, None, None, None] * (0.5 * (row_score + column_score))
    scores = jnp.where(inside, scores, -jnp.inf)
    alignment = softmax_rows(scores)
    return (hit_weight[:, :, None, None] * alignment).astype(jnp.bfloat16)


def plan_slots(flat_hits, owned_targets, tgt_count, capacity):
    owners = flat_hits // owned_targets
    local_ids = flat_hits % owned_targets
    matched = owners[:, None] == jnp.arange(tgt_count)[None, :]
    earlier = jnp.cumsum(matched.astype(jnp.int32), axis=0) - 1
    rank_in = jnp.sum(jnp.where(matched, earlier, 0), axis=1)
    slot_of = owners * capacity + rank_in
    placed = slot_of[:, None] == jnp.arange(tgt_count * capacity)[None, :]
    wanted = jnp.sum(jnp.where(placed, local_ids[:, None], 0), axis=0).reshape(tgt_count, capacity)
    return (wanted, slot_of)


def fetch_shares(target_res, flat_hits, capacity):
    tgt_count = lax.axis_size("tgt")
    owned_targets, target_rows, width = target_res.shape
    wanted, slot_of = plan_slots(flat_hits, owned_targets, tgt_count, capacity)
    requested = lax.all_to_all(wanted, "tgt", split_axis=0, concat_axis=0, tiled=True)
    outgoing = jnp.take(target_res, requested.reshape(tgt_count * capacity), axis=0)
    outgoing = outgoing.reshape(tgt_count, capacity, target_rows, width)
    arrived = lax.all_to_all(outgoing, "tgt", split_axis=0, concat_axis=0, tiled=True)
    return jnp.take(arrived.reshape(tgt_count * capacity, target_rows, width), slot_of, axis=0)


def per_device_by_hit(query_res, target_res, target_len, hits, sharpness, query_pool, target_pool):
    tgt_count = lax.axis_size("tgt")
    query_count = query_res.shape[0]
    target_rows = target_res.shape[1]
    hit_count = hits.shape[1]
    pair_count = query_count * hit_count
    model_width = query_pool.shape[1]
    capacity = max(2, (2 * pair_count + tgt_count - 1) // tgt_count)
    library = lax.all_gather(target_pool, "tgt", axis=0, tiled=True)
    logits = jnp.dot(query_pool, library.T, precision=lax.Precision.HIGHEST) / math.sqrt(
        model_width
    )
    posterior = softmax_rows(logits)
    matches = hits[:, :, None] == jnp.arange(library.shape[0])[None, None, :]
    hit_weight = softmax_rows(jnp.sum(jnp.where(matches, logits[:, None, :], 0.0), axis=-1))
    lengths = jnp.sum(jnp.where(matches, target_len[None, None, :], 0), axis=-1)
    half_width = query_res.shape[2]
    chosen = fetch_shares(target_res, hits.reshape(pair_count), capacity)
    chosen = chosen.reshape(query_count, hit_count, target_rows, half_width)
    partial_sim = jnp.einsum(
        "qid,qhjd->qhij", query_res, chosen, preferred_element_type=jnp.float32
    ) / math.sqrt(model_width)
    similar = lax.psum(partial_sim, "rep")
    weighted = weigh_alignment(similar, lengths, sharpness, hit_weight)
    profile = jnp.einsum("qhij,qhjd->qid", weighted, chosen, preferred_element_type=jnp.float32)
    return (profile.astype(jnp.bfloat16), posterior)


VMEM = pl.BlockSpec(memory_space=pltpu.VMEM)


def call_kernel(kernel, out_shape, *operands, scratch=(), flops=0):
    return pl.pallas_call(
        kernel,
        out_shape=out_shape,
        in_specs=[VMEM] * len(operands),
        out_specs=jax.tree.map(lambda _: VMEM, out_shape),
        scratch_shapes=scratch,
        cost_estimate=pl.CostEstimate(flops=flops, bytes_accessed=0, transcendentals=0),
        compiler_params=pltpu.CompilerParams(vmem_limit_bytes=VMEM_BYTES),
    )(*operands)


def share_kernel(at_ref, blocks_ref, out_ref, done):
    copy = pltpu.make_async_copy(blocks_ref.at[at_ref[0]], out_ref, done)
    copy.start()
    copy.wait()


def take_share(blocks, at):
    return pl.pallas_call(
        share_kernel,
        out_shape=jax.ShapeDtypeStruct(blocks.shape[1:], blocks.dtype),
        in_specs=[pl.BlockSpec(memory_space=pltpu.SMEM), pl.BlockSpec(memory_space=pl.ANY)],
        out_specs=pl.BlockSpec(memory_space=pl.ANY),
        scratch_shapes=[pltpu.SemaphoreType.DMA],
        cost_estimate=pl.CostEstimate(flops=0, bytes_accessed=0, transcendentals=0),
        compiler_params=pltpu.CompilerParams(vmem_limit_bytes=VMEM_BYTES),
    )(at.astype(jnp.int32)[None], blocks)


def weigh_kernel(slot_ref, hits_ref, pool_ref, owner_ref, *refs):
    libs, (posterior_ref, weight_ref) = refs[:-2], refs[-2:]
    owned, width = libs[0].shape
    target_count = posterior_ref.shape[1]
    lane = lax.broadcasted_iota(jnp.int32, (1, target_count), 1)
    pool, hits = pool_ref[...], hits_ref[...]
    logits = jnp.zeros((1, target_count), jnp.float32)
    counts = jnp.zeros((1, target_count), jnp.float32)
    for at, lib in enumerate(libs):
        products = jnp.sum(lib[...] * pool, axis=1, keepdims=True) / math.sqrt(width)
        first = owner_ref[at : at + 1, :] * owned
        for a in range(owned):
            logits = jnp.where(lane == first + a, products[a : a + 1, :], logits)
    for t in range(target_count):
        named = jnp.sum(jnp.where(hits == t, 1.0, 0.0), axis=1, keepdims=True)
        counts = jnp.where(lane == t, named, counts)
    raised = jnp.exp(logits - jnp.max(logits, axis=1, keepdims=True))
    posterior_ref[...] = raised / jnp.sum(raised, axis=1, keepdims=True)
    shown = jnp.where(counts > 0.0, logits, -jnp.inf)
    parts = counts * jnp.exp(shown - jnp.max(shown, axis=1, keepdims=True))
    weights = parts / jnp.sum(parts, axis=1, keepdims=True)
    weights = jnp.sum(jnp.where(slot_ref[...] == lane, weights, 0.0), axis=1, keepdims=True)
    weight_ref[...] = jnp.broadcast_to(weights, weight_ref.shape)


def partial_kernel(*refs):
    query, blocks, out = refs[0], refs[1:-1], refs[-1]
    rows = 0
    for block in blocks:
        out[:, rows : rows + block.shape[0]] = lax.dot_general(
            query[...], block[...], (((1,), (1,)), ((), ())), preferred_element_type=jnp.float32
        )
        rows += block.shape[0]


def partial_similar(query, blocks):
    rows = sum(block.shape[0] for block in blocks)
    shape = jax.ShapeDtypeStruct((query.shape[0], rows), jnp.float32)
    return call_kernel(partial_kernel, shape, query, *blocks)


def align_block(similar, length, half_sharp):
    column = lax.broadcasted_iota(jnp.int32, (1, similar.shape[1]), 1).astype(jnp.float32)
    inside = column < length
    fraction = 1.0 / length[:, 0:1]
    row_mean = jnp.sum(jnp.where(inside, similar, 0.0), axis=1, keepdims=True) * fraction
    row_diff = similar - row_mean
    row_var = (
        jnp.sum(jnp.where(inside, row_diff * row_diff, 0.0), axis=1, keepdims=True) * fraction
    )
    column_mean = jnp.mean(similar, axis=0, keepdims=True)
    column_diff = similar - column_mean
    column_var = jnp.mean(column_diff * column_diff, axis=0, keepdims=True)
    scores = row_diff * (half_sharp * lax.rsqrt(row_var + 1e-05)) + column_diff * (
        half_sharp * lax.rsqrt(column_var + 1e-05)
    )
    scores = jnp.where(inside, scores, -jnp.inf)
    raised = jnp.exp(scores - jnp.max(scores, axis=1, keepdims=True))
    return raised / jnp.sum(raised, axis=1, keepdims=True)


def align_kernel(model_width, slots, len_ref, sharp_ref, mine, other, out_ref):
    scale = 1.0 / math.sqrt(model_width)
    rows = mine.shape[1] // len(slots)
    for at, slot in enumerate(slots):
        part = pl.ds(at * rows, rows)
        similar = (mine[:, part] + other[:, part]) * scale
        alignment = align_block(similar, len_ref[slot : slot + 1, :rows], sharp_ref[:, 0:1])
        out_ref[:, part] = alignment.astype(out_ref.dtype)


def align(model_width, slots, lengths, half_sharp, mine, other):
    return call_kernel(
        functools.partial(align_kernel, model_width, slots),
        jax.ShapeDtypeStruct(mine.shape, jnp.bfloat16),
        lengths,
        half_sharp,
        mine,
        other,
    )


def profile_kernel(groups, weight_ref, *refs):
    aligned, blocks, out_ref = refs[: len(groups)], refs[len(groups) : -1], refs[-1]
    rows = blocks[0].shape[0]
    acc, at = None, 0
    for group, slots in zip(aligned, groups):
        for i, slot in enumerate(slots):
            term = weight_ref[slot : slot + 1, 0:1] * jnp.dot(
                group[:, i * rows : (i + 1) * rows],
                blocks[at][...],
                preferred_element_type=jnp.float32,
            )
            acc = term if acc is None else acc + term
            at += 1
    out_ref[...] = acc


def last_kernel(model_width, slot, len_ref, sharp_ref, weight_ref, mine, other, block, acc, out_ref):
    rows = block.shape[0]
    similar = (mine[...] + other[...]) * (1.0 / math.sqrt(model_width))
    alignment = align_block(similar, len_ref[slot : slot + 1, :rows], sharp_ref[:, 0:1])
    term = weight_ref[slot : slot + 1, 0:1] * jnp.dot(
        alignment.astype(jnp.bfloat16), block[...], preferred_element_type=jnp.float32
    )
    out_ref[...] = (acc[...] + term).astype(out_ref.dtype)


def per_device_by_target(
    query_res, target_res, target_len, hits, sharpness, query_pool, target_pool
):
    model_width = query_pool.shape[1]
    target_rows = target_res.shape[1]
    query = query_res[0]
    at_tgt, at_qry, at_rep = (lax.axis_index(name) for name in ("tgt", "qry", "rep"))

    def from_peer(array, k):
        return lax.ppermute(array, "tgt", [(i, i ^ k) for i in range(4)])

    def across(array, axis):
        return lax.ppermute(array, axis, [(0, 1), (1, 0)])

    def after(array, *done):
        return lax.optimization_barrier((array, *done))[0]

    split = [(2 * i + c, 2 * (i ^ (1 + c)) + c) for i in range(4) for c in range(2)]
    pool_split = lax.ppermute(target_pool, ("tgt", "rep"), split)
    pool_last = from_peer(target_pool, 3)
    pool_other = across(pool_split, "rep")
    owners = jnp.stack([at_tgt, at_tgt ^ (1 + at_rep), at_tgt ^ (2 - at_rep), at_tgt ^ 3])

    share = take_share(target_res, at_qry)
    rest = lax.dynamic_index_in_dim(target_res, 1 - at_qry, 0, keepdims=False)
    far = from_peer(share, 2)
    near = from_peer(share, 1)

    bases = [2 * (at_tgt ^ k) for k in range(4)]
    slots = [bases[0], bases[0] + 1]
    for base in bases[1:]:
        slots += [base + at_qry, base + 1 - at_qry]
    slots = jnp.stack(slots).astype(jnp.int32)[:, None]
    named = slots == jnp.arange(len(target_len))[None]
    lengths = jnp.sum(jnp.where(named, target_len[None], 0), axis=1, keepdims=True)
    lengths = jnp.broadcast_to(lengths.astype(jnp.float32), (len(target_len), target_rows))
    half_sharp = jnp.broadcast_to(0.5 * sharpness, (1, target_rows))

    def aligned(slots, mine, other):
        return align(model_width, slots, lengths, half_sharp, mine, other)

    far = after(far, pool_split, pool_last)
    near = after(near, far)
    far = after(far, near)
    last = from_peer(far, 1)
    far_rest = across(far, "qry")
    near_rest = from_peer(after(rest, far), 1)

    one_blocks = [target_res[0], target_res[1], near, far]
    one = partial_similar(query, one_blocks)
    one_other = across(one, "rep")

    last_rest = across(last, "qry")
    three = partial_similar(query, [last])
    three_other = across(three, "rep")
    three_aligned = aligned((6,), three, three_other)
    four_blocks = [far_rest, near_rest]
    four = partial_similar(after(query, three_aligned), four_blocks)
    four_other = across(four, "rep")
    posterior, weights = call_kernel(
        weigh_kernel,
        (
            jax.ShapeDtypeStruct((1, len(target_len)), jnp.float32),
            jax.ShapeDtypeStruct((len(target_len), target_rows), jnp.float32),
        ),
        slots,
        after(hits, four),
        query_pool,
        owners.astype(jnp.int32)[:, None],
        target_pool,
        pool_split,
        pool_other,
        pool_last,
    )
    one_aligned = aligned((0, 1, 2, 4), after(one, four), one_other)
    five = partial_similar(after(query, weights, one_aligned), [last_rest])
    five_other = across(five, "rep")
    four_aligned = aligned((5, 3), after(four, five), four_other)
    acc = call_kernel(
        functools.partial(profile_kernel, ((0, 1, 2, 4), (6,), (5, 3))),
        jax.ShapeDtypeStruct(query.shape, jnp.float32),
        weights,
        one_aligned,
        three_aligned,
        four_aligned,
        *one_blocks,
        last,
        *four_blocks,
    )
    profile = call_kernel(
        functools.partial(last_kernel, model_width, 7),
        jax.ShapeDtypeStruct(query.shape, jnp.bfloat16),
        lengths,
        half_sharp,
        weights,
        five,
        five_other,
        last_rest,
        acc,
    )
    return (profile[None], posterior)


def solution(mesh):
    placed = (
        P(("grp", "tgt", "qry"), None, "rep"),
        P(("grp", "tgt"), None, "rep"),
        P("grp"),
        P(("grp", "tgt", "qry"), None),
        P(("grp", "tgt", "qry")),
        P(("grp", "tgt", "qry"), None),
        P(("grp", "tgt"), None),
    )
    groups = mesh.shape["tgt"]

    def per_device(*arrays):
        query_res, target_res, _, hits = arrays[:4]
        few = (
            query_res.shape[0] == 1
            and groups == 4 <= hits.shape[1] // target_res.shape[0]
            and target_res.shape[0] == mesh.shape["qry"] == 2
            and mesh.shape["rep"] == 2
        )
        return (per_device_by_target if few else per_device_by_hit)(*arrays)

    return jax.shard_map(
        per_device,
        mesh=mesh,
        in_specs=placed,
        out_specs=(P(("grp", "tgt", "qry"), None, "rep"), P(("grp", "tgt", "qry"), None)),
        check_vma=False,
    )
```

```python
import functools
import math

import jax
import jax.numpy as jnp
from jax import lax
from jax.experimental import pallas as pl
from jax.experimental.pallas import tpu as pltpu
from jax.sharding import PartitionSpec as P

VMEM_BYTES = 16 * 1024 * 1024


def softmax_rows(logits):
    highest = jnp.max(logits, axis=-1, keepdims=True)
    raised = jnp.exp(logits - highest)
    return raised / jnp.sum(raised, axis=-1, keepdims=True)


def weigh_alignment(similar, lengths, sharpness, hit_weight):
    target_rows = similar.shape[-1]
    inside = jnp.arange(target_rows)[None, None, None, :] < lengths[:, :, None, None]
    counted = lengths[:, :, None, None].astype(jnp.float32)
    row_mean = jnp.sum(jnp.where(inside, similar, 0.0), axis=-1, keepdims=True) / counted
    row_diff = similar - row_mean
    row_var = jnp.sum(jnp.where(inside, row_diff * row_diff, 0.0), axis=-1, keepdims=True) / counted
    row_score = row_diff / jnp.sqrt(row_var + 1e-05)
    column_mean = jnp.mean(similar, axis=2, keepdims=True)
    column_diff = similar - column_mean
    column_var = jnp.mean(column_diff * column_diff, axis=2, keepdims=True)
    column_score = column_diff / jnp.sqrt(column_var + 1e-05)
    scores = sharpness[:, None, None, None] * (0.5 * (row_score + column_score))
    scores = jnp.where(inside, scores, -jnp.inf)
    alignment = softmax_rows(scores)
    return (hit_weight[:, :, None, None] * alignment).astype(jnp.bfloat16)


def plan_slots(flat_hits, owned_targets, tgt_count, capacity):
    owners = flat_hits // owned_targets
    local_ids = flat_hits % owned_targets
    matched = owners[:, None] == jnp.arange(tgt_count)[None, :]
    earlier = jnp.cumsum(matched.astype(jnp.int32), axis=0) - 1
    rank_in = jnp.sum(jnp.where(matched, earlier, 0), axis=1)
    slot_of = owners * capacity + rank_in
    placed = slot_of[:, None] == jnp.arange(tgt_count * capacity)[None, :]
    wanted = jnp.sum(jnp.where(placed, local_ids[:, None], 0), axis=0).reshape(tgt_count, capacity)
    return (wanted, slot_of)


def fetch_shares(target_res, flat_hits, capacity):
    tgt_count = lax.axis_size("tgt")
    owned_targets, target_rows, width = target_res.shape
    wanted, slot_of = plan_slots(flat_hits, owned_targets, tgt_count, capacity)
    requested = lax.all_to_all(wanted, "tgt", split_axis=0, concat_axis=0, tiled=True)
    outgoing = jnp.take(target_res, requested.reshape(tgt_count * capacity), axis=0)
    outgoing = outgoing.reshape(tgt_count, capacity, target_rows, width)
    arrived = lax.all_to_all(outgoing, "tgt", split_axis=0, concat_axis=0, tiled=True)
    return jnp.take(arrived.reshape(tgt_count * capacity, target_rows, width), slot_of, axis=0)


def per_device_by_hit(query_res, target_res, target_len, hits, sharpness, query_pool, target_pool):
    tgt_count = lax.axis_size("tgt")
    query_count = query_res.shape[0]
    target_rows = target_res.shape[1]
    hit_count = hits.shape[1]
    pair_count = query_count * hit_count
    model_width = query_pool.shape[1]
    capacity = max(2, (2 * pair_count + tgt_count - 1) // tgt_count)
    library = lax.all_gather(target_pool, "tgt", axis=0, tiled=True)
    logits = jnp.dot(query_pool, library.T, precision=lax.Precision.HIGHEST) / math.sqrt(
        model_width
    )
    posterior = softmax_rows(logits)
    matches = hits[:, :, None] == jnp.arange(library.shape[0])[None, None, :]
    hit_weight = softmax_rows(jnp.sum(jnp.where(matches, logits[:, None, :], 0.0), axis=-1))
    lengths = jnp.sum(jnp.where(matches, target_len[None, None, :], 0), axis=-1)
    half_width = query_res.shape[2]
    chosen = fetch_shares(target_res, hits.reshape(pair_count), capacity)
    chosen = chosen.reshape(query_count, hit_count, target_rows, half_width)
    partial_sim = jnp.einsum(
        "qid,qhjd->qhij", query_res, chosen, preferred_element_type=jnp.float32
    ) / math.sqrt(model_width)
    similar = lax.psum(partial_sim, "rep")
    weighted = weigh_alignment(similar, lengths, sharpness, hit_weight)
    profile = jnp.einsum("qhij,qhjd->qid", weighted, chosen, preferred_element_type=jnp.float32)
    return (profile.astype(jnp.bfloat16), posterior)


VMEM = pl.BlockSpec(memory_space=pltpu.VMEM)


def call_kernel(kernel, out_shape, *operands, scratch=(), flops=0):
    return pl.pallas_call(
        kernel,
        out_shape=out_shape,
        in_specs=[VMEM] * len(operands),
        out_specs=jax.tree.map(lambda _: VMEM, out_shape),
        scratch_shapes=scratch,
        cost_estimate=pl.CostEstimate(flops=flops, bytes_accessed=0, transcendentals=0),
        compiler_params=pltpu.CompilerParams(vmem_limit_bytes=VMEM_BYTES),
    )(*operands)


def weigh_kernel(slot_ref, hits_ref, pool_ref, owner_ref, *refs):
    libs, (posterior_ref, weight_ref) = refs[:-2], refs[-2:]
    owned, width = libs[0].shape
    target_count = posterior_ref.shape[1]
    lane = lax.broadcasted_iota(jnp.int32, (1, target_count), 1)
    pool, hits = pool_ref[...], hits_ref[...]
    logits = jnp.zeros((1, target_count), jnp.float32)
    counts = jnp.zeros((1, target_count), jnp.float32)
    for at, lib in enumerate(libs):
        products = jnp.sum(lib[...] * pool, axis=1, keepdims=True) / math.sqrt(width)
        first = owner_ref[at : at + 1, :] * owned
        for a in range(owned):
            logits = jnp.where(lane == first + a, products[a : a + 1, :], logits)
    for t in range(target_count):
        named = jnp.sum(jnp.where(hits == t, 1.0, 0.0), axis=1, keepdims=True)
        counts = jnp.where(lane == t, named, counts)
    raised = jnp.exp(logits - jnp.max(logits, axis=1, keepdims=True))
    posterior_ref[...] = raised / jnp.sum(raised, axis=1, keepdims=True)
    shown = jnp.where(counts > 0.0, logits, -jnp.inf)
    parts = counts * jnp.exp(shown - jnp.max(shown, axis=1, keepdims=True))
    weights = parts / jnp.sum(parts, axis=1, keepdims=True)
    weights = jnp.sum(jnp.where(slot_ref[...] == lane, weights, 0.0), axis=1, keepdims=True)
    weight_ref[...] = jnp.broadcast_to(weights, weight_ref.shape)


def partial_kernel(*refs):
    query, blocks, out = refs[0], refs[1:-1], refs[-1]
    rows = 0
    for block in blocks:
        out[:, rows : rows + block.shape[0]] = lax.dot_general(
            query[...], block[...], (((1,), (1,)), ((), ())), preferred_element_type=jnp.float32
        )
        rows += block.shape[0]


def partial_similar(query, blocks):
    rows = sum(block.shape[0] for block in blocks)
    shape = jax.ShapeDtypeStruct((query.shape[0], rows), jnp.float32)
    return call_kernel(partial_kernel, shape, query, *blocks)


def align_block(similar, length, half_sharp):
    column = lax.broadcasted_iota(jnp.int32, (1, similar.shape[1]), 1).astype(jnp.float32)
    inside = column < length
    fraction = 1.0 / length[:, 0:1]
    row_mean = jnp.sum(jnp.where(inside, similar, 0.0), axis=1, keepdims=True) * fraction
    row_diff = similar - row_mean
    row_var = (
        jnp.sum(jnp.where(inside, row_diff * row_diff, 0.0), axis=1, keepdims=True) * fraction
    )
    column_mean = jnp.mean(similar, axis=0, keepdims=True)
    column_diff = similar - column_mean
    column_var = jnp.mean(column_diff * column_diff, axis=0, keepdims=True)
    scores = row_diff * (half_sharp * lax.rsqrt(row_var + 1e-05)) + column_diff * (
        half_sharp * lax.rsqrt(column_var + 1e-05)
    )
    scores = jnp.where(inside, scores, -jnp.inf)
    raised = jnp.exp(scores - jnp.max(scores, axis=1, keepdims=True))
    return raised / jnp.sum(raised, axis=1, keepdims=True)


def align_kernel(model_width, slots, len_ref, sharp_ref, mine, other, out_ref):
    scale = 1.0 / math.sqrt(model_width)
    rows = mine.shape[1] // len(slots)
    for at, slot in enumerate(slots):
        part = pl.ds(at * rows, rows)
        similar = (mine[:, part] + other[:, part]) * scale
        alignment = align_block(similar, len_ref[slot : slot + 1, :rows], sharp_ref[:, 0:1])
        out_ref[:, part] = alignment.astype(out_ref.dtype)


def align(model_width, slots, lengths, half_sharp, mine, other):
    return call_kernel(
        functools.partial(align_kernel, model_width, slots),
        jax.ShapeDtypeStruct(mine.shape, jnp.bfloat16),
        lengths,
        half_sharp,
        mine,
        other,
    )


def profile_kernel(groups, weight_ref, *refs):
    aligned, blocks, out_ref = refs[: len(groups)], refs[len(groups) : -1], refs[-1]
    rows = blocks[0].shape[0]
    acc, at = None, 0
    for group, slots in zip(aligned, groups):
        for i, slot in enumerate(slots):
            term = weight_ref[slot : slot + 1, 0:1] * jnp.dot(
                group[:, i * rows : (i + 1) * rows],
                blocks[at][...],
                preferred_element_type=jnp.float32,
            )
            acc = term if acc is None else acc + term
            at += 1
    out_ref[...] = acc


def last_kernel(model_width, slot, len_ref, sharp_ref, weight_ref, mine, other, block, acc, out_ref):
    rows = block.shape[0]
    similar = (mine[...] + other[...]) * (1.0 / math.sqrt(model_width))
    alignment = align_block(similar, len_ref[slot : slot + 1, :rows], sharp_ref[:, 0:1])
    term = weight_ref[slot : slot + 1, 0:1] * jnp.dot(
        alignment.astype(jnp.bfloat16), block[...], preferred_element_type=jnp.float32
    )
    out_ref[...] = (acc[...] + term).astype(out_ref.dtype)


def per_device_by_target(
    query_res, target_res, target_len, hits, sharpness, query_pool, target_pool
):
    model_width = query_pool.shape[1]
    target_rows = target_res.shape[1]
    query = query_res[0]
    at_tgt, at_qry, at_rep = (lax.axis_index(name) for name in ("tgt", "qry", "rep"))

    def from_peer(array, k):
        return lax.ppermute(array, "tgt", [(i, i ^ k) for i in range(4)])

    def across(array, axis):
        return lax.ppermute(array, axis, [(0, 1), (1, 0)])

    def after(array, *done):
        return lax.optimization_barrier((array, *done))[0]

    split = [(2 * i + c, 2 * (i ^ (1 + c)) + c) for i in range(4) for c in range(2)]
    pool_split = lax.ppermute(target_pool, ("tgt", "rep"), split)
    pool_last = from_peer(target_pool, 3)
    pool_other = across(pool_split, "rep")
    owners = jnp.stack([at_tgt, at_tgt ^ (1 + at_rep), at_tgt ^ (2 - at_rep), at_tgt ^ 3])

    share = lax.dynamic_index_in_dim(target_res, at_qry, 0, keepdims=False)
    rest = lax.dynamic_index_in_dim(target_res, 1 - at_qry, 0, keepdims=False)
    far = from_peer(share, 2)
    near = from_peer(share, 1)

    bases = [2 * (at_tgt ^ k) for k in range(4)]
    slots = [bases[0], bases[0] + 1]
    for base in bases[1:]:
        slots += [base + at_qry, base + 1 - at_qry]
    slots = jnp.stack(slots).astype(jnp.int32)[:, None]
    named = slots == jnp.arange(len(target_len))[None]
    lengths = jnp.sum(jnp.where(named, target_len[None], 0), axis=1, keepdims=True)
    lengths = jnp.broadcast_to(lengths.astype(jnp.float32), (len(target_len), target_rows))
    half_sharp = jnp.broadcast_to(0.5 * sharpness, (1, target_rows))

    def aligned(slots, mine, other):
        return align(model_width, slots, lengths, half_sharp, mine, other)

    far = after(far, pool_split, pool_last)
    near = after(near, far)
    far = after(far, near)
    last = from_peer(far, 1)
    far_rest = across(far, "qry")
    near_rest = from_peer(after(rest, far), 1)

    one_blocks = [target_res[0], target_res[1], near, far]
    one = partial_similar(query, one_blocks)
    one_other = across(one, "rep")
    one_aligned = aligned((0, 1, 2, 4), one, one_other)
    last = after(last, one_aligned)

    last_rest = across(last, "qry")
    three = partial_similar(query, [last])
    three_other = across(three, "rep")
    three_aligned = aligned((6,), three, three_other)
    four_blocks = [far_rest, near_rest]
    four = partial_similar(after(query, three_aligned), four_blocks)
    four_other = across(four, "rep")
    posterior, weights = call_kernel(
        weigh_kernel,
        (
            jax.ShapeDtypeStruct((1, len(target_len)), jnp.float32),
            jax.ShapeDtypeStruct((len(target_len), target_rows), jnp.float32),
        ),
        slots,
        after(hits, four),
        query_pool,
        owners.astype(jnp.int32)[:, None],
        target_pool,
        pool_split,
        pool_other,
        pool_last,
    )
    five = partial_similar(after(query, weights), [last_rest])
    five_other = across(five, "rep")
    four_aligned = aligned((5, 3), after(four, five), four_other)
    acc = call_kernel(
        functools.partial(profile_kernel, ((0, 1, 2, 4), (6,), (5, 3))),
        jax.ShapeDtypeStruct(query.shape, jnp.float32),
        weights,
        one_aligned,
        three_aligned,
        four_aligned,
        *one_blocks,
        last,
        *four_blocks,
    )
    profile = call_kernel(
        functools.partial(last_kernel, model_width, 7),
        jax.ShapeDtypeStruct(query.shape, jnp.bfloat16),
        lengths,
        half_sharp,
        weights,
        five,
        five_other,
        last_rest,
        acc,
    )
    return (profile[None], posterior)


def solution(mesh):
    placed = (
        P(("grp", "tgt", "qry"), None, "rep"),
        P(("grp", "tgt"), None, "rep"),
        P("grp"),
        P(("grp", "tgt", "qry"), None),
        P(("grp", "tgt", "qry")),
        P(("grp", "tgt", "qry"), None),
        P(("grp", "tgt"), None),
    )
    groups = mesh.shape["tgt"]

    def per_device(*arrays):
        query_res, target_res, _, hits = arrays[:4]
        few = (
            query_res.shape[0] == 1
            and groups == 4 <= hits.shape[1] // target_res.shape[0]
            and target_res.shape[0] == mesh.shape["qry"] == 2
            and mesh.shape["rep"] == 2
        )
        return (per_device_by_target if few else per_device_by_hit)(*arrays)

    return jax.shard_map(
        per_device,
        mesh=mesh,
        in_specs=placed,
        out_specs=(P(("grp", "tgt", "qry"), None, "rep"), P(("grp", "tgt", "qry"), None)),
        check_vma=False,
    )
```

```python
import functools
import math

import jax
import jax.numpy as jnp
from jax import lax
from jax.experimental import pallas as pl
from jax.experimental.pallas import tpu as pltpu
from jax.sharding import PartitionSpec as P

VMEM_BYTES = 16 * 1024 * 1024


def softmax_rows(logits):
    highest = jnp.max(logits, axis=-1, keepdims=True)
    raised = jnp.exp(logits - highest)
    return raised / jnp.sum(raised, axis=-1, keepdims=True)


def weigh_alignment(similar, lengths, sharpness, hit_weight):
    target_rows = similar.shape[-1]
    inside = jnp.arange(target_rows)[None, None, None, :] < lengths[:, :, None, None]
    counted = lengths[:, :, None, None].astype(jnp.float32)
    row_mean = jnp.sum(jnp.where(inside, similar, 0.0), axis=-1, keepdims=True) / counted
    row_diff = similar - row_mean
    row_var = jnp.sum(jnp.where(inside, row_diff * row_diff, 0.0), axis=-1, keepdims=True) / counted
    row_score = row_diff / jnp.sqrt(row_var + 1e-05)
    column_mean = jnp.mean(similar, axis=2, keepdims=True)
    column_diff = similar - column_mean
    column_var = jnp.mean(column_diff * column_diff, axis=2, keepdims=True)
    column_score = column_diff / jnp.sqrt(column_var + 1e-05)
    scores = sharpness[:, None, None, None] * (0.5 * (row_score + column_score))
    scores = jnp.where(inside, scores, -jnp.inf)
    alignment = softmax_rows(scores)
    return (hit_weight[:, :, None, None] * alignment).astype(jnp.bfloat16)


def plan_slots(flat_hits, owned_targets, tgt_count, capacity):
    owners = flat_hits // owned_targets
    local_ids = flat_hits % owned_targets
    matched = owners[:, None] == jnp.arange(tgt_count)[None, :]
    earlier = jnp.cumsum(matched.astype(jnp.int32), axis=0) - 1
    rank_in = jnp.sum(jnp.where(matched, earlier, 0), axis=1)
    slot_of = owners * capacity + rank_in
    placed = slot_of[:, None] == jnp.arange(tgt_count * capacity)[None, :]
    wanted = jnp.sum(jnp.where(placed, local_ids[:, None], 0), axis=0).reshape(tgt_count, capacity)
    return (wanted, slot_of)


def fetch_shares(target_res, flat_hits, capacity):
    tgt_count = lax.axis_size("tgt")
    owned_targets, target_rows, width = target_res.shape
    wanted, slot_of = plan_slots(flat_hits, owned_targets, tgt_count, capacity)
    requested = lax.all_to_all(wanted, "tgt", split_axis=0, concat_axis=0, tiled=True)
    outgoing = jnp.take(target_res, requested.reshape(tgt_count * capacity), axis=0)
    outgoing = outgoing.reshape(tgt_count, capacity, target_rows, width)
    arrived = lax.all_to_all(outgoing, "tgt", split_axis=0, concat_axis=0, tiled=True)
    return jnp.take(arrived.reshape(tgt_count * capacity, target_rows, width), slot_of, axis=0)


def per_device_by_hit(query_res, target_res, target_len, hits, sharpness, query_pool, target_pool):
    tgt_count = lax.axis_size("tgt")
    query_count = query_res.shape[0]
    target_rows = target_res.shape[1]
    hit_count = hits.shape[1]
    pair_count = query_count * hit_count
    model_width = query_pool.shape[1]
    capacity = max(2, (2 * pair_count + tgt_count - 1) // tgt_count)
    library = lax.all_gather(target_pool, "tgt", axis=0, tiled=True)
    logits = jnp.dot(query_pool, library.T, precision=lax.Precision.HIGHEST) / math.sqrt(
        model_width
    )
    posterior = softmax_rows(logits)
    matches = hits[:, :, None] == jnp.arange(library.shape[0])[None, None, :]
    hit_weight = softmax_rows(jnp.sum(jnp.where(matches, logits[:, None, :], 0.0), axis=-1))
    lengths = jnp.sum(jnp.where(matches, target_len[None, None, :], 0), axis=-1)
    half_width = query_res.shape[2]
    chosen = fetch_shares(target_res, hits.reshape(pair_count), capacity)
    chosen = chosen.reshape(query_count, hit_count, target_rows, half_width)
    partial_sim = jnp.einsum(
        "qid,qhjd->qhij", query_res, chosen, preferred_element_type=jnp.float32
    ) / math.sqrt(model_width)
    similar = lax.psum(partial_sim, "rep")
    weighted = weigh_alignment(similar, lengths, sharpness, hit_weight)
    profile = jnp.einsum("qhij,qhjd->qid", weighted, chosen, preferred_element_type=jnp.float32)
    return (profile.astype(jnp.bfloat16), posterior)


VMEM = pl.BlockSpec(memory_space=pltpu.VMEM)


def call_kernel(kernel, out_shape, *operands, scratch=(), flops=0):
    return pl.pallas_call(
        kernel,
        out_shape=out_shape,
        in_specs=[VMEM] * len(operands),
        out_specs=jax.tree.map(lambda _: VMEM, out_shape),
        scratch_shapes=scratch,
        cost_estimate=pl.CostEstimate(flops=flops, bytes_accessed=0, transcendentals=0),
        compiler_params=pltpu.CompilerParams(vmem_limit_bytes=VMEM_BYTES),
    )(*operands)


def weigh_kernel(slot_ref, hits_ref, pool_ref, owner_ref, *refs):
    libs, (posterior_ref, weight_ref) = refs[:-2], refs[-2:]
    owned, width = libs[0].shape
    target_count = posterior_ref.shape[1]
    lane = lax.broadcasted_iota(jnp.int32, (1, target_count), 1)
    pool, hits = pool_ref[...], hits_ref[...]
    logits = jnp.zeros((1, target_count), jnp.float32)
    counts = jnp.zeros((1, target_count), jnp.float32)
    for at, lib in enumerate(libs):
        products = jnp.sum(lib[...] * pool, axis=1, keepdims=True) / math.sqrt(width)
        first = owner_ref[at : at + 1, :] * owned
        for a in range(owned):
            logits = jnp.where(lane == first + a, products[a : a + 1, :], logits)
    for t in range(target_count):
        named = jnp.sum(jnp.where(hits == t, 1.0, 0.0), axis=1, keepdims=True)
        counts = jnp.where(lane == t, named, counts)
    raised = jnp.exp(logits - jnp.max(logits, axis=1, keepdims=True))
    posterior_ref[...] = raised / jnp.sum(raised, axis=1, keepdims=True)
    shown = jnp.where(counts > 0.0, logits, -jnp.inf)
    parts = counts * jnp.exp(shown - jnp.max(shown, axis=1, keepdims=True))
    weights = parts / jnp.sum(parts, axis=1, keepdims=True)
    weights = jnp.sum(jnp.where(slot_ref[...] == lane, weights, 0.0), axis=1, keepdims=True)
    weight_ref[...] = jnp.broadcast_to(weights, weight_ref.shape)


def align_block(similar, length, half_sharp):
    column = lax.broadcasted_iota(jnp.int32, (1, similar.shape[1]), 1).astype(jnp.float32)
    inside = column < length
    fraction = 1.0 / length[:, 0:1]
    row_mean = jnp.sum(jnp.where(inside, similar, 0.0), axis=1, keepdims=True) * fraction
    row_diff = similar - row_mean
    row_var = (
        jnp.sum(jnp.where(inside, row_diff * row_diff, 0.0), axis=1, keepdims=True) * fraction
    )
    column_mean = jnp.mean(similar, axis=0, keepdims=True)
    column_diff = similar - column_mean
    column_var = jnp.mean(column_diff * column_diff, axis=0, keepdims=True)
    scores = row_diff * (half_sharp * lax.rsqrt(row_var + 1e-05)) + column_diff * (
        half_sharp * lax.rsqrt(column_var + 1e-05)
    )
    scores = jnp.where(inside, scores, -jnp.inf)
    raised = jnp.exp(scores - jnp.max(scores, axis=1, keepdims=True))
    return raised / jnp.sum(raised, axis=1, keepdims=True)


def similar_block(query, query_other, mine, other, model_width):
    total = 0.0
    for rows, blocks in ((query, mine), (query_other, other)):
        target = jnp.concatenate([block[...] for block in blocks])
        total += lax.dot_general(
            rows[...], target, (((1,), (1,)), ((), ())), preferred_element_type=jnp.float32
        )
    return total * (1.0 / math.sqrt(model_width))


def take_blocks(refs, count):
    return refs[:count], refs[count : 2 * count], refs[2 * count :]


def align_kernel(model_width, targets, len_ref, sharp_ref, query, query_other, *refs):
    out_ref = refs[-1]
    rows = out_ref.shape[1] // len(targets)
    for at, (slot, count) in enumerate(targets):
        mine, other, refs = take_blocks(refs, count)
        similar = similar_block(query, query_other, mine, other, model_width)
        alignment = align_block(similar, len_ref[slot : slot + 1, :rows], sharp_ref[:, 0:1])
        out_ref[:, at * rows : (at + 1) * rows] = alignment.astype(out_ref.dtype)


def weighted_term(weight, alignment, blocks):
    target = jnp.concatenate([block[...] for block in blocks])
    return weight * jnp.dot(alignment, target, preferred_element_type=jnp.float32)


def profile_kernel(groups, weight_ref, *refs):
    aligned, blocks, out_ref = refs[: len(groups)], refs[len(groups) : -1], refs[-1]
    acc = None
    for group, targets in zip(aligned, groups):
        rows = group.shape[1] // len(targets)
        for at, (slot, count) in enumerate(targets):
            term = weighted_term(
                weight_ref[slot : slot + 1, 0:1],
                group[:, at * rows : (at + 1) * rows],
                blocks[:count],
            )
            acc = term if acc is None else acc + term
            blocks = blocks[count:]
    out_ref[...] = acc


def last_kernel(model_width, target, len_ref, sharp_ref, query, query_other, weight_ref, *refs):
    slot, count = target
    mine, other, (acc_ref, out_ref) = take_blocks(refs, count)
    similar = similar_block(query, query_other, mine, other, model_width)
    lengths = len_ref[slot : slot + 1, : similar.shape[1]]
    alignment = align_block(similar, lengths, sharp_ref[:, 0:1])
    term = weighted_term(
        weight_ref[slot : slot + 1, 0:1], alignment.astype(jnp.bfloat16), mine
    )
    out_ref[...] = (acc_ref[...] + term).astype(out_ref.dtype)


def per_device_by_target(
    query_res, target_res, target_len, hits, sharpness, query_pool, target_pool
):
    model_width = query_pool.shape[1]
    target_rows, width = target_res.shape[1:]
    query = query_res[0]
    at_tgt, at_qry, at_rep = (lax.axis_index(name) for name in ("tgt", "qry", "rep"))

    def from_peer(array, k):
        return lax.ppermute(array, "tgt", [(i, i ^ k) for i in range(4)])

    def across(array, axis):
        return lax.ppermute(array, axis, [(0, 1), (1, 0)])

    def after(array, *done):
        return lax.optimization_barrier((array, *done))[0]

    split = [(2 * i + c, 2 * (i ^ (1 + c)) + c) for i in range(4) for c in range(2)]
    owners = jnp.stack([at_tgt, at_tgt ^ (1 + at_rep), at_tgt ^ (2 - at_rep), at_tgt ^ 3])

    share = lax.dynamic_index_in_dim(target_res, at_qry, 0, keepdims=False)
    rest = lax.dynamic_index_in_dim(target_res, 1 - at_qry, 0, keepdims=False)
    far = from_peer(share, 2)
    near = from_peer(share, 1)
    query_other = across(after(query, share), "rep")
    own_other = across(after(target_res, share), "rep")
    pool = after(target_pool, query_other, own_other)
    pool_split = lax.ppermute(pool, ("tgt", "rep"), split)
    pool_last = from_peer(pool, 3)

    bases = [2 * (at_tgt ^ k) for k in range(4)]
    slots = [bases[0], bases[0] + 1]
    for base in bases[1:]:
        slots += [base + at_qry, base + 1 - at_qry]
    slots = jnp.stack(slots).astype(jnp.int32)[:, None]
    named = slots == jnp.arange(len(target_len))[None]
    lengths = jnp.sum(jnp.where(named, target_len[None], 0), axis=1, keepdims=True)
    lengths = jnp.broadcast_to(lengths.astype(jnp.float32), (len(target_len), target_rows))
    half_sharp = jnp.broadcast_to(0.5 * sharpness, (1, target_rows))

    def aligned(slots, blocks, *done):
        return call_kernel(
            functools.partial(align_kernel, model_width, [(slot, 1) for slot in slots]),
            jax.ShapeDtypeStruct((query.shape[0], len(slots) * target_rows), jnp.bfloat16),
            lengths,
            half_sharp,
            after(query, *done) if done else query,
            query_other,
            *blocks,
        )

    far = after(far, pool_split, pool_last)
    near = after(near, far)
    last = from_peer(far, 1)
    near_rest = from_peer(after(rest, far), 1)
    near_other = across(near, "rep")
    far_other = across(far, "rep")
    far_rest = across(after(far, near_other), "qry")

    one = [target_res[0], own_other[0], target_res[1], own_other[1]]
    one += [near, near_other, far, far_other]
    one_aligned = aligned((0, 1, 2, 4), one)

    pool_other = across(after(pool_split, near_other, far_other), "rep")
    posterior, weights = call_kernel(
        weigh_kernel,
        (
            jax.ShapeDtypeStruct((1, len(target_len)), jnp.float32),
            jax.ShapeDtypeStruct((len(target_len), target_rows), jnp.float32),
        ),
        slots,
        after(hits, one_aligned),
        query_pool,
        owners.astype(jnp.int32)[:, None],
        target_pool,
        pool_split,
        pool_other,
        pool_last,
    )

    last = after(last, weights)
    last_rest = across(last, "qry")
    two = [last, across(last, "rep")]
    two_aligned = aligned((6,), two)
    last_rest = after(last_rest, two_aligned)
    last_rest_other = across(last_rest, "rep")
    three = [far_rest, across(far_rest, "rep"), near_rest, across(near_rest, "rep")]
    three_aligned = aligned((5, 3), three, last_rest)
    acc = call_kernel(
        functools.partial(
            profile_kernel,
            (((0, 1), (1, 1), (2, 1), (4, 1)), ((6, 1),), ((5, 1), (3, 1))),
        ),
        jax.ShapeDtypeStruct(query.shape, jnp.float32),
        weights,
        one_aligned,
        two_aligned,
        three_aligned,
        *one[::2],
        *two[::2],
        *three[::2],
    )
    profile = call_kernel(
        functools.partial(last_kernel, model_width, (7, 1)),
        jax.ShapeDtypeStruct(query.shape, jnp.bfloat16),
        lengths,
        half_sharp,
        query,
        query_other,
        weights,
        last_rest,
        last_rest_other,
        acc,
    )
    return (profile[None], posterior)

def solution(mesh):
    placed = (
        P(("grp", "tgt", "qry"), None, "rep"),
        P(("grp", "tgt"), None, "rep"),
        P("grp"),
        P(("grp", "tgt", "qry"), None),
        P(("grp", "tgt", "qry")),
        P(("grp", "tgt", "qry"), None),
        P(("grp", "tgt"), None),
    )
    groups = mesh.shape["tgt"]

    def per_device(*arrays):
        query_res, target_res, _, hits = arrays[:4]
        few = (
            query_res.shape[0] == 1
            and groups == 4 <= hits.shape[1] // target_res.shape[0]
            and target_res.shape[0] == mesh.shape["qry"] == 2
            and mesh.shape["rep"] == 2
        )
        return (per_device_by_target if few else per_device_by_hit)(*arrays)

    return jax.shard_map(
        per_device,
        mesh=mesh,
        in_specs=placed,
        out_specs=(P(("grp", "tgt", "qry"), None, "rep"), P(("grp", "tgt", "qry"), None)),
        check_vma=False,
    )
```

```python
import functools
import math

import jax
import jax.numpy as jnp
from jax import lax
from jax.experimental import pallas as pl
from jax.experimental.pallas import tpu as pltpu
from jax.sharding import PartitionSpec as P

VMEM_BYTES = 16 * 1024 * 1024


def softmax_rows(logits):
    highest = jnp.max(logits, axis=-1, keepdims=True)
    raised = jnp.exp(logits - highest)
    return raised / jnp.sum(raised, axis=-1, keepdims=True)


def weigh_alignment(similar, lengths, sharpness, hit_weight):
    target_rows = similar.shape[-1]
    inside = jnp.arange(target_rows)[None, None, None, :] < lengths[:, :, None, None]
    counted = lengths[:, :, None, None].astype(jnp.float32)
    row_mean = jnp.sum(jnp.where(inside, similar, 0.0), axis=-1, keepdims=True) / counted
    row_diff = similar - row_mean
    row_var = jnp.sum(jnp.where(inside, row_diff * row_diff, 0.0), axis=-1, keepdims=True) / counted
    row_score = row_diff / jnp.sqrt(row_var + 1e-05)
    column_mean = jnp.mean(similar, axis=2, keepdims=True)
    column_diff = similar - column_mean
    column_var = jnp.mean(column_diff * column_diff, axis=2, keepdims=True)
    column_score = column_diff / jnp.sqrt(column_var + 1e-05)
    scores = sharpness[:, None, None, None] * (0.5 * (row_score + column_score))
    scores = jnp.where(inside, scores, -jnp.inf)
    alignment = softmax_rows(scores)
    return (hit_weight[:, :, None, None] * alignment).astype(jnp.bfloat16)


def plan_slots(flat_hits, owned_targets, tgt_count, capacity):
    owners = flat_hits // owned_targets
    local_ids = flat_hits % owned_targets
    matched = owners[:, None] == jnp.arange(tgt_count)[None, :]
    earlier = jnp.cumsum(matched.astype(jnp.int32), axis=0) - 1
    rank_in = jnp.sum(jnp.where(matched, earlier, 0), axis=1)
    slot_of = owners * capacity + rank_in
    placed = slot_of[:, None] == jnp.arange(tgt_count * capacity)[None, :]
    wanted = jnp.sum(jnp.where(placed, local_ids[:, None], 0), axis=0).reshape(tgt_count, capacity)
    return (wanted, slot_of)


def fetch_shares(target_res, flat_hits, capacity):
    tgt_count = lax.axis_size("tgt")
    owned_targets, target_rows, width = target_res.shape
    wanted, slot_of = plan_slots(flat_hits, owned_targets, tgt_count, capacity)
    requested = lax.all_to_all(wanted, "tgt", split_axis=0, concat_axis=0, tiled=True)
    outgoing = jnp.take(target_res, requested.reshape(tgt_count * capacity), axis=0)
    outgoing = outgoing.reshape(tgt_count, capacity, target_rows, width)
    arrived = lax.all_to_all(outgoing, "tgt", split_axis=0, concat_axis=0, tiled=True)
    return jnp.take(arrived.reshape(tgt_count * capacity, target_rows, width), slot_of, axis=0)


def per_device_by_hit(query_res, target_res, target_len, hits, sharpness, query_pool, target_pool):
    tgt_count = lax.axis_size("tgt")
    query_count = query_res.shape[0]
    target_rows = target_res.shape[1]
    hit_count = hits.shape[1]
    pair_count = query_count * hit_count
    model_width = query_pool.shape[1]
    capacity = max(2, (2 * pair_count + tgt_count - 1) // tgt_count)
    library = lax.all_gather(target_pool, "tgt", axis=0, tiled=True)
    logits = jnp.dot(query_pool, library.T, precision=lax.Precision.HIGHEST) / math.sqrt(
        model_width
    )
    posterior = softmax_rows(logits)
    matches = hits[:, :, None] == jnp.arange(library.shape[0])[None, None, :]
    hit_weight = softmax_rows(jnp.sum(jnp.where(matches, logits[:, None, :], 0.0), axis=-1))
    lengths = jnp.sum(jnp.where(matches, target_len[None, None, :], 0), axis=-1)
    half_width = query_res.shape[2]
    chosen = fetch_shares(target_res, hits.reshape(pair_count), capacity)
    chosen = chosen.reshape(query_count, hit_count, target_rows, half_width)
    partial_sim = jnp.einsum(
        "qid,qhjd->qhij", query_res, chosen, preferred_element_type=jnp.float32
    ) / math.sqrt(model_width)
    similar = lax.psum(partial_sim, "rep")
    weighted = weigh_alignment(similar, lengths, sharpness, hit_weight)
    profile = jnp.einsum("qhij,qhjd->qid", weighted, chosen, preferred_element_type=jnp.float32)
    return (profile.astype(jnp.bfloat16), posterior)


VMEM = pl.BlockSpec(memory_space=pltpu.VMEM)


def call_kernel(kernel, out_shape, *operands, scratch=(), flops=0):
    return pl.pallas_call(
        kernel,
        out_shape=out_shape,
        in_specs=[VMEM] * len(operands),
        out_specs=jax.tree.map(lambda _: VMEM, out_shape),
        scratch_shapes=scratch,
        cost_estimate=pl.CostEstimate(flops=flops, bytes_accessed=0, transcendentals=0),
        compiler_params=pltpu.CompilerParams(vmem_limit_bytes=VMEM_BYTES),
    )(*operands)


def weigh_kernel(slot_ref, hits_ref, pool_ref, owner_ref, *refs):
    libs, (posterior_ref, weight_ref) = refs[:-2], refs[-2:]
    owned, width = libs[0].shape
    target_count = posterior_ref.shape[1]
    lane = lax.broadcasted_iota(jnp.int32, (1, target_count), 1)
    pool, hits = pool_ref[...], hits_ref[...]
    logits = jnp.zeros((1, target_count), jnp.float32)
    counts = jnp.zeros((1, target_count), jnp.float32)
    for at, lib in enumerate(libs):
        products = jnp.sum(lib[...] * pool, axis=1, keepdims=True) / math.sqrt(width)
        first = owner_ref[at : at + 1, :] * owned
        for a in range(owned):
            logits = jnp.where(lane == first + a, products[a : a + 1, :], logits)
    for t in range(target_count):
        named = jnp.sum(jnp.where(hits == t, 1.0, 0.0), axis=1, keepdims=True)
        counts = jnp.where(lane == t, named, counts)
    raised = jnp.exp(logits - jnp.max(logits, axis=1, keepdims=True))
    posterior_ref[...] = raised / jnp.sum(raised, axis=1, keepdims=True)
    shown = jnp.where(counts > 0.0, logits, -jnp.inf)
    parts = counts * jnp.exp(shown - jnp.max(shown, axis=1, keepdims=True))
    weights = parts / jnp.sum(parts, axis=1, keepdims=True)
    weights = jnp.sum(jnp.where(slot_ref[...] == lane, weights, 0.0), axis=1, keepdims=True)
    weight_ref[...] = jnp.broadcast_to(weights, weight_ref.shape)


def partial_kernel(*refs):
    query, blocks, out = refs[0], refs[1:-1], refs[-1]
    out[...] = lax.dot_general(
        query[...],
        jnp.concatenate([block[...] for block in blocks]),
        (((1,), (1,)), ((), ())),
        preferred_element_type=jnp.float32,
    )


def partial_similar(query, blocks):
    rows = sum(block.shape[0] for block in blocks)
    shape = jax.ShapeDtypeStruct((query.shape[0], rows), jnp.float32)
    return call_kernel(partial_kernel, shape, query, *blocks)


def align_block(similar, length, half_sharp):
    column = lax.broadcasted_iota(jnp.int32, (1, similar.shape[1]), 1).astype(jnp.float32)
    inside = column < length
    fraction = 1.0 / length[:, 0:1]
    row_mean = jnp.sum(jnp.where(inside, similar, 0.0), axis=1, keepdims=True) * fraction
    row_diff = similar - row_mean
    row_var = (
        jnp.sum(jnp.where(inside, row_diff * row_diff, 0.0), axis=1, keepdims=True) * fraction
    )
    column_mean = jnp.mean(similar, axis=0, keepdims=True)
    column_diff = similar - column_mean
    column_var = jnp.mean(column_diff * column_diff, axis=0, keepdims=True)
    scores = row_diff * (half_sharp * lax.rsqrt(row_var + 1e-05)) + column_diff * (
        half_sharp * lax.rsqrt(column_var + 1e-05)
    )
    scores = jnp.where(inside, scores, -jnp.inf)
    raised = jnp.exp(scores - jnp.max(scores, axis=1, keepdims=True))
    return raised / jnp.sum(raised, axis=1, keepdims=True)


def align_kernel(model_width, slots, len_ref, sharp_ref, mine, other, out_ref):
    scale = 1.0 / math.sqrt(model_width)
    rows = mine.shape[1] // len(slots)
    for at, slot in enumerate(slots):
        part = pl.ds(at * rows, rows)
        similar = (mine[:, part] + other[:, part]) * scale
        alignment = align_block(similar, len_ref[slot : slot + 1, :rows], sharp_ref[:, 0:1])
        out_ref[:, part] = alignment.astype(out_ref.dtype)


def align(model_width, slots, lengths, half_sharp, mine, other):
    return call_kernel(
        functools.partial(align_kernel, model_width, slots),
        jax.ShapeDtypeStruct(mine.shape, jnp.bfloat16),
        lengths,
        half_sharp,
        mine,
        other,
    )


def weighted_term(weight, alignment, blocks):
    target = blocks[0][...] if len(blocks) == 1 else jnp.concatenate([b[...] for b in blocks])
    return weight * jnp.dot(alignment, target, preferred_element_type=jnp.float32)


def profile_kernel(groups, pieces, weight_ref, *refs):
    aligned, blocks, out_ref = refs[: len(groups)], refs[len(groups) : -1], refs[-1]
    acc, at = None, 0
    for group, slots in zip(aligned, groups):
        rows = group.shape[1] // len(slots)
        for i, slot in enumerate(slots):
            count = pieces.get(slot, 1)
            term = weighted_term(
                weight_ref[slot : slot + 1, 0:1],
                group[:, i * rows : (i + 1) * rows],
                blocks[at : at + count],
            )
            acc = term if acc is None else acc + term
            at += count
    out_ref[...] = acc


def last_kernel(model_width, targets, len_ref, sharp_ref, weight_ref, mine, other, *refs):
    blocks, (acc_ref, out_ref) = refs[:-2], refs[-2:]
    rows = mine.shape[1] // len(targets)
    acc = acc_ref[...]
    for at, (slot, count) in enumerate(targets):
        part = pl.ds(at * rows, rows)
        similar = (mine[:, part] + other[:, part]) * (1.0 / math.sqrt(model_width))
        alignment = align_block(similar, len_ref[slot : slot + 1, :rows], sharp_ref[:, 0:1])
        acc += weighted_term(
            weight_ref[slot : slot + 1, 0:1], alignment.astype(jnp.bfloat16), blocks[:count]
        )
        blocks = blocks[count:]
    out_ref[...] = acc.astype(out_ref.dtype)


def per_device_by_target(
    query_res, target_res, target_len, hits, sharpness, query_pool, target_pool
):
    model_width = query_pool.shape[1]
    target_rows = target_res.shape[1]
    query = query_res[0]
    at_tgt, at_qry, at_rep = (lax.axis_index(name) for name in ("tgt", "qry", "rep"))

    def from_peer(array, k):
        return lax.ppermute(array, "tgt", [(i, i ^ k) for i in range(4)])

    def across(array, axis):
        return lax.ppermute(array, axis, [(0, 1), (1, 0)])

    def after(array, *done):
        return lax.optimization_barrier((array, *done))[0]

    split = [(2 * i + c, 2 * (i ^ (1 + c)) + c) for i in range(4) for c in range(2)]
    pool_split = lax.ppermute(target_pool, ("tgt", "rep"), split)
    pool_last = from_peer(target_pool, 3)
    pool_other = across(pool_split, "rep")
    owners = jnp.stack([at_tgt, at_tgt ^ (1 + at_rep), at_tgt ^ (2 - at_rep), at_tgt ^ 3])

    share = lax.dynamic_index_in_dim(target_res, at_qry, 0, keepdims=False)
    rest = lax.dynamic_index_in_dim(target_res, 1 - at_qry, 0, keepdims=False)
    far = from_peer(share, 2)
    near = from_peer(share, 1)

    bases = [2 * (at_tgt ^ k) for k in range(4)]
    slots = [bases[0], bases[0] + 1]
    for base in bases[1:]:
        slots += [base + at_qry, base + 1 - at_qry]
    slots = jnp.stack(slots).astype(jnp.int32)[:, None]
    named = slots == jnp.arange(len(target_len))[None]
    lengths = jnp.sum(jnp.where(named, target_len[None], 0), axis=1, keepdims=True)
    lengths = jnp.broadcast_to(lengths.astype(jnp.float32), (len(target_len), target_rows))
    half_sharp = jnp.broadcast_to(0.5 * sharpness, (1, target_rows))

    def aligned(slots, mine, other):
        return align(model_width, slots, lengths, half_sharp, mine, other)

    far = after(far, pool_split, pool_last)
    near = after(near, far)
    far = after(far, near)
    half = target_rows // 2
    last = [from_peer(far[:half], 1), from_peer(far[half:], 1)]
    near_rest = from_peer(after(rest, far), 1)

    one_blocks = [target_res[0], target_res[1], near, far]
    one = partial_similar(query, one_blocks)
    one_other = across(one, "rep")
    far_rest = across(after(far, one_other), "qry")

    last_rest = [across(piece, "qry") for piece in last]
    two_blocks = [far_rest, *last]
    two = partial_similar(query, two_blocks)
    two_other = across(two, "rep")
    one_aligned = aligned((0, 1, 2, 4), after(one, two), one_other)

    posterior, weights = call_kernel(
        weigh_kernel,
        (
            jax.ShapeDtypeStruct((1, len(target_len)), jnp.float32),
            jax.ShapeDtypeStruct((len(target_len), target_rows), jnp.float32),
        ),
        slots,
        after(hits, two),
        query_pool,
        owners.astype(jnp.int32)[:, None],
        target_pool,
        pool_split,
        pool_other,
        pool_last,
    )

    three_blocks = [near_rest, *last_rest]
    three = partial_similar(after(query, weights, one_aligned), three_blocks)
    three_other = across(three, "rep")
    two_aligned = aligned((5, 6), after(two, three), two_other)
    acc = call_kernel(
        functools.partial(
            profile_kernel, ((0, 1, 2, 4), (5, 6)), {6: 2}
        ),
        jax.ShapeDtypeStruct(query.shape, jnp.float32),
        weights,
        one_aligned,
        two_aligned,
        *one_blocks,
        *two_blocks,
    )
    profile = call_kernel(
        functools.partial(last_kernel, model_width, ((3, 1), (7, 2))),
        jax.ShapeDtypeStruct(query.shape, jnp.bfloat16),
        lengths,
        half_sharp,
        weights,
        three,
        three_other,
        *three_blocks,
        acc,
    )
    return (profile[None], posterior)


def solution(mesh):
    placed = (
        P(("grp", "tgt", "qry"), None, "rep"),
        P(("grp", "tgt"), None, "rep"),
        P("grp"),
        P(("grp", "tgt", "qry"), None),
        P(("grp", "tgt", "qry")),
        P(("grp", "tgt", "qry"), None),
        P(("grp", "tgt"), None),
    )
    groups = mesh.shape["tgt"]

    def per_device(*arrays):
        query_res, target_res, _, hits = arrays[:4]
        few = (
            query_res.shape[0] == 1
            and groups == 4 <= hits.shape[1] // target_res.shape[0]
            and target_res.shape[0] == mesh.shape["qry"] == 2
            and mesh.shape["rep"] == 2
        )
        return (per_device_by_target if few else per_device_by_hit)(*arrays)

    return jax.shard_map(
        per_device,
        mesh=mesh,
        in_specs=placed,
        out_specs=(P(("grp", "tgt", "qry"), None, "rep"), P(("grp", "tgt", "qry"), None)),
        check_vma=False,
    )
```

```python
import functools
import math

import jax
import jax.numpy as jnp
from jax import lax
from jax.experimental import pallas as pl
from jax.experimental.pallas import tpu as pltpu
from jax.sharding import PartitionSpec as P

VMEM_BYTES = 16 * 1024 * 1024


def softmax_rows(logits):
    highest = jnp.max(logits, axis=-1, keepdims=True)
    raised = jnp.exp(logits - highest)
    return raised / jnp.sum(raised, axis=-1, keepdims=True)


def weigh_alignment(similar, lengths, sharpness, hit_weight):
    target_rows = similar.shape[-1]
    inside = jnp.arange(target_rows)[None, None, None, :] < lengths[:, :, None, None]
    counted = lengths[:, :, None, None].astype(jnp.float32)
    row_mean = jnp.sum(jnp.where(inside, similar, 0.0), axis=-1, keepdims=True) / counted
    row_diff = similar - row_mean
    row_var = jnp.sum(jnp.where(inside, row_diff * row_diff, 0.0), axis=-1, keepdims=True) / counted
    row_score = row_diff / jnp.sqrt(row_var + 1e-05)
    column_mean = jnp.mean(similar, axis=2, keepdims=True)
    column_diff = similar - column_mean
    column_var = jnp.mean(column_diff * column_diff, axis=2, keepdims=True)
    column_score = column_diff / jnp.sqrt(column_var + 1e-05)
    scores = sharpness[:, None, None, None] * (0.5 * (row_score + column_score))
    scores = jnp.where(inside, scores, -jnp.inf)
    alignment = softmax_rows(scores)
    return (hit_weight[:, :, None, None] * alignment).astype(jnp.bfloat16)


def plan_slots(flat_hits, owned_targets, tgt_count, capacity):
    owners = flat_hits // owned_targets
    local_ids = flat_hits % owned_targets
    matched = owners[:, None] == jnp.arange(tgt_count)[None, :]
    earlier = jnp.cumsum(matched.astype(jnp.int32), axis=0) - 1
    rank_in = jnp.sum(jnp.where(matched, earlier, 0), axis=1)
    slot_of = owners * capacity + rank_in
    placed = slot_of[:, None] == jnp.arange(tgt_count * capacity)[None, :]
    wanted = jnp.sum(jnp.where(placed, local_ids[:, None], 0), axis=0).reshape(tgt_count, capacity)
    return (wanted, slot_of)


def fetch_shares(target_res, flat_hits, capacity):
    tgt_count = lax.axis_size("tgt")
    owned_targets, target_rows, width = target_res.shape
    wanted, slot_of = plan_slots(flat_hits, owned_targets, tgt_count, capacity)
    requested = lax.all_to_all(wanted, "tgt", split_axis=0, concat_axis=0, tiled=True)
    outgoing = jnp.take(target_res, requested.reshape(tgt_count * capacity), axis=0)
    outgoing = outgoing.reshape(tgt_count, capacity, target_rows, width)
    arrived = lax.all_to_all(outgoing, "tgt", split_axis=0, concat_axis=0, tiled=True)
    return jnp.take(arrived.reshape(tgt_count * capacity, target_rows, width), slot_of, axis=0)


def per_device_by_hit(query_res, target_res, target_len, hits, sharpness, query_pool, target_pool):
    tgt_count = lax.axis_size("tgt")
    query_count = query_res.shape[0]
    target_rows = target_res.shape[1]
    hit_count = hits.shape[1]
    pair_count = query_count * hit_count
    model_width = query_pool.shape[1]
    capacity = max(2, (2 * pair_count + tgt_count - 1) // tgt_count)
    library = lax.all_gather(target_pool, "tgt", axis=0, tiled=True)
    logits = jnp.dot(query_pool, library.T, precision=lax.Precision.HIGHEST) / math.sqrt(
        model_width
    )
    posterior = softmax_rows(logits)
    matches = hits[:, :, None] == jnp.arange(library.shape[0])[None, None, :]
    hit_weight = softmax_rows(jnp.sum(jnp.where(matches, logits[:, None, :], 0.0), axis=-1))
    lengths = jnp.sum(jnp.where(matches, target_len[None, None, :], 0), axis=-1)
    half_width = query_res.shape[2]
    chosen = fetch_shares(target_res, hits.reshape(pair_count), capacity)
    chosen = chosen.reshape(query_count, hit_count, target_rows, half_width)
    partial_sim = jnp.einsum(
        "qid,qhjd->qhij", query_res, chosen, preferred_element_type=jnp.float32
    ) / math.sqrt(model_width)
    similar = lax.psum(partial_sim, "rep")
    weighted = weigh_alignment(similar, lengths, sharpness, hit_weight)
    profile = jnp.einsum("qhij,qhjd->qid", weighted, chosen, preferred_element_type=jnp.float32)
    return (profile.astype(jnp.bfloat16), posterior)


VMEM = pl.BlockSpec(memory_space=pltpu.VMEM)


def call_kernel(kernel, out_shape, *operands, scratch=(), flops=0):
    return pl.pallas_call(
        kernel,
        out_shape=out_shape,
        in_specs=[VMEM] * len(operands),
        out_specs=jax.tree.map(lambda _: VMEM, out_shape),
        scratch_shapes=scratch,
        cost_estimate=pl.CostEstimate(flops=flops, bytes_accessed=0, transcendentals=0),
        compiler_params=pltpu.CompilerParams(vmem_limit_bytes=VMEM_BYTES),
    )(*operands)


def weigh_kernel(slot_ref, hits_ref, pool_ref, owner_ref, *refs):
    libs, (posterior_ref, weight_ref) = refs[:-2], refs[-2:]
    owned, width = libs[0].shape
    target_count = posterior_ref.shape[1]
    target = lax.broadcasted_iota(jnp.int32, (target_count, 1), 0)
    counts = jnp.sum(jnp.where(hits_ref[...] == target, 1.0, 0.0), axis=1, keepdims=True)
    logits = jnp.zeros((target_count, 1), jnp.float32)
    for at, lib in enumerate(libs):
        products = jnp.sum(lib[...] * pool_ref[...], axis=1, keepdims=True) / math.sqrt(width)
        first = owner_ref[at : at + 1, 0:1] * owned
        for a in range(owned):
            logits = jnp.where(target == first + a, products[a : a + 1, :], logits)
    raised = jnp.exp(logits - jnp.max(logits, axis=0, keepdims=True))
    posterior = raised / jnp.sum(raised, axis=0, keepdims=True)
    shown = jnp.where(counts > 0.0, logits, -jnp.inf)
    parts = counts * jnp.exp(shown - jnp.max(shown, axis=0, keepdims=True))
    weights = parts / jnp.sum(parts, axis=0, keepdims=True)
    lane = lax.broadcasted_iota(jnp.int32, (1, target_count), 1)
    posterior_ref[...] = jnp.sum(jnp.where(target == lane, posterior, 0.0), axis=0, keepdims=True)
    weights = jnp.sum(jnp.where(target == lane, weights, 0.0), axis=0, keepdims=True)
    weights = jnp.where(slot_ref[:, 0:1] == lane, weights, 0.0)
    weights = jnp.sum(weights, axis=1, keepdims=True)
    weight_ref[...] = jnp.broadcast_to(weights, weight_ref.shape)


def partial_kernel(*refs):
    query, blocks, out = refs[0], refs[1:-1], refs[-1]
    out[...] = lax.dot_general(
        query[...],
        jnp.concatenate([block[...] for block in blocks]),
        (((1,), (1,)), ((), ())),
        preferred_element_type=jnp.float32,
    )


def partial_similar(query, blocks):
    rows = sum(block.shape[0] for block in blocks)
    shape = jax.ShapeDtypeStruct((query.shape[0], rows), jnp.float32)
    return call_kernel(partial_kernel, shape, query, *blocks)


def align_block(similar, length, half_sharp):
    column = lax.broadcasted_iota(jnp.int32, (1, similar.shape[1]), 1).astype(jnp.float32)
    inside = column < length
    fraction = 1.0 / length[:, 0:1]
    row_mean = jnp.sum(jnp.where(inside, similar, 0.0), axis=1, keepdims=True) * fraction
    row_diff = similar - row_mean
    row_var = (
        jnp.sum(jnp.where(inside, row_diff * row_diff, 0.0), axis=1, keepdims=True) * fraction
    )
    column_mean = jnp.mean(similar, axis=0, keepdims=True)
    column_diff = similar - column_mean
    column_var = jnp.mean(column_diff * column_diff, axis=0, keepdims=True)
    scores = row_diff * (half_sharp * lax.rsqrt(row_var + 1e-05)) + column_diff * (
        half_sharp * lax.rsqrt(column_var + 1e-05)
    )
    scores = jnp.where(inside, scores, -jnp.inf)
    raised = jnp.exp(scores - jnp.max(scores, axis=1, keepdims=True))
    return raised / jnp.sum(raised, axis=1, keepdims=True)


def align_kernel(model_width, slots, len_ref, sharp_ref, mine, other, out_ref):
    scale = 1.0 / math.sqrt(model_width)
    rows = mine.shape[1] // len(slots)
    for at, slot in enumerate(slots):
        part = pl.ds(at * rows, rows)
        similar = (mine[:, part] + other[:, part]) * scale
        alignment = align_block(similar, len_ref[slot : slot + 1, :rows], sharp_ref[:, 0:1])
        out_ref[:, part] = alignment.astype(out_ref.dtype)


def align(model_width, slots, lengths, half_sharp, mine, other):
    return call_kernel(
        functools.partial(align_kernel, model_width, slots),
        jax.ShapeDtypeStruct(mine.shape, jnp.bfloat16),
        lengths,
        half_sharp,
        mine,
        other,
    )


def weighted_term(weight, alignment, blocks):
    target = blocks[0][...] if len(blocks) == 1 else jnp.concatenate([b[...] for b in blocks])
    return weight * jnp.dot(alignment, target, preferred_element_type=jnp.float32)


def profile_kernel(model_width, groups, targets, *refs):
    weight_ref, aligned, refs = refs[0], refs[1 : 1 + len(groups)], refs[1 + len(groups) :]
    blocks, out_ref = refs[:-1], refs[-1]
    acc = None

    def add(acc, target, alignment, blocks):
        slot, count = target
        term = weighted_term(weight_ref[slot : slot + 1, 0:1], alignment, blocks[:count])
        return (term if acc is None else acc + term), blocks[count:]

    for group, members in zip(aligned, groups):
        rows = group.shape[1] // len(members)
        for at, target in enumerate(members):
            acc, blocks = add(acc, target, group[:, at * rows : (at + 1) * rows], blocks)
    if targets:
        len_ref, sharp_ref, mine, other, *blocks = blocks
        rows = mine.shape[1] // len(targets)
        for at, target in enumerate(targets):
            part = pl.ds(at * rows, rows)
            similar = (mine[:, part] + other[:, part]) * (1.0 / math.sqrt(model_width))
            lengths = len_ref[target[0] : target[0] + 1, :rows]
            alignment = align_block(similar, lengths, sharp_ref[:, 0:1])
            acc, blocks = add(acc, target, alignment.astype(jnp.bfloat16), blocks)
    if len(blocks):
        acc += blocks[0][...]
    out_ref[...] = acc.astype(out_ref.dtype)


def per_device_by_target(
    query_res, target_res, target_len, hits, sharpness, query_pool, target_pool
):
    model_width = query_pool.shape[1]
    target_rows = target_res.shape[1]
    query = query_res[0]
    at_tgt, at_qry, at_rep = (lax.axis_index(name) for name in ("tgt", "qry", "rep"))

    def from_peer(array, k):
        return lax.ppermute(array, "tgt", [(i, i ^ k) for i in range(4)])

    def across(array, axis):
        return lax.ppermute(array, axis, [(0, 1), (1, 0)])

    def after(array, *done):
        return lax.optimization_barrier((array, *done))[0]

    split = [(2 * i + c, 2 * (i ^ (1 + c)) + c) for i in range(4) for c in range(2)]
    pool_split = lax.ppermute(target_pool, ("tgt", "rep"), split)
    pool_last = from_peer(target_pool, 3)

    share = lax.dynamic_index_in_dim(target_res, at_qry, 0, keepdims=False)
    rest = lax.dynamic_index_in_dim(target_res, 1 - at_qry, 0, keepdims=False)
    far = from_peer(share, 2)
    near = from_peer(share, 1)

    cross = [(2 * i + x, 2 * (i ^ 1) + 1 - x) for i in range(4) for x in range(2)]

    bases = [2 * (at_tgt ^ k) for k in range(4)]
    slots = [bases[0], bases[0] + 1]
    for base in bases[1:]:
        slots += [base + at_qry, base + 1 - at_qry]
    owners = [at_tgt, at_tgt ^ (1 + at_rep), at_tgt ^ (2 - at_rep), at_tgt ^ 3]
    table = (len(target_len), target_rows)
    slots = jnp.broadcast_to(jnp.stack(slots)[:, None], table)
    owners = jnp.broadcast_to(jnp.stack(owners + owners)[:, None], table)
    named = slots[:, : table[0]] == jnp.arange(table[0])[None]
    lengths = jnp.sum(jnp.where(named, target_len[None], 0), axis=1, keepdims=True)
    lengths = jnp.broadcast_to(lengths.astype(jnp.float32), table)
    half_sharp = jnp.broadcast_to(0.5 * sharpness, (1, target_rows))

    def aligned(slots, mine, other):
        return align(model_width, slots, lengths, half_sharp, mine, other)

    def add_up(groups, targets, dtype, *operands):
        return call_kernel(
            functools.partial(profile_kernel, model_width, groups, targets),
            jax.ShapeDtypeStruct(query.shape, dtype),
            weights,
            *operands,
        )

    own_blocks = [target_res[0], target_res[1]]
    own = partial_similar(after(query, share), own_blocks)
    own_other = across(own, "rep")
    own_aligned = aligned((0, 1), own, own_other)

    far = after(far, pool_split, pool_last, own_aligned, slots, owners)
    near = after(near, far)
    far = after(far, near)
    last_rest = lax.ppermute(far, ("tgt", "qry"), cross)
    last = from_peer(far, 1)
    far_rest = across(far, "qry")
    near_rest = from_peer(after(rest, far), 1)

    one_blocks = [near, far]
    one = partial_similar(query, one_blocks)
    one_other = across(one, "rep")
    one_aligned = aligned((2, 4), one, one_other)
    pool_other = across(pool_split, "rep")
    posterior, weights = call_kernel(
        weigh_kernel,
        (
            jax.ShapeDtypeStruct((1, table[0]), jnp.float32),
            jax.ShapeDtypeStruct(table, jnp.float32),
        ),
        slots,
        after(hits, one_aligned),
        query_pool,
        owners,
        target_pool,
        pool_split,
        pool_other,
        pool_last,
    )
    acc = add_up(
        (((0, 1), (1, 1)), ((2, 1), (4, 1))),
        (),
        jnp.float32,
        own_aligned,
        one_aligned,
        *own_blocks,
        *one_blocks,
    )

    two_blocks = [far_rest, near_rest]
    two = partial_similar(after(query, acc), two_blocks)
    two_other = across(two, "rep")
    three_blocks = [last, last_rest]
    three = partial_similar(after(query, two), three_blocks)
    three_other = across(three, "rep")
    acc = add_up(
        (),
        ((5, 1), (3, 1)),
        jnp.float32,
        lengths,
        half_sharp,
        after(two, three),
        two_other,
        *two_blocks,
        acc,
    )
    profile = add_up(
        (),
        ((6, 1), (7, 1)),
        jnp.bfloat16,
        lengths,
        half_sharp,
        three,
        three_other,
        *three_blocks,
        acc,
    )
    return (profile[None], posterior)


def solution(mesh):
    placed = (
        P(("grp", "tgt", "qry"), None, "rep"),
        P(("grp", "tgt"), None, "rep"),
        P("grp"),
        P(("grp", "tgt", "qry"), None),
        P(("grp", "tgt", "qry")),
        P(("grp", "tgt", "qry"), None),
        P(("grp", "tgt"), None),
    )
    groups = mesh.shape["tgt"]

    def per_device(*arrays):
        query_res, target_res, _, hits = arrays[:4]
        few = (
            query_res.shape[0] == 1
            and groups == 4 <= hits.shape[1] // target_res.shape[0]
            and target_res.shape[0] == mesh.shape["qry"] == 2
            and mesh.shape["rep"] == 2
        )
        return (per_device_by_target if few else per_device_by_hit)(*arrays)

    return jax.shard_map(
        per_device,
        mesh=mesh,
        in_specs=placed,
        out_specs=(P(("grp", "tgt", "qry"), None, "rep"), P(("grp", "tgt", "qry"), None)),
        check_vma=False,
    )
```

```python
import functools
import math

import jax
import jax.numpy as jnp
from jax import lax
from jax.experimental import pallas as pl
from jax.experimental.pallas import tpu as pltpu
from jax.sharding import PartitionSpec as P

VMEM_BYTES = 16 * 1024 * 1024


def softmax_rows(logits):
    highest = jnp.max(logits, axis=-1, keepdims=True)
    raised = jnp.exp(logits - highest)
    return raised / jnp.sum(raised, axis=-1, keepdims=True)


def weigh_alignment(similar, lengths, sharpness, hit_weight):
    target_rows = similar.shape[-1]
    inside = jnp.arange(target_rows)[None, None, None, :] < lengths[:, :, None, None]
    counted = lengths[:, :, None, None].astype(jnp.float32)
    row_mean = jnp.sum(jnp.where(inside, similar, 0.0), axis=-1, keepdims=True) / counted
    row_diff = similar - row_mean
    row_var = jnp.sum(jnp.where(inside, row_diff * row_diff, 0.0), axis=-1, keepdims=True) / counted
    row_score = row_diff / jnp.sqrt(row_var + 1e-05)
    column_mean = jnp.mean(similar, axis=2, keepdims=True)
    column_diff = similar - column_mean
    column_var = jnp.mean(column_diff * column_diff, axis=2, keepdims=True)
    column_score = column_diff / jnp.sqrt(column_var + 1e-05)
    scores = sharpness[:, None, None, None] * (0.5 * (row_score + column_score))
    scores = jnp.where(inside, scores, -jnp.inf)
    alignment = softmax_rows(scores)
    return (hit_weight[:, :, None, None] * alignment).astype(jnp.bfloat16)


def plan_slots(flat_hits, owned_targets, tgt_count, capacity):
    owners = flat_hits // owned_targets
    local_ids = flat_hits % owned_targets
    matched = owners[:, None] == jnp.arange(tgt_count)[None, :]
    earlier = jnp.cumsum(matched.astype(jnp.int32), axis=0) - 1
    rank_in = jnp.sum(jnp.where(matched, earlier, 0), axis=1)
    slot_of = owners * capacity + rank_in
    placed = slot_of[:, None] == jnp.arange(tgt_count * capacity)[None, :]
    wanted = jnp.sum(jnp.where(placed, local_ids[:, None], 0), axis=0).reshape(tgt_count, capacity)
    return (wanted, slot_of)


def fetch_shares(target_res, flat_hits, capacity):
    tgt_count = lax.axis_size("tgt")
    owned_targets, target_rows, width = target_res.shape
    wanted, slot_of = plan_slots(flat_hits, owned_targets, tgt_count, capacity)
    requested = lax.all_to_all(wanted, "tgt", split_axis=0, concat_axis=0, tiled=True)
    outgoing = jnp.take(target_res, requested.reshape(tgt_count * capacity), axis=0)
    outgoing = outgoing.reshape(tgt_count, capacity, target_rows, width)
    arrived = lax.all_to_all(outgoing, "tgt", split_axis=0, concat_axis=0, tiled=True)
    return jnp.take(arrived.reshape(tgt_count * capacity, target_rows, width), slot_of, axis=0)


def per_device_by_hit(query_res, target_res, target_len, hits, sharpness, query_pool, target_pool):
    tgt_count = lax.axis_size("tgt")
    query_count = query_res.shape[0]
    target_rows = target_res.shape[1]
    hit_count = hits.shape[1]
    pair_count = query_count * hit_count
    model_width = query_pool.shape[1]
    capacity = max(2, (2 * pair_count + tgt_count - 1) // tgt_count)
    library = lax.all_gather(target_pool, "tgt", axis=0, tiled=True)
    logits = jnp.dot(query_pool, library.T, precision=lax.Precision.HIGHEST) / math.sqrt(
        model_width
    )
    posterior = softmax_rows(logits)
    matches = hits[:, :, None] == jnp.arange(library.shape[0])[None, None, :]
    hit_weight = softmax_rows(jnp.sum(jnp.where(matches, logits[:, None, :], 0.0), axis=-1))
    lengths = jnp.sum(jnp.where(matches, target_len[None, None, :], 0), axis=-1)
    half_width = query_res.shape[2]
    chosen = fetch_shares(target_res, hits.reshape(pair_count), capacity)
    chosen = chosen.reshape(query_count, hit_count, target_rows, half_width)
    partial_sim = jnp.einsum(
        "qid,qhjd->qhij", query_res, chosen, preferred_element_type=jnp.float32
    ) / math.sqrt(model_width)
    similar = lax.psum(partial_sim, "rep")
    weighted = weigh_alignment(similar, lengths, sharpness, hit_weight)
    profile = jnp.einsum("qhij,qhjd->qid", weighted, chosen, preferred_element_type=jnp.float32)
    return (profile.astype(jnp.bfloat16), posterior)


VMEM = pl.BlockSpec(memory_space=pltpu.VMEM)


def call_kernel(kernel, out_shape, *operands, scratch=(), flops=0):
    return pl.pallas_call(
        kernel,
        out_shape=out_shape,
        in_specs=[VMEM] * len(operands),
        out_specs=jax.tree.map(lambda _: VMEM, out_shape),
        scratch_shapes=scratch,
        cost_estimate=pl.CostEstimate(flops=flops, bytes_accessed=0, transcendentals=0),
        compiler_params=pltpu.CompilerParams(vmem_limit_bytes=VMEM_BYTES),
    )(*operands)


def weigh_kernel(slot_ref, hits_ref, pool_ref, owner_ref, *refs):
    libs, (posterior_ref, weight_ref) = refs[:-2], refs[-2:]
    owned, width = libs[0].shape
    target_count = posterior_ref.shape[1]
    target = lax.broadcasted_iota(jnp.int32, (target_count, 1), 0)
    counts = jnp.sum(jnp.where(hits_ref[...] == target, 1.0, 0.0), axis=1, keepdims=True)
    logits = jnp.zeros((target_count, 1), jnp.float32)
    for at, lib in enumerate(libs):
        products = jnp.sum(lib[...] * pool_ref[...], axis=1, keepdims=True) / math.sqrt(width)
        first = owner_ref[at : at + 1, 0:1] * owned
        for a in range(owned):
            logits = jnp.where(target == first + a, products[a : a + 1, :], logits)
    raised = jnp.exp(logits - jnp.max(logits, axis=0, keepdims=True))
    posterior = raised / jnp.sum(raised, axis=0, keepdims=True)
    shown = jnp.where(counts > 0.0, logits, -jnp.inf)
    parts = counts * jnp.exp(shown - jnp.max(shown, axis=0, keepdims=True))
    weights = parts / jnp.sum(parts, axis=0, keepdims=True)
    lane = lax.broadcasted_iota(jnp.int32, (1, target_count), 1)
    posterior_ref[...] = jnp.sum(jnp.where(target == lane, posterior, 0.0), axis=0, keepdims=True)
    weights = jnp.sum(jnp.where(target == lane, weights, 0.0), axis=0, keepdims=True)
    weights = jnp.where(slot_ref[:, 0:1] == lane, weights, 0.0)
    weights = jnp.sum(weights, axis=1, keepdims=True)
    weight_ref[...] = jnp.broadcast_to(weights, weight_ref.shape)


def partial_kernel(*refs):
    query, blocks, out = refs[0], refs[1:-1], refs[-1]
    out[...] = lax.dot_general(
        query[...],
        jnp.concatenate([block[...] for block in blocks]),
        (((1,), (1,)), ((), ())),
        preferred_element_type=jnp.float32,
    )


def partial_similar(query, blocks):
    rows = sum(block.shape[0] for block in blocks)
    shape = jax.ShapeDtypeStruct((query.shape[0], rows), jnp.float32)
    return call_kernel(partial_kernel, shape, query, *blocks)


def align_block(similar, length, half_sharp):
    column = lax.broadcasted_iota(jnp.int32, (1, similar.shape[1]), 1).astype(jnp.float32)
    inside = column < length
    fraction = 1.0 / length[:, 0:1]
    row_mean = jnp.sum(jnp.where(inside, similar, 0.0), axis=1, keepdims=True) * fraction
    row_diff = similar - row_mean
    row_var = (
        jnp.sum(jnp.where(inside, row_diff * row_diff, 0.0), axis=1, keepdims=True) * fraction
    )
    column_mean = jnp.mean(similar, axis=0, keepdims=True)
    column_diff = similar - column_mean
    column_var = jnp.mean(column_diff * column_diff, axis=0, keepdims=True)
    scores = row_diff * (half_sharp * lax.rsqrt(row_var + 1e-05)) + column_diff * (
        half_sharp * lax.rsqrt(column_var + 1e-05)
    )
    scores = jnp.where(inside, scores, -jnp.inf)
    raised = jnp.exp(scores - jnp.max(scores, axis=1, keepdims=True))
    return raised / jnp.sum(raised, axis=1, keepdims=True)


def align_kernel(model_width, slots, len_ref, sharp_ref, mine, other, out_ref):
    scale = 1.0 / math.sqrt(model_width)
    rows = mine.shape[1] // len(slots)
    for at, slot in enumerate(slots):
        part = pl.ds(at * rows, rows)
        similar = (mine[:, part] + other[:, part]) * scale
        alignment = align_block(similar, len_ref[slot : slot + 1, :rows], sharp_ref[:, 0:1])
        out_ref[:, part] = alignment.astype(out_ref.dtype)


def align(model_width, slots, lengths, half_sharp, mine, other):
    return call_kernel(
        functools.partial(align_kernel, model_width, slots),
        jax.ShapeDtypeStruct(mine.shape, jnp.bfloat16),
        lengths,
        half_sharp,
        mine,
        other,
    )


def weighted_term(weight, alignment, blocks):
    target = blocks[0][...] if len(blocks) == 1 else jnp.concatenate([b[...] for b in blocks])
    return weight * jnp.dot(alignment, target, preferred_element_type=jnp.float32)


def profile_kernel(model_width, groups, targets, *refs):
    weight_ref, aligned, refs = refs[0], refs[1 : 1 + len(groups)], refs[1 + len(groups) :]
    blocks, out_ref = refs[:-1], refs[-1]
    acc = None

    def add(acc, target, alignment, blocks):
        slot, count = target
        term = weighted_term(weight_ref[slot : slot + 1, 0:1], alignment, blocks[:count])
        return (term if acc is None else acc + term), blocks[count:]

    for group, members in zip(aligned, groups):
        rows = group.shape[1] // len(members)
        for at, target in enumerate(members):
            acc, blocks = add(acc, target, group[:, at * rows : (at + 1) * rows], blocks)
    if targets:
        len_ref, sharp_ref, mine, other, *blocks = blocks
        rows = mine.shape[1] // len(targets)
        for at, target in enumerate(targets):
            part = pl.ds(at * rows, rows)
            similar = (mine[:, part] + other[:, part]) * (1.0 / math.sqrt(model_width))
            lengths = len_ref[target[0] : target[0] + 1, :rows]
            alignment = align_block(similar, lengths, sharp_ref[:, 0:1])
            acc, blocks = add(acc, target, alignment.astype(jnp.bfloat16), blocks)
    if len(blocks):
        acc += blocks[0][...]
    out_ref[...] = acc.astype(out_ref.dtype)


def per_device_by_target(
    query_res, target_res, target_len, hits, sharpness, query_pool, target_pool
):
    model_width = query_pool.shape[1]
    target_rows = target_res.shape[1]
    query = query_res[0]
    at_tgt, at_qry, at_rep = (lax.axis_index(name) for name in ("tgt", "qry", "rep"))

    def from_peer(array, k):
        return lax.ppermute(array, "tgt", [(i, i ^ k) for i in range(4)])

    def across(array, axis):
        return lax.ppermute(array, axis, [(0, 1), (1, 0)])

    def after(array, *done):
        return lax.optimization_barrier((array, *done))[0]

    split = [(2 * i + c, 2 * (i ^ (1 + c)) + c) for i in range(4) for c in range(2)]
    pool_split = lax.ppermute(target_pool, ("tgt", "rep"), split)
    pool_last = from_peer(target_pool, 3)
    pool_split = after(pool_split, pool_last)

    share = lax.dynamic_index_in_dim(target_res, at_qry, 0, keepdims=False)
    rest = lax.dynamic_index_in_dim(target_res, 1 - at_qry, 0, keepdims=False)
    far = from_peer(share, 2)
    near = from_peer(share, 1)

    bases = [2 * (at_tgt ^ k) for k in range(4)]
    slots = [bases[0], bases[0] + 1]
    for base in bases[1:]:
        slots += [base + at_qry, base + 1 - at_qry]
    owners = [at_tgt, at_tgt ^ (1 + at_rep), at_tgt ^ (2 - at_rep), at_tgt ^ 3]
    table = (len(target_len), target_rows)
    slots = jnp.broadcast_to(jnp.stack(slots)[:, None], table)
    owners = jnp.broadcast_to(jnp.stack(owners + owners)[:, None], table)
    named = slots[:, : table[0]] == jnp.arange(table[0])[None]
    lengths = jnp.sum(jnp.where(named, target_len[None], 0), axis=1, keepdims=True)
    lengths = jnp.broadcast_to(lengths.astype(jnp.float32), table)
    half_sharp = jnp.broadcast_to(0.5 * sharpness, (1, target_rows))

    def aligned(slots, mine, other):
        return align(model_width, slots, lengths, half_sharp, mine, other)

    def add_up(groups, targets, dtype, *operands):
        return call_kernel(
            functools.partial(profile_kernel, model_width, groups, targets),
            jax.ShapeDtypeStruct(query.shape, dtype),
            weights,
            *operands,
        )

    far = after(far, pool_split, pool_last, slots, owners, lengths, half_sharp)
    near = after(near, far)
    far = after(far, near)
    half = target_rows // 2
    last = [from_peer(far[:half], 1), from_peer(far[half:], 1)]
    pool_other = across(pool_split, "rep")
    near_rest = from_peer(after(rest, far), 1)

    one_blocks = [target_res[0], target_res[1], near, far]
    one = partial_similar(query, one_blocks)
    one_other = across(one, "rep")
    far_rest = across(after(far, one_other), "qry")
    last_rest = [across(piece, "qry") for piece in last]
    posterior, weights = call_kernel(
        weigh_kernel,
        (
            jax.ShapeDtypeStruct((1, table[0]), jnp.float32),
            jax.ShapeDtypeStruct(table, jnp.float32),
        ),
        slots,
        after(hits, last[1]),
        query_pool,
        owners,
        target_pool,
        pool_split,
        pool_other,
        pool_last,
        flops=1_000_000_000,
    )
    far_rest = after(far_rest, weights)
    two_blocks = [far_rest, *last]
    two = partial_similar(query, two_blocks)
    two_other = across(two, "rep")
    one_aligned = aligned((0, 1, 2, 4), after(one, two), one_other)

    acc = add_up(
        (((0, 1), (1, 1), (2, 1), (4, 1)),),
        (),
        jnp.float32,
        one_aligned,
        *one_blocks,
    )

    three_blocks = [near_rest, *last_rest]
    three = partial_similar(after(query, acc), three_blocks)
    three_other = across(three, "rep")
    acc = add_up(
        (),
        ((5, 1), (6, 2)),
        jnp.float32,
        lengths,
        half_sharp,
        after(two, three),
        two_other,
        *two_blocks,
        acc,
    )
    profile = add_up(
        (),
        ((3, 1), (7, 2)),
        jnp.bfloat16,
        lengths,
        half_sharp,
        three,
        three_other,
        *three_blocks,
        acc,
    )
    return (profile[None], posterior)


def solution(mesh):
    placed = (
        P(("grp", "tgt", "qry"), None, "rep"),
        P(("grp", "tgt"), None, "rep"),
        P("grp"),
        P(("grp", "tgt", "qry"), None),
        P(("grp", "tgt", "qry")),
        P(("grp", "tgt", "qry"), None),
        P(("grp", "tgt"), None),
    )
    groups = mesh.shape["tgt"]

    def per_device(*arrays):
        query_res, target_res, _, hits = arrays[:4]
        few = (
            query_res.shape[0] == 1
            and groups == 4 <= hits.shape[1] // target_res.shape[0]
            and target_res.shape[0] == mesh.shape["qry"] == 2
            and mesh.shape["rep"] == 2
        )
        return (per_device_by_target if few else per_device_by_hit)(*arrays)

    return jax.shard_map(
        per_device,
        mesh=mesh,
        in_specs=placed,
        out_specs=(P(("grp", "tgt", "qry"), None, "rep"), P(("grp", "tgt", "qry"), None)),
        check_vma=False,
    )
```

```python
import functools
import math

import jax
import jax.numpy as jnp
from jax import lax
from jax.experimental import pallas as pl
from jax.experimental.pallas import tpu as pltpu
from jax.sharding import PartitionSpec as P

VMEM_BYTES = 16 * 1024 * 1024


def softmax_rows(logits):
    highest = jnp.max(logits, axis=-1, keepdims=True)
    raised = jnp.exp(logits - highest)
    return raised / jnp.sum(raised, axis=-1, keepdims=True)


def weigh_alignment(similar, lengths, sharpness, hit_weight):
    target_rows = similar.shape[-1]
    inside = jnp.arange(target_rows)[None, None, None, :] < lengths[:, :, None, None]
    counted = lengths[:, :, None, None].astype(jnp.float32)
    row_mean = jnp.sum(jnp.where(inside, similar, 0.0), axis=-1, keepdims=True) / counted
    row_diff = similar - row_mean
    row_var = jnp.sum(jnp.where(inside, row_diff * row_diff, 0.0), axis=-1, keepdims=True) / counted
    row_score = row_diff / jnp.sqrt(row_var + 1e-05)
    column_mean = jnp.mean(similar, axis=2, keepdims=True)
    column_diff = similar - column_mean
    column_var = jnp.mean(column_diff * column_diff, axis=2, keepdims=True)
    column_score = column_diff / jnp.sqrt(column_var + 1e-05)
    scores = sharpness[:, None, None, None] * (0.5 * (row_score + column_score))
    scores = jnp.where(inside, scores, -jnp.inf)
    alignment = softmax_rows(scores)
    return (hit_weight[:, :, None, None] * alignment).astype(jnp.bfloat16)


def plan_slots(flat_hits, owned_targets, tgt_count, capacity):
    owners = flat_hits // owned_targets
    local_ids = flat_hits % owned_targets
    matched = owners[:, None] == jnp.arange(tgt_count)[None, :]
    earlier = jnp.cumsum(matched.astype(jnp.int32), axis=0) - 1
    rank_in = jnp.sum(jnp.where(matched, earlier, 0), axis=1)
    slot_of = owners * capacity + rank_in
    placed = slot_of[:, None] == jnp.arange(tgt_count * capacity)[None, :]
    wanted = jnp.sum(jnp.where(placed, local_ids[:, None], 0), axis=0).reshape(tgt_count, capacity)
    return (wanted, slot_of)


def fetch_shares(target_res, flat_hits, capacity):
    tgt_count = lax.axis_size("tgt")
    owned_targets, target_rows, width = target_res.shape
    wanted, slot_of = plan_slots(flat_hits, owned_targets, tgt_count, capacity)
    requested = lax.all_to_all(wanted, "tgt", split_axis=0, concat_axis=0, tiled=True)
    outgoing = jnp.take(target_res, requested.reshape(tgt_count * capacity), axis=0)
    outgoing = outgoing.reshape(tgt_count, capacity, target_rows, width)
    arrived = lax.all_to_all(outgoing, "tgt", split_axis=0, concat_axis=0, tiled=True)
    return jnp.take(arrived.reshape(tgt_count * capacity, target_rows, width), slot_of, axis=0)


def per_device_by_hit(query_res, target_res, target_len, hits, sharpness, query_pool, target_pool):
    tgt_count = lax.axis_size("tgt")
    query_count = query_res.shape[0]
    target_rows = target_res.shape[1]
    hit_count = hits.shape[1]
    pair_count = query_count * hit_count
    model_width = query_pool.shape[1]
    capacity = max(2, (2 * pair_count + tgt_count - 1) // tgt_count)
    library = lax.all_gather(target_pool, "tgt", axis=0, tiled=True)
    logits = jnp.dot(query_pool, library.T, precision=lax.Precision.HIGHEST) / math.sqrt(
        model_width
    )
    posterior = softmax_rows(logits)
    matches = hits[:, :, None] == jnp.arange(library.shape[0])[None, None, :]
    hit_weight = softmax_rows(jnp.sum(jnp.where(matches, logits[:, None, :], 0.0), axis=-1))
    lengths = jnp.sum(jnp.where(matches, target_len[None, None, :], 0), axis=-1)
    half_width = query_res.shape[2]
    chosen = fetch_shares(target_res, hits.reshape(pair_count), capacity)
    chosen = chosen.reshape(query_count, hit_count, target_rows, half_width)
    partial_sim = jnp.einsum(
        "qid,qhjd->qhij", query_res, chosen, preferred_element_type=jnp.float32
    ) / math.sqrt(model_width)
    similar = lax.psum(partial_sim, "rep")
    weighted = weigh_alignment(similar, lengths, sharpness, hit_weight)
    profile = jnp.einsum("qhij,qhjd->qid", weighted, chosen, preferred_element_type=jnp.float32)
    return (profile.astype(jnp.bfloat16), posterior)


VMEM = pl.BlockSpec(memory_space=pltpu.VMEM)


def call_kernel(kernel, out_shape, *operands, scratch=(), flops=0):
    return pl.pallas_call(
        kernel,
        out_shape=out_shape,
        in_specs=[VMEM] * len(operands),
        out_specs=jax.tree.map(lambda _: VMEM, out_shape),
        scratch_shapes=scratch,
        cost_estimate=pl.CostEstimate(flops=flops, bytes_accessed=0, transcendentals=0),
        compiler_params=pltpu.CompilerParams(vmem_limit_bytes=VMEM_BYTES),
    )(*operands)


def weigh_kernel(slot_ref, hits_ref, pool_ref, owner_ref, *refs):
    libs, (posterior_ref, weight_ref) = refs[:-2], refs[-2:]
    owned, width = libs[0].shape
    target_count = posterior_ref.shape[0]
    target = lax.broadcasted_iota(jnp.int32, (target_count, 1), 0)
    counts = jnp.sum(jnp.where(hits_ref[...] == target, 1.0, 0.0), axis=1, keepdims=True)
    logits = jnp.zeros((target_count, 1), jnp.float32)
    for at, lib in enumerate(libs):
        products = jnp.sum(lib[...] * pool_ref[...], axis=1, keepdims=True) / math.sqrt(width)
        first = owner_ref[at : at + 1, 0:1] * owned
        for a in range(owned):
            logits = jnp.where(target == first + a, products[a : a + 1, :], logits)
    raised = jnp.exp(logits - jnp.max(logits, axis=0, keepdims=True))
    posterior = raised / jnp.sum(raised, axis=0, keepdims=True)
    shown = jnp.where(counts > 0.0, logits, -jnp.inf)
    parts = counts * jnp.exp(shown - jnp.max(shown, axis=0, keepdims=True))
    weights = parts / jnp.sum(parts, axis=0, keepdims=True)
    lane = lax.broadcasted_iota(jnp.int32, (1, target_count), 1)
    posterior_ref[...] = jnp.broadcast_to(posterior, posterior_ref.shape)
    weights = jnp.sum(jnp.where(target == lane, weights, 0.0), axis=0, keepdims=True)
    weights = jnp.where(slot_ref[:, 0:1] == lane, weights, 0.0)
    weights = jnp.sum(weights, axis=1, keepdims=True)
    weight_ref[...] = jnp.broadcast_to(weights, weight_ref.shape)


def partial_kernel(*refs):
    query, blocks, out = refs[0], refs[1:-1], refs[-1]
    out[...] = lax.dot_general(
        query[...],
        jnp.concatenate([block[...] for block in blocks]),
        (((1,), (1,)), ((), ())),
        preferred_element_type=jnp.float32,
    )


def partial_similar(query, blocks):
    rows = sum(block.shape[0] for block in blocks)
    shape = jax.ShapeDtypeStruct((query.shape[0], rows), jnp.float32)
    return call_kernel(partial_kernel, shape, query, *blocks)


def align_block(similar, length, half_sharp):
    column = lax.broadcasted_iota(jnp.int32, (1, similar.shape[1]), 1).astype(jnp.float32)
    inside = column < length
    fraction = 1.0 / length[:, 0:1]
    row_mean = jnp.sum(jnp.where(inside, similar, 0.0), axis=1, keepdims=True) * fraction
    row_diff = similar - row_mean
    row_var = (
        jnp.sum(jnp.where(inside, row_diff * row_diff, 0.0), axis=1, keepdims=True) * fraction
    )
    column_mean = jnp.mean(similar, axis=0, keepdims=True)
    column_diff = similar - column_mean
    column_var = jnp.mean(column_diff * column_diff, axis=0, keepdims=True)
    scores = row_diff * (half_sharp * lax.rsqrt(row_var + 1e-05)) + column_diff * (
        half_sharp * lax.rsqrt(column_var + 1e-05)
    )
    scores = jnp.where(inside, scores, -jnp.inf)
    raised = jnp.exp(scores - jnp.max(scores, axis=1, keepdims=True))
    return raised / jnp.sum(raised, axis=1, keepdims=True)


def weighted_term(weight, alignment, blocks):
    target = blocks[0][...] if len(blocks) == 1 else jnp.concatenate([b[...] for b in blocks])
    return weight * jnp.dot(alignment, target, preferred_element_type=jnp.float32)


def profile_kernel(model_width, targets, last, weight_ref, len_ref, sharp_ref, mine, other, *refs):
    blocks, out_ref = list(refs[:-1]), refs[-1]
    if last:
        posterior_ref, out_ref, posterior_out = blocks[-2], blocks[-1], out_ref
        blocks = blocks[:-2]
        count = posterior_out.shape[1]
        row = lax.broadcasted_iota(jnp.int32, (count, 1), 0)
        lane = lax.broadcasted_iota(jnp.int32, (1, count), 1)
        chosen = jnp.where(row == lane, posterior_ref[:, 0:1], 0.0)
        posterior_out[...] = jnp.sum(chosen, axis=0, keepdims=True)
    rows = mine.shape[1] // len(targets)
    acc = None
    for at, (slot, count) in enumerate(targets):
        part = pl.ds(at * rows, rows)
        similar = (mine[:, part] + other[:, part]) * (1.0 / math.sqrt(model_width))
        alignment = align_block(similar, len_ref[slot : slot + 1, :rows], sharp_ref[:, 0:1])
        term = weighted_term(
            weight_ref[slot : slot + 1, 0:1], alignment.astype(jnp.bfloat16), blocks[:count]
        )
        acc = term if acc is None else acc + term
        blocks = blocks[count:]
    if blocks:
        acc += blocks[0][...]
    out_ref[...] = acc.astype(out_ref.dtype)


def per_device_by_target(
    query_res, target_res, target_len, hits, sharpness, query_pool, target_pool
):
    model_width = query_pool.shape[1]
    target_rows = target_res.shape[1]
    query = query_res[0]
    at_tgt, at_qry, at_rep = (lax.axis_index(name) for name in ("tgt", "qry", "rep"))

    def from_peer(array, k):
        return lax.ppermute(array, "tgt", [(i, i ^ k) for i in range(4)])

    def across(array, axis):
        return lax.ppermute(array, axis, [(0, 1), (1, 0)])

    def after(array, *done):
        return lax.optimization_barrier((array, *done))[0]

    split = [(2 * i + c, 2 * (i ^ (1 + c)) + c) for i in range(4) for c in range(2)]
    pool_split = lax.ppermute(target_pool, ("tgt", "rep"), split)
    pool_last = from_peer(target_pool, 3)
    pool_split = after(pool_split, pool_last)

    share = lax.dynamic_index_in_dim(target_res, at_qry, 0, keepdims=False)
    rest = lax.dynamic_index_in_dim(target_res, 1 - at_qry, 0, keepdims=False)
    far = from_peer(share, 2)
    near = from_peer(share, 1)

    bases = [2 * (at_tgt ^ k) for k in range(4)]
    slots = [bases[0], bases[0] + 1]
    for base in bases[1:]:
        slots += [base + at_qry, base + 1 - at_qry]
    owners = [at_tgt, at_tgt ^ (1 + at_rep), at_tgt ^ (2 - at_rep), at_tgt ^ 3]
    table = (len(target_len), target_rows)
    slots = jnp.broadcast_to(jnp.stack(slots)[:, None], table)
    owners = jnp.broadcast_to(jnp.stack(owners + owners)[:, None], table)
    named = slots[:, : table[0]] == jnp.arange(table[0])[None]
    lengths = jnp.sum(jnp.where(named, target_len[None], 0), axis=1, keepdims=True)
    lengths = jnp.broadcast_to(lengths.astype(jnp.float32), table)
    half_sharp = jnp.broadcast_to(0.5 * sharpness, (1, target_rows))

    def add_up(targets, out_shape, *operands):
        return call_kernel(
            functools.partial(profile_kernel, model_width, targets, isinstance(out_shape, tuple)),
            out_shape,
            weights,
            lengths,
            half_sharp,
            *operands,
        )

    acc_shape = jax.ShapeDtypeStruct(query.shape, jnp.float32)
    far = after(far, pool_split, pool_last, slots, owners, lengths, half_sharp)
    near = after(near, far)
    far = after(far, near)
    half = target_rows // 2
    last = [from_peer(far[:half], 1), from_peer(far[half:], 1)]
    pool_other = across(pool_split, "rep")
    near_rest = from_peer(after(rest, far), 1)

    one_blocks = [target_res[0], target_res[1], near, far]
    one = partial_similar(query, one_blocks)
    one_other = across(one, "rep")
    far_rest = across(after(far, one_other), "qry")
    last_rest = [across(piece, "qry") for piece in last]
    posterior, weights = call_kernel(
        weigh_kernel,
        (
            jax.ShapeDtypeStruct(table, jnp.float32),
            jax.ShapeDtypeStruct(table, jnp.float32),
        ),
        slots,
        after(hits, last[1]),
        query_pool,
        owners,
        target_pool,
        pool_split,
        pool_other,
        pool_last,
        flops=1_000_000_000,
    )
    far_rest = after(far_rest, weights)
    two_blocks = [far_rest, *last]
    two = partial_similar(query, two_blocks)
    two_other = across(two, "rep")

    acc = add_up(
        ((0, 1), (1, 1), (2, 1), (4, 1)), acc_shape, after(one, two), one_other, *one_blocks
    )

    three_blocks = [near_rest, *last_rest]
    three = partial_similar(after(query, acc), three_blocks)
    three_other = across(three, "rep")
    acc = add_up(((5, 1), (6, 2)), acc_shape, after(two, three), two_other, *two_blocks, acc)
    profile, posterior = add_up(
        ((3, 1), (7, 2)),
        (
            jax.ShapeDtypeStruct(query.shape, jnp.bfloat16),
            jax.ShapeDtypeStruct((1, table[0]), jnp.float32),
        ),
        three,
        three_other,
        *three_blocks,
        acc,
        posterior,
    )
    return (profile[None], posterior)


def solution(mesh):
    placed = (
        P(("grp", "tgt", "qry"), None, "rep"),
        P(("grp", "tgt"), None, "rep"),
        P("grp"),
        P(("grp", "tgt", "qry"), None),
        P(("grp", "tgt", "qry")),
        P(("grp", "tgt", "qry"), None),
        P(("grp", "tgt"), None),
    )
    groups = mesh.shape["tgt"]

    def per_device(*arrays):
        query_res, target_res, _, hits = arrays[:4]
        few = (
            query_res.shape[0] == 1
            and groups == 4 <= hits.shape[1] // target_res.shape[0]
            and target_res.shape[0] == mesh.shape["qry"] == 2
            and mesh.shape["rep"] == 2
        )
        return (per_device_by_target if few else per_device_by_hit)(*arrays)

    return jax.shard_map(
        per_device,
        mesh=mesh,
        in_specs=placed,
        out_specs=(P(("grp", "tgt", "qry"), None, "rep"), P(("grp", "tgt", "qry"), None)),
        check_vma=False,
    )
```

```python
import functools
import math

import jax
import jax.numpy as jnp
from jax import lax
from jax.experimental import pallas as pl
from jax.experimental.pallas import tpu as pltpu
from jax.sharding import PartitionSpec as P

VMEM_BYTES = 16 * 1024 * 1024


def softmax_rows(logits):
    highest = jnp.max(logits, axis=-1, keepdims=True)
    raised = jnp.exp(logits - highest)
    return raised / jnp.sum(raised, axis=-1, keepdims=True)


def weigh_alignment(similar, lengths, sharpness, hit_weight):
    target_rows = similar.shape[-1]
    inside = jnp.arange(target_rows)[None, None, None, :] < lengths[:, :, None, None]
    counted = lengths[:, :, None, None].astype(jnp.float32)
    row_mean = jnp.sum(jnp.where(inside, similar, 0.0), axis=-1, keepdims=True) / counted
    row_diff = similar - row_mean
    row_var = jnp.sum(jnp.where(inside, row_diff * row_diff, 0.0), axis=-1, keepdims=True) / counted
    row_score = row_diff / jnp.sqrt(row_var + 1e-05)
    column_mean = jnp.mean(similar, axis=2, keepdims=True)
    column_diff = similar - column_mean
    column_var = jnp.mean(column_diff * column_diff, axis=2, keepdims=True)
    column_score = column_diff / jnp.sqrt(column_var + 1e-05)
    scores = sharpness[:, None, None, None] * (0.5 * (row_score + column_score))
    scores = jnp.where(inside, scores, -jnp.inf)
    alignment = softmax_rows(scores)
    return (hit_weight[:, :, None, None] * alignment).astype(jnp.bfloat16)


def plan_slots(flat_hits, owned_targets, tgt_count, capacity):
    owners = flat_hits // owned_targets
    local_ids = flat_hits % owned_targets
    matched = owners[:, None] == jnp.arange(tgt_count)[None, :]
    earlier = jnp.cumsum(matched.astype(jnp.int32), axis=0) - 1
    rank_in = jnp.sum(jnp.where(matched, earlier, 0), axis=1)
    slot_of = owners * capacity + rank_in
    placed = slot_of[:, None] == jnp.arange(tgt_count * capacity)[None, :]
    wanted = jnp.sum(jnp.where(placed, local_ids[:, None], 0), axis=0).reshape(tgt_count, capacity)
    return (wanted, slot_of)


def fetch_shares(target_res, flat_hits, capacity):
    tgt_count = lax.axis_size("tgt")
    owned_targets, target_rows, width = target_res.shape
    wanted, slot_of = plan_slots(flat_hits, owned_targets, tgt_count, capacity)
    requested = lax.all_to_all(wanted, "tgt", split_axis=0, concat_axis=0, tiled=True)
    outgoing = jnp.take(target_res, requested.reshape(tgt_count * capacity), axis=0)
    outgoing = outgoing.reshape(tgt_count, capacity, target_rows, width)
    arrived = lax.all_to_all(outgoing, "tgt", split_axis=0, concat_axis=0, tiled=True)
    return jnp.take(arrived.reshape(tgt_count * capacity, target_rows, width), slot_of, axis=0)


def per_device_by_hit(query_res, target_res, target_len, hits, sharpness, query_pool, target_pool):
    tgt_count = lax.axis_size("tgt")
    query_count = query_res.shape[0]
    target_rows = target_res.shape[1]
    hit_count = hits.shape[1]
    pair_count = query_count * hit_count
    model_width = query_pool.shape[1]
    capacity = max(2, (2 * pair_count + tgt_count - 1) // tgt_count)
    library = lax.all_gather(target_pool, "tgt", axis=0, tiled=True)
    logits = jnp.dot(query_pool, library.T, precision=lax.Precision.HIGHEST) / math.sqrt(
        model_width
    )
    posterior = softmax_rows(logits)
    matches = hits[:, :, None] == jnp.arange(library.shape[0])[None, None, :]
    hit_weight = softmax_rows(jnp.sum(jnp.where(matches, logits[:, None, :], 0.0), axis=-1))
    lengths = jnp.sum(jnp.where(matches, target_len[None, None, :], 0), axis=-1)
    half_width = query_res.shape[2]
    chosen = fetch_shares(target_res, hits.reshape(pair_count), capacity)
    chosen = chosen.reshape(query_count, hit_count, target_rows, half_width)
    partial_sim = jnp.einsum(
        "qid,qhjd->qhij", query_res, chosen, preferred_element_type=jnp.float32
    ) / math.sqrt(model_width)
    similar = lax.psum(partial_sim, "rep")
    weighted = weigh_alignment(similar, lengths, sharpness, hit_weight)
    profile = jnp.einsum("qhij,qhjd->qid", weighted, chosen, preferred_element_type=jnp.float32)
    return (profile.astype(jnp.bfloat16), posterior)


VMEM = pl.BlockSpec(memory_space=pltpu.VMEM)


def call_kernel(kernel, out_shape, *operands, scratch=(), flops=0):
    return pl.pallas_call(
        kernel,
        out_shape=out_shape,
        in_specs=[VMEM] * len(operands),
        out_specs=jax.tree.map(lambda _: VMEM, out_shape),
        scratch_shapes=scratch,
        cost_estimate=pl.CostEstimate(flops=flops, bytes_accessed=0, transcendentals=0),
        compiler_params=pltpu.CompilerParams(vmem_limit_bytes=VMEM_BYTES),
    )(*operands)


def share_kernel(at_ref, blocks_ref, share_ref, done):
    copy = pltpu.make_async_copy(blocks_ref.at[at_ref[0]], share_ref, done)
    copy.start()
    copy.wait()


def take_share(blocks, at):
    return pl.pallas_call(
        share_kernel,
        out_shape=jax.ShapeDtypeStruct(blocks.shape[1:], blocks.dtype),
        in_specs=[pl.BlockSpec(memory_space=pltpu.SMEM), pl.BlockSpec(memory_space=pl.ANY)],
        out_specs=pl.BlockSpec(memory_space=pl.ANY),
        scratch_shapes=[pltpu.SemaphoreType.DMA],
        cost_estimate=pl.CostEstimate(flops=0, bytes_accessed=0, transcendentals=0),
        compiler_params=pltpu.CompilerParams(vmem_limit_bytes=62*1024*1024),
    )(at.astype(jnp.int32)[None], blocks)


def weigh_kernel(slot_ref, hits_ref, pool_ref, owner_ref, *refs):
    libs, (posterior_ref, weight_ref) = refs[:-2], refs[-2:]
    owned, width = libs[0].shape
    target_count = posterior_ref.shape[0]
    target = lax.broadcasted_iota(jnp.int32, (target_count, 1), 0)
    counts = jnp.sum(jnp.where(hits_ref[...] == target, 1.0, 0.0), axis=1, keepdims=True)
    logits = jnp.zeros((target_count, 1), jnp.float32)
    for at, lib in enumerate(libs):
        products = jnp.sum(lib[...] * pool_ref[...], axis=1, keepdims=True) / math.sqrt(width)
        first = owner_ref[at : at + 1, 0:1] * owned
        for a in range(owned):
            logits = jnp.where(target == first + a, products[a : a + 1, :], logits)
    raised = jnp.exp(logits - jnp.max(logits, axis=0, keepdims=True))
    posterior = raised / jnp.sum(raised, axis=0, keepdims=True)
    shown = jnp.where(counts > 0.0, logits, -jnp.inf)
    parts = counts * jnp.exp(shown - jnp.max(shown, axis=0, keepdims=True))
    weights = parts / jnp.sum(parts, axis=0, keepdims=True)
    lane = lax.broadcasted_iota(jnp.int32, (1, target_count), 1)
    posterior_ref[...] = jnp.broadcast_to(posterior, posterior_ref.shape)
    weights = jnp.sum(jnp.where(target == lane, weights, 0.0), axis=0, keepdims=True)
    weights = jnp.where(slot_ref[:, 0:1] == lane, weights, 0.0)
    weights = jnp.sum(weights, axis=1, keepdims=True)
    weight_ref[...] = jnp.broadcast_to(weights, weight_ref.shape)


def partial_kernel(*refs):
    query, blocks, out = refs[0], refs[1:-1], refs[-1]
    out[...] = lax.dot_general(
        query[...],
        jnp.concatenate([block[...] for block in blocks]),
        (((1,), (1,)), ((), ())),
        preferred_element_type=jnp.float32,
    )


def partial_similar(query, blocks):
    rows = sum(block.shape[0] for block in blocks)
    shape = jax.ShapeDtypeStruct((query.shape[0], rows), jnp.float32)
    return call_kernel(partial_kernel, shape, query, *blocks)


def align_block(similar, length, half_sharp):
    column = lax.broadcasted_iota(jnp.int32, (1, similar.shape[1]), 1).astype(jnp.float32)
    inside = column < length
    fraction = 1.0 / length[:, 0:1]
    row_mean = jnp.sum(jnp.where(inside, similar, 0.0), axis=1, keepdims=True) * fraction
    row_diff = similar - row_mean
    row_var = (
        jnp.sum(jnp.where(inside, row_diff * row_diff, 0.0), axis=1, keepdims=True) * fraction
    )
    column_mean = jnp.mean(similar, axis=0, keepdims=True)
    column_diff = similar - column_mean
    column_var = jnp.mean(column_diff * column_diff, axis=0, keepdims=True)
    scores = row_diff * (half_sharp * lax.rsqrt(row_var + 1e-05)) + column_diff * (
        half_sharp * lax.rsqrt(column_var + 1e-05)
    )
    scores = jnp.where(inside, scores, -jnp.inf)
    raised = jnp.exp(scores - jnp.max(scores, axis=1, keepdims=True))
    return raised / jnp.sum(raised, axis=1, keepdims=True)


def weighted_term(weight, alignment, blocks):
    target = blocks[0][...] if len(blocks) == 1 else jnp.concatenate([b[...] for b in blocks])
    return weight * jnp.dot(alignment, target, preferred_element_type=jnp.float32)


def profile_kernel(model_width, targets, last, weight_ref, len_ref, sharp_ref, mine, other, *refs):
    blocks, out_ref = list(refs[:-1]), refs[-1]
    if last:
        posterior_ref, out_ref, posterior_out = blocks[-2], blocks[-1], out_ref
        blocks = blocks[:-2]
        count = posterior_out.shape[1]
        row = lax.broadcasted_iota(jnp.int32, (count, 1), 0)
        lane = lax.broadcasted_iota(jnp.int32, (1, count), 1)
        chosen = jnp.where(row == lane, posterior_ref[:, 0:1], 0.0)
        posterior_out[...] = jnp.sum(chosen, axis=0, keepdims=True)
    rows = mine.shape[1] // len(targets)
    acc = None
    for at, (slot, count) in enumerate(targets):
        part = pl.ds(at * rows, rows)
        similar = (mine[:, part] + other[:, part]) * (1.0 / math.sqrt(model_width))
        alignment = align_block(similar, len_ref[slot : slot + 1, :rows], sharp_ref[:, 0:1])
        term = weighted_term(
            weight_ref[slot : slot + 1, 0:1], alignment.astype(jnp.bfloat16), blocks[:count]
        )
        acc = term if acc is None else acc + term
        blocks = blocks[count:]
    if blocks:
        acc += blocks[0][...]
    out_ref[...] = acc.astype(out_ref.dtype)


def per_device_by_target(
    query_res, target_res, target_len, hits, sharpness, query_pool, target_pool
):
    model_width = query_pool.shape[1]
    target_rows = target_res.shape[1]
    query = query_res[0]
    at_tgt, at_qry, at_rep = (lax.axis_index(name) for name in ("tgt", "qry", "rep"))

    def from_peer(array, k):
        return lax.ppermute(array, "tgt", [(i, i ^ k) for i in range(4)])

    def across(array, axis):
        return lax.ppermute(array, axis, [(0, 1), (1, 0)])

    def after(array, *done):
        return lax.optimization_barrier((array, *done))[0]

    split = [(2 * i + c, 2 * (i ^ (1 + c)) + c) for i in range(4) for c in range(2)]

    share = take_share(target_res, at_qry)
    far = from_peer(share, 2)
    rest = lax.dynamic_index_in_dim(after(target_res, share), 1 - at_qry, 0, keepdims=False)
    pool = after(target_pool, rest)
    pool_split = lax.ppermute(pool, ("tgt", "rep"), split)
    pool_last = from_peer(pool, 3)
    pool_split = after(pool_split, pool_last)
    near = from_peer(share, 1)

    bases = [2 * (at_tgt ^ k) for k in range(4)]
    slots = [bases[0], bases[0] + 1]
    for base in bases[1:]:
        slots += [base + at_qry, base + 1 - at_qry]
    owners = [at_tgt, at_tgt ^ (1 + at_rep), at_tgt ^ (2 - at_rep), at_tgt ^ 3]
    table = (len(target_len), target_rows)
    slots = jnp.broadcast_to(jnp.stack(slots)[:, None], table)
    owners = jnp.broadcast_to(jnp.stack(owners + owners)[:, None], table)
    named = slots[:, : table[0]] == jnp.arange(table[0])[None]
    lengths = jnp.sum(jnp.where(named, target_len[None], 0), axis=1, keepdims=True)
    lengths = jnp.broadcast_to(lengths.astype(jnp.float32), table)
    half_sharp = jnp.broadcast_to(0.5 * sharpness, (1, target_rows))

    def add_up(targets, out_shape, *operands):
        return call_kernel(
            functools.partial(profile_kernel, model_width, targets, isinstance(out_shape, tuple)),
            out_shape,
            weights,
            lengths,
            half_sharp,
            *operands,
        )

    acc_shape = jax.ShapeDtypeStruct(query.shape, jnp.float32)
    far = after(far, pool_split, pool_last, slots, owners, lengths, half_sharp)
    near = after(near, far)
    far = after(far, near)
    half = target_rows // 2
    last = [from_peer(far[:half], 1), from_peer(far[half:], 1)]
    pool_other = across(pool_split, "rep")
    near_rest = from_peer(after(rest, far), 1)

    own = after(target_res, share)
    one_blocks = [own[0], own[1], near, far]
    one = partial_similar(query, one_blocks)
    one_other = across(one, "rep")
    far_rest = across(after(far, one_other), "qry")
    last_rest = [across(piece, "qry") for piece in last]
    posterior, weights = call_kernel(
        weigh_kernel,
        (
            jax.ShapeDtypeStruct(table, jnp.float32),
            jax.ShapeDtypeStruct(table, jnp.float32),
        ),
        slots,
        after(hits, last[1]),
        query_pool,
        owners,
        target_pool,
        pool_split,
        pool_other,
        pool_last,
        flops=1_000_000_000,
    )
    far_rest = after(far_rest, weights)
    two_blocks = [far_rest, *last]
    two = partial_similar(query, two_blocks)
    two_other = across(two, "rep")

    acc = add_up(
        ((0, 1), (1, 1), (2, 1), (4, 1)), acc_shape, after(one, two), one_other, *one_blocks
    )

    three_blocks = [near_rest, *last_rest]
    three = partial_similar(after(query, acc), three_blocks)
    three_other = across(three, "rep")
    acc = add_up(((5, 1), (6, 2)), acc_shape, after(two, three), two_other, *two_blocks, acc)
    profile, posterior = add_up(
        ((3, 1), (7, 2)),
        (
            jax.ShapeDtypeStruct(query.shape, jnp.bfloat16),
            jax.ShapeDtypeStruct((1, table[0]), jnp.float32),
        ),
        three,
        three_other,
        *three_blocks,
        acc,
        posterior,
    )
    return (profile[None], posterior)


def solution(mesh):
    placed = (
        P(("grp", "tgt", "qry"), None, "rep"),
        P(("grp", "tgt"), None, "rep"),
        P("grp"),
        P(("grp", "tgt", "qry"), None),
        P(("grp", "tgt", "qry")),
        P(("grp", "tgt", "qry"), None),
        P(("grp", "tgt"), None),
    )
    groups = mesh.shape["tgt"]

    def per_device(*arrays):
        query_res, target_res, _, hits = arrays[:4]
        few = (
            query_res.shape[0] == 1
            and groups == 4 <= hits.shape[1] // target_res.shape[0]
            and target_res.shape[0] == mesh.shape["qry"] == 2
            and mesh.shape["rep"] == 2
        )
        return (per_device_by_target if few else per_device_by_hit)(*arrays)

    return jax.shard_map(
        per_device,
        mesh=mesh,
        in_specs=placed,
        out_specs=(P(("grp", "tgt", "qry"), None, "rep"), P(("grp", "tgt", "qry"), None)),
        check_vma=False,
    )
```

```python
import functools
import math

import jax
import jax.numpy as jnp
from jax import lax
from jax.experimental import pallas as pl
from jax.experimental.pallas import tpu as pltpu
from jax.sharding import PartitionSpec as P

VMEM_BYTES = 16 * 1024 * 1024


def softmax_rows(logits):
    highest = jnp.max(logits, axis=-1, keepdims=True)
    raised = jnp.exp(logits - highest)
    return raised / jnp.sum(raised, axis=-1, keepdims=True)


def weigh_alignment(similar, lengths, sharpness, hit_weight):
    target_rows = similar.shape[-1]
    inside = jnp.arange(target_rows)[None, None, None, :] < lengths[:, :, None, None]
    counted = lengths[:, :, None, None].astype(jnp.float32)
    row_mean = jnp.sum(jnp.where(inside, similar, 0.0), axis=-1, keepdims=True) / counted
    row_diff = similar - row_mean
    row_var = jnp.sum(jnp.where(inside, row_diff * row_diff, 0.0), axis=-1, keepdims=True) / counted
    row_score = row_diff / jnp.sqrt(row_var + 1e-05)
    column_mean = jnp.mean(similar, axis=2, keepdims=True)
    column_diff = similar - column_mean
    column_var = jnp.mean(column_diff * column_diff, axis=2, keepdims=True)
    column_score = column_diff / jnp.sqrt(column_var + 1e-05)
    scores = sharpness[:, None, None, None] * (0.5 * (row_score + column_score))
    scores = jnp.where(inside, scores, -jnp.inf)
    alignment = softmax_rows(scores)
    return (hit_weight[:, :, None, None] * alignment).astype(jnp.bfloat16)


def plan_slots(flat_hits, owned_targets, tgt_count, capacity):
    owners = flat_hits // owned_targets
    local_ids = flat_hits % owned_targets
    matched = owners[:, None] == jnp.arange(tgt_count)[None, :]
    earlier = jnp.cumsum(matched.astype(jnp.int32), axis=0) - 1
    rank_in = jnp.sum(jnp.where(matched, earlier, 0), axis=1)
    slot_of = owners * capacity + rank_in
    placed = slot_of[:, None] == jnp.arange(tgt_count * capacity)[None, :]
    wanted = jnp.sum(jnp.where(placed, local_ids[:, None], 0), axis=0).reshape(tgt_count, capacity)
    return (wanted, slot_of)


def fetch_shares(target_res, flat_hits, capacity):
    tgt_count = lax.axis_size("tgt")
    owned_targets, target_rows, width = target_res.shape
    wanted, slot_of = plan_slots(flat_hits, owned_targets, tgt_count, capacity)
    requested = lax.all_to_all(wanted, "tgt", split_axis=0, concat_axis=0, tiled=True)
    outgoing = jnp.take(target_res, requested.reshape(tgt_count * capacity), axis=0)
    outgoing = outgoing.reshape(tgt_count, capacity, target_rows, width)
    arrived = lax.all_to_all(outgoing, "tgt", split_axis=0, concat_axis=0, tiled=True)
    return jnp.take(arrived.reshape(tgt_count * capacity, target_rows, width), slot_of, axis=0)


def per_device_by_hit(query_res, target_res, target_len, hits, sharpness, query_pool, target_pool):
    tgt_count = lax.axis_size("tgt")
    query_count = query_res.shape[0]
    target_rows = target_res.shape[1]
    hit_count = hits.shape[1]
    pair_count = query_count * hit_count
    model_width = query_pool.shape[1]
    capacity = max(2, (2 * pair_count + tgt_count - 1) // tgt_count)
    library = lax.all_gather(target_pool, "tgt", axis=0, tiled=True)
    logits = jnp.dot(query_pool, library.T, precision=lax.Precision.HIGHEST) / math.sqrt(
        model_width
    )
    posterior = softmax_rows(logits)
    matches = hits[:, :, None] == jnp.arange(library.shape[0])[None, None, :]
    hit_weight = softmax_rows(jnp.sum(jnp.where(matches, logits[:, None, :], 0.0), axis=-1))
    lengths = jnp.sum(jnp.where(matches, target_len[None, None, :], 0), axis=-1)
    half_width = query_res.shape[2]
    chosen = fetch_shares(target_res, hits.reshape(pair_count), capacity)
    chosen = chosen.reshape(query_count, hit_count, target_rows, half_width)
    partial_sim = jnp.einsum(
        "qid,qhjd->qhij", query_res, chosen, preferred_element_type=jnp.float32
    ) / math.sqrt(model_width)
    similar = lax.psum(partial_sim, "rep")
    weighted = weigh_alignment(similar, lengths, sharpness, hit_weight)
    profile = jnp.einsum("qhij,qhjd->qid", weighted, chosen, preferred_element_type=jnp.float32)
    return (profile.astype(jnp.bfloat16), posterior)


VMEM = pl.BlockSpec(memory_space=pltpu.VMEM)


def call_kernel(kernel, out_shape, *operands, scratch=(), flops=0):
    return pl.pallas_call(
        kernel,
        out_shape=out_shape,
        in_specs=[VMEM] * len(operands),
        out_specs=jax.tree.map(lambda _: VMEM, out_shape),
        scratch_shapes=scratch,
        cost_estimate=pl.CostEstimate(flops=flops, bytes_accessed=0, transcendentals=0),
        compiler_params=pltpu.CompilerParams(vmem_limit_bytes=VMEM_BYTES),
    )(*operands)


def weigh_kernel(slot_ref, hits_ref, pool_ref, owner_ref, *refs):
    libs, (posterior_ref, weight_ref) = refs[:-2], refs[-2:]
    owned, width = libs[0].shape
    target_count = posterior_ref.shape[0]
    target = lax.broadcasted_iota(jnp.int32, (target_count, 1), 0)
    counts = jnp.sum(jnp.where(hits_ref[...] == target, 1.0, 0.0), axis=1, keepdims=True)
    logits = jnp.zeros((target_count, 1), jnp.float32)
    for at, lib in enumerate(libs):
        products = jnp.sum(lib[...] * pool_ref[...], axis=1, keepdims=True) / math.sqrt(width)
        first = owner_ref[at : at + 1, 0:1] * owned
        for a in range(owned):
            logits = jnp.where(target == first + a, products[a : a + 1, :], logits)
    raised = jnp.exp(logits - jnp.max(logits, axis=0, keepdims=True))
    posterior = raised / jnp.sum(raised, axis=0, keepdims=True)
    shown = jnp.where(counts > 0.0, logits, -jnp.inf)
    parts = counts * jnp.exp(shown - jnp.max(shown, axis=0, keepdims=True))
    weights = parts / jnp.sum(parts, axis=0, keepdims=True)
    lane = lax.broadcasted_iota(jnp.int32, (1, target_count), 1)
    posterior_ref[...] = jnp.broadcast_to(posterior, posterior_ref.shape)
    weights = jnp.sum(jnp.where(target == lane, weights, 0.0), axis=0, keepdims=True)
    weights = jnp.where(slot_ref[:, 0:1] == lane, weights, 0.0)
    weights = jnp.sum(weights, axis=1, keepdims=True)
    weight_ref[...] = jnp.broadcast_to(weights, weight_ref.shape)


def partial_kernel(groups, *refs):
    query, blocks, outs = refs[0], refs[1 : -len(groups)], refs[-len(groups) :]
    for count, out in zip(groups, outs):
        out[...] = lax.dot_general(
            query[...],
            jnp.concatenate([block[...] for block in blocks[:count]]),
            (((1,), (1,)), ((), ())),
            preferred_element_type=jnp.float32,
        )
        blocks = blocks[count:]


def partial_similar(query, *groups, flops=0):
    shapes = tuple(
        jax.ShapeDtypeStruct((query.shape[0], sum(b.shape[0] for b in group)), jnp.float32)
        for group in groups
    )
    kernel = functools.partial(partial_kernel, [len(group) for group in groups])
    blocks = [block for group in groups for block in group]
    return call_kernel(kernel, shapes, query, *blocks, flops=flops)


def align_block(similar, length, half_sharp):
    column = lax.broadcasted_iota(jnp.int32, (1, similar.shape[1]), 1).astype(jnp.float32)
    inside = column < length
    fraction = 1.0 / length[:, 0:1]
    row_mean = jnp.sum(jnp.where(inside, similar, 0.0), axis=1, keepdims=True) * fraction
    row_diff = similar - row_mean
    row_var = (
        jnp.sum(jnp.where(inside, row_diff * row_diff, 0.0), axis=1, keepdims=True) * fraction
    )
    column_mean = jnp.mean(similar, axis=0, keepdims=True)
    column_diff = similar - column_mean
    column_var = jnp.mean(column_diff * column_diff, axis=0, keepdims=True)
    scores = row_diff * (half_sharp * lax.rsqrt(row_var + 1e-05)) + column_diff * (
        half_sharp * lax.rsqrt(column_var + 1e-05)
    )
    scores = jnp.where(inside, scores, -jnp.inf)
    raised = jnp.exp(scores - jnp.max(scores, axis=1, keepdims=True))
    return raised / jnp.sum(raised, axis=1, keepdims=True)


def profile_kernel(model_width, groups, last, weight_ref, len_ref, sharp_ref, *refs):
    acc = None
    for slots, counts in groups:
        mine, other, refs = refs[0], refs[1], refs[2:]
        rows = mine.shape[1] // len(slots)
        for at, (slot, count) in enumerate(zip(slots, counts)):
            part = pl.ds(at * rows, rows)
            similar = (mine[:, part] + other[:, part]) * (1.0 / math.sqrt(model_width))
            alignment = align_block(similar, len_ref[slot : slot + 1, :rows], sharp_ref[:, 0:1])
            target = jnp.concatenate([block[...] for block in refs[:count]])
            term = weight_ref[slot : slot + 1, 0:1] * jnp.dot(
                alignment.astype(jnp.bfloat16), target, preferred_element_type=jnp.float32
            )
            acc = term if acc is None else acc + term
            refs = refs[count:]
    if last:
        acc_ref, posterior_ref, out_ref, posterior_out = refs
        count = posterior_out.shape[1]
        row = lax.broadcasted_iota(jnp.int32, (count, 1), 0)
        lane = lax.broadcasted_iota(jnp.int32, (1, count), 1)
        chosen = jnp.where(row == lane, posterior_ref[:, 0:1], 0.0)
        posterior_out[...] = jnp.sum(chosen, axis=0, keepdims=True)
        acc += acc_ref[...]
    else:
        out_ref = refs[-1]
        if len(refs) > 1:
            acc += refs[0][...]
    out_ref[...] = acc.astype(out_ref.dtype)


def per_device_by_target(
    query_res, target_res, target_len, hits, sharpness, query_pool, target_pool
):
    model_width = query_pool.shape[1]
    target_rows = target_res.shape[1]
    query = query_res[0]
    at_tgt, at_qry, at_rep = (lax.axis_index(name) for name in ("tgt", "qry", "rep"))

    def from_peer(array, k):
        return lax.ppermute(array, "tgt", [(i, i ^ k) for i in range(4)])

    def across(array, axis):
        return lax.ppermute(array, axis, [(0, 1), (1, 0)])

    def after(array, *done):
        return lax.optimization_barrier((array, *done))[0]

    split = [(2 * i + c, 2 * (i ^ (1 + c)) + c) for i in range(4) for c in range(2)]
    pool_split = lax.ppermute(target_pool, ("tgt", "rep"), split)
    pool_last = from_peer(target_pool, 3)
    pool_split = after(pool_split, pool_last)

    share = lax.dynamic_index_in_dim(target_res, at_qry, 0, keepdims=False)
    rest = lax.dynamic_index_in_dim(target_res, 1 - at_qry, 0, keepdims=False)
    far = from_peer(share, 2)
    near = from_peer(share, 1)

    bases = [2 * (at_tgt ^ k) for k in range(4)]
    slots = [bases[0], bases[0] + 1]
    for base in bases[1:]:
        slots += [base + at_qry, base + 1 - at_qry]
    owners = [at_tgt, at_tgt ^ (1 + at_rep), at_tgt ^ (2 - at_rep), at_tgt ^ 3]
    table = (len(target_len), target_rows)
    slots = jnp.broadcast_to(jnp.stack(slots)[:, None], table)
    owners = jnp.broadcast_to(jnp.stack(owners + owners)[:, None], table)
    named = slots[:, : table[0]] == jnp.arange(table[0])[None]
    lengths = jnp.sum(jnp.where(named, target_len[None], 0), axis=1, keepdims=True)
    lengths = jnp.broadcast_to(lengths.astype(jnp.float32), table)
    half_sharp = jnp.broadcast_to(0.5 * sharpness, (1, target_rows))

    def add_up(groups, out_shape, *operands):
        return call_kernel(
            functools.partial(profile_kernel, model_width, groups, isinstance(out_shape, tuple)),
            out_shape,
            weights,
            lengths,
            half_sharp,
            *operands,
        )

    acc_shape = jax.ShapeDtypeStruct(query.shape, jnp.float32)
    far = after(far, pool_split, pool_last, slots, owners, lengths, half_sharp)
    near = after(near, far)
    far = after(far, near)
    half = target_rows // 2
    last = [from_peer(far[:half], 1), from_peer(far[half:], 1)]
    pool_other = across(pool_split, "rep")
    near_rest = from_peer(after(rest, far), 1)

    own_blocks = [target_res[0], target_res[1]]
    one_blocks = [near, far]
    (one,) = partial_similar(query, own_blocks + one_blocks)
    one_other = across(one, "rep")
    far_rest = across(after(far, one_other), "qry")
    last_rest = [across(piece, "qry") for piece in last]
    posterior, weights = call_kernel(
        weigh_kernel,
        (
            jax.ShapeDtypeStruct(table, jnp.float32),
            jax.ShapeDtypeStruct(table, jnp.float32),
        ),
        slots,
        after(hits, last[1]),
        query_pool,
        owners,
        target_pool,
        pool_split,
        pool_other,
        pool_last,
        flops=1000000000,
    )
    far_rest = after(far_rest, weights)
    two_blocks = [far_rest, *last]
    two, two_b = partial_similar(query, [far_rest], last, flops=0)
    two_other, two_b_other = across(two, "rep"), across(two_b, "rep")

    acc = add_up(
        (((0, 1, 2, 4), (1, 1, 1, 1)),),
        acc_shape,
        after(one, two),
        one_other,
        *own_blocks,
        *one_blocks,
    )

    (three,) = partial_similar(after(query, two), [near_rest])
    three_other = across(three, "rep")
    (four,) = partial_similar(after(query, acc, three), last_rest)
    four_other = across(four, "rep")
    acc = add_up(
        (((5,), (1,)), ((6,), (2,)), ((3,), (1,))),
        acc_shape,
        after(two, four),
        two_other,
        far_rest,
        two_b,
        two_b_other,
        *last,
        three,
        three_other,
        near_rest,
        acc,
    )
    profile, posterior = add_up(
        (((7,), (2,)),),
        (
            jax.ShapeDtypeStruct(query.shape, jnp.bfloat16),
            jax.ShapeDtypeStruct((1, table[0]), jnp.float32),
        ),
        four,
        four_other,
        *last_rest,
        acc,
        posterior,
    )
    return (profile[None], posterior)


def solution(mesh):
    placed = (
        P(("grp", "tgt", "qry"), None, "rep"),
        P(("grp", "tgt"), None, "rep"),
        P("grp"),
        P(("grp", "tgt", "qry"), None),
        P(("grp", "tgt", "qry")),
        P(("grp", "tgt", "qry"), None),
        P(("grp", "tgt"), None),
    )
    groups = mesh.shape["tgt"]

    def per_device(*arrays):
        query_res, target_res, _, hits = arrays[:4]
        few = (
            query_res.shape[0] == 1
            and groups == 4 <= hits.shape[1] // target_res.shape[0]
            and target_res.shape[0] == mesh.shape["qry"] == 2
            and mesh.shape["rep"] == 2
        )
        return (per_device_by_target if few else per_device_by_hit)(*arrays)

    return jax.shard_map(
        per_device,
        mesh=mesh,
        in_specs=placed,
        out_specs=(P(("grp", "tgt", "qry"), None, "rep"), P(("grp", "tgt", "qry"), None)),
        check_vma=False,
    )
```

```python
import functools
import math

import jax
import jax.numpy as jnp
from jax import lax
from jax.experimental import pallas as pl
from jax.experimental.pallas import tpu as pltpu
from jax.sharding import PartitionSpec as P

VMEM_BYTES = 16 * 1024 * 1024


def softmax_rows(logits):
    highest = jnp.max(logits, axis=-1, keepdims=True)
    raised = jnp.exp(logits - highest)
    return raised / jnp.sum(raised, axis=-1, keepdims=True)


def weigh_alignment(similar, lengths, sharpness, hit_weight):
    target_rows = similar.shape[-1]
    inside = jnp.arange(target_rows)[None, None, None, :] < lengths[:, :, None, None]
    counted = lengths[:, :, None, None].astype(jnp.float32)
    row_mean = jnp.sum(jnp.where(inside, similar, 0.0), axis=-1, keepdims=True) / counted
    row_diff = similar - row_mean
    row_var = jnp.sum(jnp.where(inside, row_diff * row_diff, 0.0), axis=-1, keepdims=True) / counted
    row_score = row_diff / jnp.sqrt(row_var + 1e-05)
    column_mean = jnp.mean(similar, axis=2, keepdims=True)
    column_diff = similar - column_mean
    column_var = jnp.mean(column_diff * column_diff, axis=2, keepdims=True)
    column_score = column_diff / jnp.sqrt(column_var + 1e-05)
    scores = sharpness[:, None, None, None] * (0.5 * (row_score + column_score))
    scores = jnp.where(inside, scores, -jnp.inf)
    alignment = softmax_rows(scores)
    return (hit_weight[:, :, None, None] * alignment).astype(jnp.bfloat16)


def plan_slots(flat_hits, owned_targets, tgt_count, capacity):
    owners = flat_hits // owned_targets
    local_ids = flat_hits % owned_targets
    matched = owners[:, None] == jnp.arange(tgt_count)[None, :]
    earlier = jnp.cumsum(matched.astype(jnp.int32), axis=0) - 1
    rank_in = jnp.sum(jnp.where(matched, earlier, 0), axis=1)
    slot_of = owners * capacity + rank_in
    placed = slot_of[:, None] == jnp.arange(tgt_count * capacity)[None, :]
    wanted = jnp.sum(jnp.where(placed, local_ids[:, None], 0), axis=0).reshape(tgt_count, capacity)
    return (wanted, slot_of)


def fetch_shares(target_res, flat_hits, capacity):
    tgt_count = lax.axis_size("tgt")
    owned_targets, target_rows, width = target_res.shape
    wanted, slot_of = plan_slots(flat_hits, owned_targets, tgt_count, capacity)
    requested = lax.all_to_all(wanted, "tgt", split_axis=0, concat_axis=0, tiled=True)
    outgoing = jnp.take(target_res, requested.reshape(tgt_count * capacity), axis=0)
    outgoing = outgoing.reshape(tgt_count, capacity, target_rows, width)
    arrived = lax.all_to_all(outgoing, "tgt", split_axis=0, concat_axis=0, tiled=True)
    return jnp.take(arrived.reshape(tgt_count * capacity, target_rows, width), slot_of, axis=0)


def per_device_by_hit(query_res, target_res, target_len, hits, sharpness, query_pool, target_pool):
    tgt_count = lax.axis_size("tgt")
    query_count = query_res.shape[0]
    target_rows = target_res.shape[1]
    hit_count = hits.shape[1]
    pair_count = query_count * hit_count
    model_width = query_pool.shape[1]
    capacity = max(2, (2 * pair_count + tgt_count - 1) // tgt_count)
    library = lax.all_gather(target_pool, "tgt", axis=0, tiled=True)
    logits = jnp.dot(query_pool, library.T, precision=lax.Precision.HIGHEST) / math.sqrt(
        model_width
    )
    posterior = softmax_rows(logits)
    matches = hits[:, :, None] == jnp.arange(library.shape[0])[None, None, :]
    hit_weight = softmax_rows(jnp.sum(jnp.where(matches, logits[:, None, :], 0.0), axis=-1))
    lengths = jnp.sum(jnp.where(matches, target_len[None, None, :], 0), axis=-1)
    half_width = query_res.shape[2]
    chosen = fetch_shares(target_res, hits.reshape(pair_count), capacity)
    chosen = chosen.reshape(query_count, hit_count, target_rows, half_width)
    partial_sim = jnp.einsum(
        "qid,qhjd->qhij", query_res, chosen, preferred_element_type=jnp.float32
    ) / math.sqrt(model_width)
    similar = lax.psum(partial_sim, "rep")
    weighted = weigh_alignment(similar, lengths, sharpness, hit_weight)
    profile = jnp.einsum("qhij,qhjd->qid", weighted, chosen, preferred_element_type=jnp.float32)
    return (profile.astype(jnp.bfloat16), posterior)


VMEM = pl.BlockSpec(memory_space=pltpu.VMEM)


def call_kernel(kernel, out_shape, *operands, scratch=(), flops=0):
    return pl.pallas_call(
        kernel,
        out_shape=out_shape,
        in_specs=[VMEM] * len(operands),
        out_specs=jax.tree.map(lambda _: VMEM, out_shape),
        scratch_shapes=scratch,
        cost_estimate=pl.CostEstimate(flops=flops, bytes_accessed=0, transcendentals=0),
        compiler_params=pltpu.CompilerParams(vmem_limit_bytes=VMEM_BYTES),
    )(*operands)


def weigh_kernel(table_ref, hits_ref, pool_ref, *refs):
    libs, (posterior_ref, weight_ref) = refs[:-2], refs[-2:]
    owned, width = libs[0].shape
    target_count = posterior_ref.shape[0]
    target = lax.broadcasted_iota(jnp.int32, (target_count, 1), 0).astype(jnp.float32)
    hits = hits_ref[...].astype(jnp.float32)
    counts = jnp.sum(jnp.where(hits == target, 1.0, 0.0), axis=1, keepdims=True)
    logits = jnp.zeros((target_count, 1), jnp.float32)
    for at, lib in enumerate(libs):
        products = jnp.sum(lib[...] * pool_ref[...], axis=1, keepdims=True) / math.sqrt(width)
        first = table_ref[target_count + at : target_count + at + 1, 0:1] * owned
        for a in range(owned):
            logits = jnp.where(target == first + a, products[a : a + 1, :], logits)
    raised = jnp.exp(logits - jnp.max(logits, axis=0, keepdims=True))
    posterior = raised / jnp.sum(raised, axis=0, keepdims=True)
    shown = jnp.where(counts > 0.0, logits, -jnp.inf)
    parts = counts * jnp.exp(shown - jnp.max(shown, axis=0, keepdims=True))
    weights = parts / jnp.sum(parts, axis=0, keepdims=True)
    lane = lax.broadcasted_iota(jnp.int32, (1, target_count), 1).astype(jnp.float32)
    posterior_ref[...] = jnp.broadcast_to(posterior, posterior_ref.shape)
    weights = jnp.sum(jnp.where(target == lane, weights, 0.0), axis=0, keepdims=True)
    weights = jnp.where(table_ref[:target_count, 0:1] == lane, weights, 0.0)
    weights = jnp.sum(weights, axis=1, keepdims=True)
    weight_ref[...] = jnp.broadcast_to(weights, weight_ref.shape)


def partial_kernel(groups, *refs):
    query, blocks, outs = refs[0], refs[1 : -len(groups)], refs[-len(groups) :]
    for count, out in zip(groups, outs):
        out[...] = lax.dot_general(
            query[...],
            jnp.concatenate([block[...] for block in blocks[:count]]),
            (((1,), (1,)), ((), ())),
            preferred_element_type=jnp.float32,
        )
        blocks = blocks[count:]


def partial_similar(query, *groups, flops=0):
    shapes = tuple(
        jax.ShapeDtypeStruct((query.shape[0], sum(b.shape[0] for b in group)), jnp.float32)
        for group in groups
    )
    kernel = functools.partial(partial_kernel, [len(group) for group in groups])
    blocks = [block for group in groups for block in group]
    return call_kernel(kernel, shapes, query, *blocks, flops=flops)


def align_block(similar, length, half_sharp):
    column = lax.broadcasted_iota(jnp.int32, (1, similar.shape[1]), 1).astype(jnp.float32)
    inside = column < length
    fraction = 1.0 / length[:, 0:1]
    row_mean = jnp.sum(jnp.where(inside, similar, 0.0), axis=1, keepdims=True) * fraction
    row_diff = similar - row_mean
    row_var = (
        jnp.sum(jnp.where(inside, row_diff * row_diff, 0.0), axis=1, keepdims=True) * fraction
    )
    column_mean = jnp.mean(similar, axis=0, keepdims=True)
    column_diff = similar - column_mean
    column_var = jnp.mean(column_diff * column_diff, axis=0, keepdims=True)
    scores = row_diff * (half_sharp * lax.rsqrt(row_var + 1e-05)) + column_diff * (
        half_sharp * lax.rsqrt(column_var + 1e-05)
    )
    scores = jnp.where(inside, scores, -jnp.inf)
    raised = jnp.exp(scores - jnp.max(scores, axis=1, keepdims=True))
    return raised / jnp.sum(raised, axis=1, keepdims=True)


def profile_kernel(model_width, groups, last, weight_ref, table_ref, sharp_ref, *refs):
    acc, lengths = None, 2 * weight_ref.shape[0]
    for slots, counts in groups:
        mine, other, refs = refs[0], refs[1], refs[2:]
        rows = mine.shape[1] // len(slots)
        for at, (slot, count) in enumerate(zip(slots, counts)):
            part = pl.ds(at * rows, rows)
            similar = (mine[:, part] + other[:, part]) * (1.0 / math.sqrt(model_width))
            length = table_ref[lengths + slot : lengths + slot + 1, :rows]
            alignment = align_block(similar, length, sharp_ref[:, 0:1])
            target = jnp.concatenate([block[...] for block in refs[:count]])
            term = weight_ref[slot : slot + 1, 0:1] * jnp.dot(
                alignment.astype(jnp.bfloat16), target, preferred_element_type=jnp.float32
            )
            acc = term if acc is None else acc + term
            refs = refs[count:]
    if last:
        acc_ref, posterior_ref, out_ref, posterior_out = refs
        count = posterior_out.shape[1]
        row = lax.broadcasted_iota(jnp.int32, (count, 1), 0)
        lane = lax.broadcasted_iota(jnp.int32, (1, count), 1)
        chosen = jnp.where(row == lane, posterior_ref[:, 0:1], 0.0)
        posterior_out[...] = jnp.sum(chosen, axis=0, keepdims=True)
        acc += acc_ref[...]
    else:
        out_ref = refs[-1]
        if len(refs) > 1:
            acc += refs[0][...]
    out_ref[...] = acc.astype(out_ref.dtype)


def per_device_by_target(
    query_res, target_res, target_len, hits, sharpness, query_pool, target_pool
):
    model_width = query_pool.shape[1]
    target_rows = target_res.shape[1]
    query = query_res[0]
    at_tgt, at_qry, at_rep = (lax.axis_index(name) for name in ("tgt", "qry", "rep"))

    def from_peer(array, k):
        return lax.ppermute(array, "tgt", [(i, i ^ k) for i in range(4)])

    def across(array, axis):
        return lax.ppermute(array, axis, [(0, 1), (1, 0)])

    def after(array, *done):
        return lax.optimization_barrier((array, *done))[0]

    split = [(2 * i + c, 2 * (i ^ (1 + c)) + c) for i in range(4) for c in range(2)]
    pool_split = lax.ppermute(target_pool, ("tgt", "rep"), split)
    pool_last = from_peer(target_pool, 3)
    pool_split = after(pool_split, pool_last)

    share = lax.dynamic_index_in_dim(target_res, at_qry, 0, keepdims=False)
    rest = lax.dynamic_index_in_dim(target_res, 1 - at_qry, 0, keepdims=False)
    far = from_peer(share, 2)
    near = from_peer(share, 1)

    bases = [2 * (at_tgt ^ k) for k in range(4)]
    slots = [bases[0], bases[0] + 1]
    for base in bases[1:]:
        slots += [base + at_qry, base + 1 - at_qry]
    owners = [at_tgt, at_tgt ^ (1 + at_rep), at_tgt ^ (2 - at_rep), at_tgt ^ 3]
    count = len(target_len)
    slots = jnp.stack(slots)
    named = slots[:, None] == jnp.arange(count)[None]
    lengths = jnp.sum(jnp.where(named, target_len[None], 0), axis=1)
    table = jnp.concatenate([slots, jnp.stack(owners + owners), lengths]).astype(jnp.float32)
    table = jnp.broadcast_to(table[:, None], (3 * count, target_rows))
    half_sharp = jnp.broadcast_to(0.5 * sharpness, (1, target_rows))

    def add_up(groups, out_shape, *operands):
        return call_kernel(
            functools.partial(profile_kernel, model_width, groups, isinstance(out_shape, tuple)),
            out_shape,
            weights,
            table,
            half_sharp,
            *operands,
        )

    acc_shape = jax.ShapeDtypeStruct(query.shape, jnp.float32)
    own_blocks = [target_res[0], target_res[1]]
    (own,) = partial_similar(after(query, share), own_blocks)
    own_other = across(own, "rep")

    far = after(far, pool_split, pool_last, table, half_sharp)
    near = after(near, far)
    far = after(far, near)
    half = target_rows // 2
    last = [from_peer(far[:half], 1), from_peer(far[half:], 1)]
    pool_other = across(pool_split, "rep")
    near_rest = from_peer(after(rest, far), 1)

    one_blocks = [near, far]
    (one,) = partial_similar(query, one_blocks)
    one_other = across(one, "rep")
    far_rest = across(after(far, one_other), "qry")
    last = [last[0], after(last[1], pool_other)]
    last_rest = [across(piece, "qry") for piece in last]
    posterior, weights = call_kernel(
        weigh_kernel,
        (
            jax.ShapeDtypeStruct((count, target_rows), jnp.float32),
            jax.ShapeDtypeStruct((count, target_rows), jnp.float32),
        ),
        table,
        after(hits, last[1]),
        query_pool,
        target_pool,
        pool_split,
        pool_other,
        pool_last,
        flops=1500000000,
    )
    far_rest = after(far_rest, weights)
    two_blocks = [far_rest, *last]
    (two,) = partial_similar(query, two_blocks, flops=0)
    two_other = across(two, "rep")

    acc = add_up(
        (((0, 1), (1, 1)), ((2, 4), (1, 1))),
        acc_shape,
        after(own, two),
        own_other,
        *own_blocks,
        one,
        one_other,
        *one_blocks,
    )

    three_blocks = [near_rest, *last_rest]
    (three,) = partial_similar(after(query, acc), three_blocks)
    three_other = across(three, "rep")
    acc = add_up(
        (((5, 6), (1, 2)),), acc_shape, after(two, three), two_other, *two_blocks, acc
    )
    profile, posterior = add_up(
        (((3, 7), (1, 2)),),
        (
            jax.ShapeDtypeStruct(query.shape, jnp.bfloat16),
            jax.ShapeDtypeStruct((1, count), jnp.float32),
        ),
        three,
        three_other,
        *three_blocks,
        acc,
        posterior,
    )
    return (profile[None], posterior)


def solution(mesh):
    placed = (
        P(("grp", "tgt", "qry"), None, "rep"),
        P(("grp", "tgt"), None, "rep"),
        P("grp"),
        P(("grp", "tgt", "qry"), None),
        P(("grp", "tgt", "qry")),
        P(("grp", "tgt", "qry"), None),
        P(("grp", "tgt"), None),
    )
    groups = mesh.shape["tgt"]

    def per_device(*arrays):
        query_res, target_res, _, hits = arrays[:4]
        few = (
            query_res.shape[0] == 1
            and groups == 4 <= hits.shape[1] // target_res.shape[0]
            and target_res.shape[0] == mesh.shape["qry"] == 2
            and mesh.shape["rep"] == 2
        )
        return (per_device_by_target if few else per_device_by_hit)(*arrays)

    return jax.shard_map(
        per_device,
        mesh=mesh,
        in_specs=placed,
        out_specs=(P(("grp", "tgt", "qry"), None, "rep"), P(("grp", "tgt", "qry"), None)),
        check_vma=False,
    )
```

```python
import functools
import math

import jax
import jax.numpy as jnp
from jax import lax
from jax.experimental import pallas as pl
from jax.experimental.pallas import tpu as pltpu
from jax.sharding import PartitionSpec as P

VMEM_BYTES = 16 * 1024 * 1024


def softmax_rows(logits):
    highest = jnp.max(logits, axis=-1, keepdims=True)
    raised = jnp.exp(logits - highest)
    return raised / jnp.sum(raised, axis=-1, keepdims=True)


def weigh_alignment(similar, lengths, sharpness, hit_weight):
    target_rows = similar.shape[-1]
    inside = jnp.arange(target_rows)[None, None, None, :] < lengths[:, :, None, None]
    counted = lengths[:, :, None, None].astype(jnp.float32)
    row_mean = jnp.sum(jnp.where(inside, similar, 0.0), axis=-1, keepdims=True) / counted
    row_diff = similar - row_mean
    row_var = jnp.sum(jnp.where(inside, row_diff * row_diff, 0.0), axis=-1, keepdims=True) / counted
    row_score = row_diff / jnp.sqrt(row_var + 1e-05)
    column_mean = jnp.mean(similar, axis=2, keepdims=True)
    column_diff = similar - column_mean
    column_var = jnp.mean(column_diff * column_diff, axis=2, keepdims=True)
    column_score = column_diff / jnp.sqrt(column_var + 1e-05)
    scores = sharpness[:, None, None, None] * (0.5 * (row_score + column_score))
    scores = jnp.where(inside, scores, -jnp.inf)
    alignment = softmax_rows(scores)
    return (hit_weight[:, :, None, None] * alignment).astype(jnp.bfloat16)


def plan_slots(flat_hits, owned_targets, tgt_count, capacity):
    owners = flat_hits // owned_targets
    local_ids = flat_hits % owned_targets
    matched = owners[:, None] == jnp.arange(tgt_count)[None, :]
    earlier = jnp.cumsum(matched.astype(jnp.int32), axis=0) - 1
    rank_in = jnp.sum(jnp.where(matched, earlier, 0), axis=1)
    slot_of = owners * capacity + rank_in
    placed = slot_of[:, None] == jnp.arange(tgt_count * capacity)[None, :]
    wanted = jnp.sum(jnp.where(placed, local_ids[:, None], 0), axis=0).reshape(tgt_count, capacity)
    return (wanted, slot_of)


def fetch_shares(target_res, flat_hits, capacity):
    tgt_count = lax.axis_size("tgt")
    owned_targets, target_rows, width = target_res.shape
    wanted, slot_of = plan_slots(flat_hits, owned_targets, tgt_count, capacity)
    requested = lax.all_to_all(wanted, "tgt", split_axis=0, concat_axis=0, tiled=True)
    outgoing = jnp.take(target_res, requested.reshape(tgt_count * capacity), axis=0)
    outgoing = outgoing.reshape(tgt_count, capacity, target_rows, width)
    arrived = lax.all_to_all(outgoing, "tgt", split_axis=0, concat_axis=0, tiled=True)
    return jnp.take(arrived.reshape(tgt_count * capacity, target_rows, width), slot_of, axis=0)


def per_device_by_hit(query_res, target_res, target_len, hits, sharpness, query_pool, target_pool):
    tgt_count = lax.axis_size("tgt")
    query_count = query_res.shape[0]
    target_rows = target_res.shape[1]
    hit_count = hits.shape[1]
    pair_count = query_count * hit_count
    model_width = query_pool.shape[1]
    capacity = max(2, (2 * pair_count + tgt_count - 1) // tgt_count)
    library = lax.all_gather(target_pool, "tgt", axis=0, tiled=True)
    logits = jnp.dot(query_pool, library.T, precision=lax.Precision.HIGHEST) / math.sqrt(
        model_width
    )
    posterior = softmax_rows(logits)
    matches = hits[:, :, None] == jnp.arange(library.shape[0])[None, None, :]
    hit_weight = softmax_rows(jnp.sum(jnp.where(matches, logits[:, None, :], 0.0), axis=-1))
    lengths = jnp.sum(jnp.where(matches, target_len[None, None, :], 0), axis=-1)
    half_width = query_res.shape[2]
    chosen = fetch_shares(target_res, hits.reshape(pair_count), capacity)
    chosen = chosen.reshape(query_count, hit_count, target_rows, half_width)
    partial_sim = jnp.einsum(
        "qid,qhjd->qhij", query_res, chosen, preferred_element_type=jnp.float32
    ) / math.sqrt(model_width)
    similar = lax.psum(partial_sim, "rep")
    weighted = weigh_alignment(similar, lengths, sharpness, hit_weight)
    profile = jnp.einsum("qhij,qhjd->qid", weighted, chosen, preferred_element_type=jnp.float32)
    return (profile.astype(jnp.bfloat16), posterior)


VMEM = pl.BlockSpec(memory_space=pltpu.VMEM)


def call_kernel(kernel, out_shape, *operands, scratch=(), flops=0):
    return pl.pallas_call(
        kernel,
        out_shape=out_shape,
        in_specs=[VMEM] * len(operands),
        out_specs=jax.tree.map(lambda _: VMEM, out_shape),
        scratch_shapes=scratch,
        cost_estimate=pl.CostEstimate(flops=flops, bytes_accessed=0, transcendentals=0),
        compiler_params=pltpu.CompilerParams(vmem_limit_bytes=VMEM_BYTES),
    )(*operands)


def weigh_kernel(table_ref, hits_ref, pool_ref, *refs):
    libs, (posterior_ref, weight_ref) = refs[:-2], refs[-2:]
    owned, width = libs[0].shape
    target_count = posterior_ref.shape[0]
    target = lax.broadcasted_iota(jnp.int32, (target_count, 1), 0).astype(jnp.float32)
    hits = hits_ref[...].astype(jnp.float32)
    counts = jnp.sum(jnp.where(hits == target, 1.0, 0.0), axis=1, keepdims=True)
    logits = jnp.zeros((target_count, 1), jnp.float32)
    for at, lib in enumerate(libs):
        products = jnp.sum(lib[...] * pool_ref[...], axis=1, keepdims=True) / math.sqrt(width)
        first = table_ref[target_count + at : target_count + at + 1, 0:1] * owned
        for a in range(owned):
            logits = jnp.where(target == first + a, products[a : a + 1, :], logits)
    raised = jnp.exp(logits - jnp.max(logits, axis=0, keepdims=True))
    posterior = raised / jnp.sum(raised, axis=0, keepdims=True)
    shown = jnp.where(counts > 0.0, logits, -jnp.inf)
    parts = counts * jnp.exp(shown - jnp.max(shown, axis=0, keepdims=True))
    weights = parts / jnp.sum(parts, axis=0, keepdims=True)
    lane = lax.broadcasted_iota(jnp.int32, (1, target_count), 1).astype(jnp.float32)
    posterior_ref[...] = jnp.broadcast_to(posterior, posterior_ref.shape)
    weights = jnp.sum(jnp.where(target == lane, weights, 0.0), axis=0, keepdims=True)
    weights = jnp.where(table_ref[:target_count, 0:1] == lane, weights, 0.0)
    weights = jnp.sum(weights, axis=1, keepdims=True)
    weight_ref[...] = jnp.broadcast_to(weights, weight_ref.shape)


def partial_kernel(groups, *refs):
    query, blocks, outs = refs[0], refs[1 : -len(groups)], refs[-len(groups) :]
    for count, out in zip(groups, outs):
        out[...] = lax.dot_general(
            query[...],
            jnp.concatenate([block[...] for block in blocks[:count]]),
            (((1,), (1,)), ((), ())),
            preferred_element_type=jnp.float32,
        )
        blocks = blocks[count:]


def partial_similar(query, *groups, flops=0):
    shapes = tuple(
        jax.ShapeDtypeStruct((query.shape[0], sum(b.shape[0] for b in group)), jnp.float32)
        for group in groups
    )
    kernel = functools.partial(partial_kernel, [len(group) for group in groups])
    blocks = [block for group in groups for block in group]
    return call_kernel(kernel, shapes, query, *blocks, flops=flops)


def align_block(similar, length, half_sharp):
    column = lax.broadcasted_iota(jnp.int32, (1, similar.shape[1]), 1).astype(jnp.float32)
    inside = column < length
    fraction = 1.0 / length[:, 0:1]
    row_mean = jnp.sum(jnp.where(inside, similar, 0.0), axis=1, keepdims=True) * fraction
    row_diff = similar - row_mean
    row_var = (
        jnp.sum(jnp.where(inside, row_diff * row_diff, 0.0), axis=1, keepdims=True) * fraction
    )
    column_mean = jnp.mean(similar, axis=0, keepdims=True)
    column_diff = similar - column_mean
    column_var = jnp.mean(column_diff * column_diff, axis=0, keepdims=True)
    scores = row_diff * (half_sharp * lax.rsqrt(row_var + 1e-05)) + column_diff * (
        half_sharp * lax.rsqrt(column_var + 1e-05)
    )
    scores = jnp.where(inside, scores, -jnp.inf)
    raised = jnp.exp(scores - jnp.max(scores, axis=1, keepdims=True))
    return raised / jnp.sum(raised, axis=1, keepdims=True)


def profile_kernel(model_width, groups, last, weight_ref, table_ref, sharp_ref, *refs):
    acc, lengths = None, 2 * weight_ref.shape[0]
    for slots, counts in groups:
        mine, other, refs = refs[0], refs[1], refs[2:]
        rows = mine.shape[1] // len(slots)
        for at, (slot, count) in enumerate(zip(slots, counts)):
            part = pl.ds(at * rows, rows)
            similar = (mine[:, part] + other[:, part]) * (1.0 / math.sqrt(model_width))
            length = table_ref[lengths + slot : lengths + slot + 1, :rows]
            alignment = align_block(similar, length, sharp_ref[:, 0:1])
            target = jnp.concatenate([block[...] for block in refs[:count]])
            term = weight_ref[slot : slot + 1, 0:1] * jnp.dot(
                alignment.astype(jnp.bfloat16), target, preferred_element_type=jnp.float32
            )
            acc = term if acc is None else acc + term
            refs = refs[count:]
    if last:
        acc_ref, posterior_ref, out_ref, posterior_out = refs
        count = posterior_out.shape[1]
        row = lax.broadcasted_iota(jnp.int32, (count, 1), 0)
        lane = lax.broadcasted_iota(jnp.int32, (1, count), 1)
        chosen = jnp.where(row == lane, posterior_ref[:, 0:1], 0.0)
        posterior_out[...] = jnp.sum(chosen, axis=0, keepdims=True)
        acc += acc_ref[...]
    else:
        out_ref = refs[-1]
        if len(refs) > 1:
            acc += refs[0][...]
    out_ref[...] = acc.astype(out_ref.dtype)


def per_device_by_target(
    query_res, target_res, target_len, hits, sharpness, query_pool, target_pool
):
    model_width = query_pool.shape[1]
    target_rows = target_res.shape[1]
    query = query_res[0]
    at_tgt, at_qry, at_rep = (lax.axis_index(name) for name in ("tgt", "qry", "rep"))

    def from_peer(array, k):
        return lax.ppermute(array, "tgt", [(i, i ^ k) for i in range(4)])

    def across(array, axis):
        return lax.ppermute(array, axis, [(0, 1), (1, 0)])

    def after(array, *done):
        return lax.optimization_barrier((array, *done))[0]

    split = [(2 * i + c, 2 * (i ^ (1 + c)) + c) for i in range(4) for c in range(2)]
    pool_split = lax.ppermute(target_pool, ("tgt", "rep"), split)
    pool_last = from_peer(target_pool, 3)
    pool_split = after(pool_split, pool_last)

    share = lax.dynamic_index_in_dim(target_res, at_qry, 0, keepdims=False)
    rest = lax.dynamic_index_in_dim(target_res, 1 - at_qry, 0, keepdims=False)
    far = from_peer(share, 2)
    near = from_peer(share, 1)

    bases = [2 * (at_tgt ^ k) for k in range(4)]
    slots = [bases[0], bases[0] + 1]
    for base in bases[1:]:
        slots += [base + at_qry, base + 1 - at_qry]
    owners = [at_tgt, at_tgt ^ (1 + at_rep), at_tgt ^ (2 - at_rep), at_tgt ^ 3]
    count = len(target_len)
    slots = jnp.stack(slots)
    named = slots[:, None] == jnp.arange(count)[None]
    lengths = jnp.sum(jnp.where(named, target_len[None], 0), axis=1)
    table = jnp.concatenate([slots, jnp.stack(owners + owners), lengths]).astype(jnp.float32)
    table = jnp.broadcast_to(table[:, None], (3 * count, target_rows))
    half_sharp = jnp.broadcast_to(0.5 * sharpness, (1, target_rows))

    def add_up(groups, out_shape, *operands):
        return call_kernel(
            functools.partial(profile_kernel, model_width, groups, isinstance(out_shape, tuple)),
            out_shape,
            weights,
            table,
            half_sharp,
            *operands,
        )

    acc_shape = jax.ShapeDtypeStruct(query.shape, jnp.float32)
    far = after(far, pool_split, pool_last, table, half_sharp)
    near = after(near, far)
    far = after(far, near)
    half = target_rows // 2
    last = [from_peer(far[:half], 1), from_peer(far[half:], 1)]
    pool_other = across(pool_split, "rep")
    near_rest = from_peer(after(rest, far), 1)

    own_blocks = [target_res[0], target_res[1]]
    one_blocks = [near, far]
    (one,) = partial_similar(query, own_blocks + one_blocks)
    one_other = across(one, "rep")
    far_rest = across(after(far, one_other), "qry")
    last_rest = [across(piece, "qry") for piece in last]
    posterior, weights = call_kernel(
        weigh_kernel,
        (
            jax.ShapeDtypeStruct((count, target_rows), jnp.float32),
            jax.ShapeDtypeStruct((count, target_rows), jnp.float32),
        ),
        table,
        after(hits, last[1]),
        query_pool,
        target_pool,
        pool_split,
        pool_other,
        pool_last,
        flops=1000000000,
    )
    far_rest = after(far_rest, weights)
    two_blocks = [far_rest, *last]
    (two,) = partial_similar(query, two_blocks, flops=0)
    two_other = across(two, "rep")

    acc = add_up(
        (((0, 1, 2, 4), (1, 1, 1, 1)),),
        acc_shape,
        after(one, two),
        one_other,
        *own_blocks,
        *one_blocks,
    )

    three_blocks = [near_rest, *last_rest]
    (three,) = partial_similar(after(query, acc), three_blocks)
    three_other = across(three, "rep")
    acc = add_up(
        (((5, 6), (1, 2)),), acc_shape, after(two, three), two_other, *two_blocks, acc
    )
    profile, posterior = add_up(
        (((3, 7), (1, 2)),),
        (
            jax.ShapeDtypeStruct(query.shape, jnp.bfloat16),
            jax.ShapeDtypeStruct((1, count), jnp.float32),
        ),
        three,
        three_other,
        *three_blocks,
        acc,
        posterior,
    )
    return (profile[None], posterior)


def solution(mesh):
    placed = (
        P(("grp", "tgt", "qry"), None, "rep"),
        P(("grp", "tgt"), None, "rep"),
        P("grp"),
        P(("grp", "tgt", "qry"), None),
        P(("grp", "tgt", "qry")),
        P(("grp", "tgt", "qry"), None),
        P(("grp", "tgt"), None),
    )
    groups = mesh.shape["tgt"]

    def per_device(*arrays):
        query_res, target_res, _, hits = arrays[:4]
        few = (
            query_res.shape[0] == 1
            and groups == 4 <= hits.shape[1] // target_res.shape[0]
            and target_res.shape[0] == mesh.shape["qry"] == 2
            and mesh.shape["rep"] == 2
        )
        return (per_device_by_target if few else per_device_by_hit)(*arrays)

    return jax.shard_map(
        per_device,
        mesh=mesh,
        in_specs=placed,
        out_specs=(P(("grp", "tgt", "qry"), None, "rep"), P(("grp", "tgt", "qry"), None)),
        check_vma=False,
    )
```

```python
import functools
import math

import jax
import jax.numpy as jnp
from jax import lax
from jax.experimental import pallas as pl
from jax.experimental.pallas import tpu as pltpu
from jax.sharding import PartitionSpec as P

VMEM_BYTES = 16 * 1024 * 1024


def softmax_rows(logits):
    highest = jnp.max(logits, axis=-1, keepdims=True)
    raised = jnp.exp(logits - highest)
    return raised / jnp.sum(raised, axis=-1, keepdims=True)


def weigh_alignment(similar, lengths, sharpness, hit_weight):
    target_rows = similar.shape[-1]
    inside = jnp.arange(target_rows)[None, None, None, :] < lengths[:, :, None, None]
    counted = lengths[:, :, None, None].astype(jnp.float32)
    row_mean = jnp.sum(jnp.where(inside, similar, 0.0), axis=-1, keepdims=True) / counted
    row_diff = similar - row_mean
    row_var = jnp.sum(jnp.where(inside, row_diff * row_diff, 0.0), axis=-1, keepdims=True) / counted
    row_score = row_diff / jnp.sqrt(row_var + 1e-05)
    column_mean = jnp.mean(similar, axis=2, keepdims=True)
    column_diff = similar - column_mean
    column_var = jnp.mean(column_diff * column_diff, axis=2, keepdims=True)
    column_score = column_diff / jnp.sqrt(column_var + 1e-05)
    scores = sharpness[:, None, None, None] * (0.5 * (row_score + column_score))
    scores = jnp.where(inside, scores, -jnp.inf)
    alignment = softmax_rows(scores)
    return (hit_weight[:, :, None, None] * alignment).astype(jnp.bfloat16)


def plan_slots(flat_hits, owned_targets, tgt_count, capacity):
    owners = flat_hits // owned_targets
    local_ids = flat_hits % owned_targets
    matched = owners[:, None] == jnp.arange(tgt_count)[None, :]
    earlier = jnp.cumsum(matched.astype(jnp.int32), axis=0) - 1
    rank_in = jnp.sum(jnp.where(matched, earlier, 0), axis=1)
    slot_of = owners * capacity + rank_in
    placed = slot_of[:, None] == jnp.arange(tgt_count * capacity)[None, :]
    wanted = jnp.sum(jnp.where(placed, local_ids[:, None], 0), axis=0).reshape(tgt_count, capacity)
    return (wanted, slot_of)


def fetch_shares(target_res, flat_hits, capacity):
    tgt_count = lax.axis_size("tgt")
    owned_targets, target_rows, width = target_res.shape
    wanted, slot_of = plan_slots(flat_hits, owned_targets, tgt_count, capacity)
    requested = lax.all_to_all(wanted, "tgt", split_axis=0, concat_axis=0, tiled=True)
    outgoing = jnp.take(target_res, requested.reshape(tgt_count * capacity), axis=0)
    outgoing = outgoing.reshape(tgt_count, capacity, target_rows, width)
    arrived = lax.all_to_all(outgoing, "tgt", split_axis=0, concat_axis=0, tiled=True)
    return jnp.take(arrived.reshape(tgt_count * capacity, target_rows, width), slot_of, axis=0)


def per_device_by_hit(query_res, target_res, target_len, hits, sharpness, query_pool, target_pool):
    tgt_count = lax.axis_size("tgt")
    query_count = query_res.shape[0]
    target_rows = target_res.shape[1]
    hit_count = hits.shape[1]
    pair_count = query_count * hit_count
    model_width = query_pool.shape[1]
    capacity = max(2, (2 * pair_count + tgt_count - 1) // tgt_count)
    library = lax.all_gather(target_pool, "tgt", axis=0, tiled=True)
    logits = jnp.dot(query_pool, library.T, precision=lax.Precision.HIGHEST) / math.sqrt(
        model_width
    )
    posterior = softmax_rows(logits)
    matches = hits[:, :, None] == jnp.arange(library.shape[0])[None, None, :]
    hit_weight = softmax_rows(jnp.sum(jnp.where(matches, logits[:, None, :], 0.0), axis=-1))
    lengths = jnp.sum(jnp.where(matches, target_len[None, None, :], 0), axis=-1)
    half_width = query_res.shape[2]
    chosen = fetch_shares(target_res, hits.reshape(pair_count), capacity)
    chosen = chosen.reshape(query_count, hit_count, target_rows, half_width)
    partial_sim = jnp.einsum(
        "qid,qhjd->qhij", query_res, chosen, preferred_element_type=jnp.float32
    ) / math.sqrt(model_width)
    similar = lax.psum(partial_sim, "rep")
    weighted = weigh_alignment(similar, lengths, sharpness, hit_weight)
    profile = jnp.einsum("qhij,qhjd->qid", weighted, chosen, preferred_element_type=jnp.float32)
    return (profile.astype(jnp.bfloat16), posterior)


VMEM = pl.BlockSpec(memory_space=pltpu.VMEM)


def call_kernel(kernel, out_shape, *operands, scratch=(), flops=0):
    return pl.pallas_call(
        kernel,
        out_shape=out_shape,
        in_specs=[VMEM] * len(operands),
        out_specs=jax.tree.map(lambda _: VMEM, out_shape),
        scratch_shapes=scratch,
        cost_estimate=pl.CostEstimate(flops=flops, bytes_accessed=0, transcendentals=0),
        compiler_params=pltpu.CompilerParams(vmem_limit_bytes=VMEM_BYTES),
    )(*operands)


def weigh_kernel(slot_ref, hits_ref, pool_ref, owner_ref, *refs):
    libs, (posterior_ref, weight_ref) = refs[:-2], refs[-2:]
    owned, width = libs[0].shape
    target_count = posterior_ref.shape[0]
    target = lax.broadcasted_iota(jnp.int32, (target_count, 1), 0)
    counts = jnp.sum(jnp.where(hits_ref[...] == target, 1.0, 0.0), axis=1, keepdims=True)
    logits = jnp.zeros((target_count, 1), jnp.float32)
    for at, lib in enumerate(libs):
        products = jnp.sum(lib[...] * pool_ref[...], axis=1, keepdims=True) / math.sqrt(width)
        first = owner_ref[at : at + 1, 0:1] * owned
        for a in range(owned):
            logits = jnp.where(target == first + a, products[a : a + 1, :], logits)
    raised = jnp.exp(logits - jnp.max(logits, axis=0, keepdims=True))
    posterior = raised / jnp.sum(raised, axis=0, keepdims=True)
    shown = jnp.where(counts > 0.0, logits, -jnp.inf)
    parts = counts * jnp.exp(shown - jnp.max(shown, axis=0, keepdims=True))
    weights = parts / jnp.sum(parts, axis=0, keepdims=True)
    lane = lax.broadcasted_iota(jnp.int32, (1, target_count), 1)
    posterior_ref[...] = jnp.broadcast_to(posterior, posterior_ref.shape)
    weights = jnp.sum(jnp.where(target == lane, weights, 0.0), axis=0, keepdims=True)
    weights = jnp.where(slot_ref[:, 0:1] == lane, weights, 0.0)
    weights = jnp.sum(weights, axis=1, keepdims=True)
    weight_ref[...] = jnp.broadcast_to(weights, weight_ref.shape)


def partial_kernel(*refs):
    query, blocks, out = refs[0], refs[1:-1], refs[-1]
    out[...] = lax.dot_general(
        query[...],
        jnp.concatenate([block[...] for block in blocks]),
        (((1,), (1,)), ((), ())),
        preferred_element_type=jnp.float32,
    )


def partial_similar(query, blocks):
    rows = sum(block.shape[0] for block in blocks)
    shape = jax.ShapeDtypeStruct((query.shape[0], rows), jnp.float32)
    return call_kernel(partial_kernel, shape, query, *blocks)


def align_block(similar, length, half_sharp):
    column = lax.broadcasted_iota(jnp.int32, (1, similar.shape[1]), 1).astype(jnp.float32)
    inside = column < length
    fraction = 1.0 / length[:, 0:1]
    row_mean = jnp.sum(jnp.where(inside, similar, 0.0), axis=1, keepdims=True) * fraction
    row_diff = similar - row_mean
    row_var = (
        jnp.sum(jnp.where(inside, row_diff * row_diff, 0.0), axis=1, keepdims=True) * fraction
    )
    column_mean = jnp.mean(similar, axis=0, keepdims=True)
    column_diff = similar - column_mean
    column_var = jnp.mean(column_diff * column_diff, axis=0, keepdims=True)
    scores = row_diff * (half_sharp * lax.rsqrt(row_var + 1e-05)) + column_diff * (
        half_sharp * lax.rsqrt(column_var + 1e-05)
    )
    scores = jnp.where(inside, scores, -jnp.inf)
    raised = jnp.exp(scores - jnp.max(scores, axis=1, keepdims=True))
    return raised, jnp.sum(raised, axis=1, keepdims=True)


def weighted_term(weight, alignment, blocks):
    target = blocks[0][...] if len(blocks) == 1 else jnp.concatenate([b[...] for b in blocks])
    return weight * jnp.dot(alignment, target, preferred_element_type=jnp.float32)


def profile_kernel(model_width, targets, last, weight_ref, len_ref, sharp_ref, mine, other, *refs):
    blocks, out_ref = list(refs[:-1]), refs[-1]
    if last:
        posterior_ref, out_ref, posterior_out = blocks[-2], blocks[-1], out_ref
        blocks = blocks[:-2]
        count = posterior_out.shape[1]
        row = lax.broadcasted_iota(jnp.int32, (count, 1), 0)
        lane = lax.broadcasted_iota(jnp.int32, (1, count), 1)
        chosen = jnp.where(row == lane, posterior_ref[:, 0:1], 0.0)
        posterior_out[...] = jnp.sum(chosen, axis=0, keepdims=True)
    rows = mine.shape[1] // len(targets)
    acc = None
    for at, (slot, count) in enumerate(targets):
        part = pl.ds(at * rows, rows)
        similar = (mine[:, part] + other[:, part]) * (1.0 / math.sqrt(model_width))
        raised, total = align_block(similar, len_ref[slot : slot + 1, :rows], sharp_ref[:, 0:1])
        term = weighted_term(
            weight_ref[slot : slot + 1, 0:1] / total, raised.astype(jnp.bfloat16), blocks[:count]
        )
        acc = term if acc is None else acc + term
        blocks = blocks[count:]
    if blocks:
        acc += blocks[0][...]
    out_ref[...] = acc.astype(out_ref.dtype)


def per_device_by_target(
    query_res, target_res, target_len, hits, sharpness, query_pool, target_pool
):
    model_width = query_pool.shape[1]
    target_rows = target_res.shape[1]
    query = query_res[0]
    at_tgt, at_qry, at_rep = (lax.axis_index(name) for name in ("tgt", "qry", "rep"))

    def from_peer(array, k):
        return lax.ppermute(array, "tgt", [(i, i ^ k) for i in range(4)])

    def across(array, axis):
        return lax.ppermute(array, axis, [(0, 1), (1, 0)])

    def after(array, *done):
        return lax.optimization_barrier((array, *done))[0]

    split = [(2 * i + c, 2 * (i ^ (1 + c)) + c) for i in range(4) for c in range(2)]
    pool_split = lax.ppermute(target_pool, ("tgt", "rep"), split)
    pool_last = from_peer(target_pool, 3)
    pool_split = after(pool_split, pool_last)

    share = lax.dynamic_index_in_dim(target_res, at_qry, 0, keepdims=False)
    rest = lax.dynamic_index_in_dim(target_res, 1 - at_qry, 0, keepdims=False)
    far = from_peer(share, 2)
    near = from_peer(share, 1)

    bases = [2 * (at_tgt ^ k) for k in range(4)]
    slots = [bases[0], bases[0] + 1]
    for base in bases[1:]:
        slots += [base + at_qry, base + 1 - at_qry]
    owners = [at_tgt, at_tgt ^ (1 + at_rep), at_tgt ^ (2 - at_rep), at_tgt ^ 3]
    table = (len(target_len), target_rows)
    slots = jnp.broadcast_to(jnp.stack(slots)[:, None], table)
    owners = jnp.broadcast_to(jnp.stack(owners + owners)[:, None], table)
    named = slots[:, : table[0]] == jnp.arange(table[0])[None]
    lengths = jnp.sum(jnp.where(named, target_len[None], 0), axis=1, keepdims=True)
    lengths = jnp.broadcast_to(lengths.astype(jnp.float32), table)
    half_sharp = jnp.broadcast_to(0.5 * sharpness, (1, target_rows))

    def add_up(targets, out_shape, *operands):
        return call_kernel(
            functools.partial(profile_kernel, model_width, targets, isinstance(out_shape, tuple)),
            out_shape,
            weights,
            lengths,
            half_sharp,
            *operands,
        )

    acc_shape = jax.ShapeDtypeStruct(query.shape, jnp.float32)
    far = after(far, pool_split, pool_last, slots, owners, lengths, half_sharp)
    near = after(near, far)
    far = after(far, near)
    half = target_rows // 2
    last = [from_peer(far[:half], 1), from_peer(far[half:], 1)]
    pool_other = across(pool_split, "rep")
    near_rest = from_peer(after(rest, far), 1)

    one_blocks = [target_res[0], target_res[1], near, far]
    one = partial_similar(query, one_blocks)
    one_other = across(one, "rep")
    far_rest = across(after(far, one_other), "qry")
    last_rest = [across(piece, "qry") for piece in last]
    posterior, weights = call_kernel(
        weigh_kernel,
        (
            jax.ShapeDtypeStruct(table, jnp.float32),
            jax.ShapeDtypeStruct(table, jnp.float32),
        ),
        slots,
        after(hits, last[1]),
        query_pool,
        owners,
        target_pool,
        pool_split,
        pool_other,
        pool_last,
        flops=1_000_000_000,
    )
    far_rest = after(far_rest, weights)
    two_blocks = [far_rest, *last]
    two = partial_similar(query, two_blocks)
    two_other = across(two, "rep")

    acc = add_up(
        ((0, 1), (1, 1), (2, 1), (4, 1)), acc_shape, after(one, two), one_other, *one_blocks
    )

    three_blocks = [near_rest, *last_rest]
    three = partial_similar(after(query, acc), three_blocks)
    three_other = across(three, "rep")
    acc = add_up(((5, 1), (6, 2)), acc_shape, after(two, three), two_other, *two_blocks, acc)
    profile, posterior = add_up(
        ((3, 1), (7, 2)),
        (
            jax.ShapeDtypeStruct(query.shape, jnp.bfloat16),
            jax.ShapeDtypeStruct((1, table[0]), jnp.float32),
        ),
        three,
        three_other,
        *three_blocks,
        acc,
        posterior,
    )
    return (profile[None], posterior)


def solution(mesh):
    placed = (
        P(("grp", "tgt", "qry"), None, "rep"),
        P(("grp", "tgt"), None, "rep"),
        P("grp"),
        P(("grp", "tgt", "qry"), None),
        P(("grp", "tgt", "qry")),
        P(("grp", "tgt", "qry"), None),
        P(("grp", "tgt"), None),
    )
    groups = mesh.shape["tgt"]

    def per_device(*arrays):
        query_res, target_res, _, hits = arrays[:4]
        few = (
            query_res.shape[0] == 1
            and groups == 4 <= hits.shape[1] // target_res.shape[0]
            and target_res.shape[0] == mesh.shape["qry"] == 2
            and mesh.shape["rep"] == 2
        )
        return (per_device_by_target if few else per_device_by_hit)(*arrays)

    return jax.shard_map(
        per_device,
        mesh=mesh,
        in_specs=placed,
        out_specs=(P(("grp", "tgt", "qry"), None, "rep"), P(("grp", "tgt", "qry"), None)),
        check_vma=False,
    )
```

```python
import functools
import math

import jax
import jax.numpy as jnp
from jax import lax
from jax.experimental import pallas as pl
from jax.experimental.pallas import tpu as pltpu
from jax.sharding import PartitionSpec as P

VMEM_BYTES = 16 * 1024 * 1024


def softmax_rows(logits):
    highest = jnp.max(logits, axis=-1, keepdims=True)
    raised = jnp.exp(logits - highest)
    return raised / jnp.sum(raised, axis=-1, keepdims=True)


def weigh_alignment(similar, lengths, sharpness, hit_weight):
    target_rows = similar.shape[-1]
    inside = jnp.arange(target_rows)[None, None, None, :] < lengths[:, :, None, None]
    counted = lengths[:, :, None, None].astype(jnp.float32)
    row_mean = jnp.sum(jnp.where(inside, similar, 0.0), axis=-1, keepdims=True) / counted
    row_diff = similar - row_mean
    row_var = jnp.sum(jnp.where(inside, row_diff * row_diff, 0.0), axis=-1, keepdims=True) / counted
    row_score = row_diff / jnp.sqrt(row_var + 1e-05)
    column_mean = jnp.mean(similar, axis=2, keepdims=True)
    column_diff = similar - column_mean
    column_var = jnp.mean(column_diff * column_diff, axis=2, keepdims=True)
    column_score = column_diff / jnp.sqrt(column_var + 1e-05)
    scores = sharpness[:, None, None, None] * (0.5 * (row_score + column_score))
    scores = jnp.where(inside, scores, -jnp.inf)
    alignment = softmax_rows(scores)
    return (hit_weight[:, :, None, None] * alignment).astype(jnp.bfloat16)


def plan_slots(flat_hits, owned_targets, tgt_count, capacity):
    owners = flat_hits // owned_targets
    local_ids = flat_hits % owned_targets
    matched = owners[:, None] == jnp.arange(tgt_count)[None, :]
    earlier = jnp.cumsum(matched.astype(jnp.int32), axis=0) - 1
    rank_in = jnp.sum(jnp.where(matched, earlier, 0), axis=1)
    slot_of = owners * capacity + rank_in
    placed = slot_of[:, None] == jnp.arange(tgt_count * capacity)[None, :]
    wanted = jnp.sum(jnp.where(placed, local_ids[:, None], 0), axis=0).reshape(tgt_count, capacity)
    return (wanted, slot_of)


def fetch_shares(target_res, flat_hits, capacity):
    tgt_count = lax.axis_size("tgt")
    owned_targets, target_rows, width = target_res.shape
    wanted, slot_of = plan_slots(flat_hits, owned_targets, tgt_count, capacity)
    requested = lax.all_to_all(wanted, "tgt", split_axis=0, concat_axis=0, tiled=True)
    outgoing = jnp.take(target_res, requested.reshape(tgt_count * capacity), axis=0)
    outgoing = outgoing.reshape(tgt_count, capacity, target_rows, width)
    arrived = lax.all_to_all(outgoing, "tgt", split_axis=0, concat_axis=0, tiled=True)
    return jnp.take(arrived.reshape(tgt_count * capacity, target_rows, width), slot_of, axis=0)


def per_device_by_hit(query_res, target_res, target_len, hits, sharpness, query_pool, target_pool):
    tgt_count = lax.axis_size("tgt")
    query_count = query_res.shape[0]
    target_rows = target_res.shape[1]
    hit_count = hits.shape[1]
    pair_count = query_count * hit_count
    model_width = query_pool.shape[1]
    capacity = max(2, (2 * pair_count + tgt_count - 1) // tgt_count)
    library = lax.all_gather(target_pool, "tgt", axis=0, tiled=True)
    logits = jnp.dot(query_pool, library.T, precision=lax.Precision.HIGHEST) / math.sqrt(
        model_width
    )
    posterior = softmax_rows(logits)
    matches = hits[:, :, None] == jnp.arange(library.shape[0])[None, None, :]
    hit_weight = softmax_rows(jnp.sum(jnp.where(matches, logits[:, None, :], 0.0), axis=-1))
    lengths = jnp.sum(jnp.where(matches, target_len[None, None, :], 0), axis=-1)
    half_width = query_res.shape[2]
    chosen = fetch_shares(target_res, hits.reshape(pair_count), capacity)
    chosen = chosen.reshape(query_count, hit_count, target_rows, half_width)
    partial_sim = jnp.einsum(
        "qid,qhjd->qhij", query_res, chosen, preferred_element_type=jnp.float32
    ) / math.sqrt(model_width)
    similar = lax.psum(partial_sim, "rep")
    weighted = weigh_alignment(similar, lengths, sharpness, hit_weight)
    profile = jnp.einsum("qhij,qhjd->qid", weighted, chosen, preferred_element_type=jnp.float32)
    return (profile.astype(jnp.bfloat16), posterior)


VMEM = pl.BlockSpec(memory_space=pltpu.VMEM)


def call_kernel(kernel, out_shape, *operands, scratch=(), flops=0):
    return pl.pallas_call(
        kernel,
        out_shape=out_shape,
        in_specs=[VMEM] * len(operands),
        out_specs=jax.tree.map(lambda _: VMEM, out_shape),
        scratch_shapes=scratch,
        cost_estimate=pl.CostEstimate(flops=flops, bytes_accessed=0, transcendentals=0),
        compiler_params=pltpu.CompilerParams(vmem_limit_bytes=VMEM_BYTES),
    )(*operands)


def weigh_kernel(slot_ref, hits_ref, pool_ref, owner_ref, *refs):
    libs, (posterior_ref, weight_ref) = refs[:-2], refs[-2:]
    owned, width = libs[0].shape
    target_count = posterior_ref.shape[0]
    target = lax.broadcasted_iota(jnp.int32, (target_count, 1), 0)
    counts = jnp.sum(jnp.where(hits_ref[...] == target, 1.0, 0.0), axis=1, keepdims=True)
    logits = jnp.zeros((target_count, 1), jnp.float32)
    for at, lib in enumerate(libs):
        products = jnp.sum(lib[...] * pool_ref[...], axis=1, keepdims=True) / math.sqrt(width)
        first = owner_ref[at : at + 1, 0:1] * owned
        for a in range(owned):
            logits = jnp.where(target == first + a, products[a : a + 1, :], logits)
    raised = jnp.exp(logits - jnp.max(logits, axis=0, keepdims=True))
    posterior = raised / jnp.sum(raised, axis=0, keepdims=True)
    shown = jnp.where(counts > 0.0, logits, -jnp.inf)
    parts = counts * jnp.exp(shown - jnp.max(shown, axis=0, keepdims=True))
    weights = parts / jnp.sum(parts, axis=0, keepdims=True)
    lane = lax.broadcasted_iota(jnp.int32, (1, target_count), 1)
    posterior_ref[...] = jnp.broadcast_to(posterior, posterior_ref.shape)
    weights = jnp.sum(jnp.where(target == lane, weights, 0.0), axis=0, keepdims=True)
    weights = jnp.where(slot_ref[:, 0:1] == lane, weights, 0.0)
    weights = jnp.sum(weights, axis=1, keepdims=True)
    weight_ref[...] = jnp.broadcast_to(weights, weight_ref.shape)


def partial_kernel(*refs):
    query, blocks, out = refs[0], refs[1:-1], refs[-1]
    out[...] = lax.dot_general(
        query[...],
        jnp.concatenate([block[...] for block in blocks]),
        (((1,), (1,)), ((), ())),
        preferred_element_type=jnp.float32,
    )


def partial_similar(query, blocks):
    rows = sum(block.shape[0] for block in blocks)
    shape = jax.ShapeDtypeStruct((query.shape[0], rows), jnp.float32)
    return call_kernel(partial_kernel, shape, query, *blocks)


def align_block(similar, length, half_sharp, weight):
    column = lax.broadcasted_iota(jnp.int32, (1, similar.shape[1]), 1).astype(jnp.float32)
    inside = column < length
    fraction = 1.0 / length[:, 0:1]
    row_mean = jnp.sum(jnp.where(inside, similar, 0.0), axis=1, keepdims=True) * fraction
    row_diff = similar - row_mean
    row_var = (
        jnp.sum(jnp.where(inside, row_diff * row_diff, 0.0), axis=1, keepdims=True) * fraction
    )
    column_mean = jnp.mean(similar, axis=0, keepdims=True)
    column_diff = similar - column_mean
    column_var = jnp.mean(column_diff * column_diff, axis=0, keepdims=True)
    scores = row_diff * (half_sharp * lax.rsqrt(row_var + 1e-05)) + column_diff * (
        half_sharp * lax.rsqrt(column_var + 1e-05)
    )
    scores = jnp.where(inside, scores, -jnp.inf)
    raised = jnp.exp(scores - jnp.max(scores, axis=1, keepdims=True))
    return raised * (weight / jnp.sum(raised, axis=1, keepdims=True))


def profile_kernel(model_width, targets, last, weight_ref, len_ref, sharp_ref, mine, other, *refs):
    blocks, out_ref = list(refs[:-1]), refs[-1]
    if last:
        posterior_ref, out_ref, posterior_out = blocks[-2], blocks[-1], out_ref
        blocks = blocks[:-2]
        count = posterior_out.shape[1]
        row = lax.broadcasted_iota(jnp.int32, (count, 1), 0)
        lane = lax.broadcasted_iota(jnp.int32, (1, count), 1)
        chosen = jnp.where(row == lane, posterior_ref[:, 0:1], 0.0)
        posterior_out[...] = jnp.sum(chosen, axis=0, keepdims=True)
    rows = mine.shape[1] // len(targets)
    weighted, rows_of = [], []
    for at, (slot, count) in enumerate(targets):
        part = pl.ds(at * rows, rows)
        similar = (mine[:, part] + other[:, part]) * (1.0 / math.sqrt(model_width))
        weight = weight_ref[slot : slot + 1, 0:1]
        aligned = align_block(similar, len_ref[slot : slot + 1, :rows], sharp_ref[:, 0:1], weight)
        weighted.append(aligned.astype(jnp.bfloat16))
        rows_of += [block[...] for block in blocks[:count]]
        blocks = blocks[count:]
    acc = jnp.dot(
        jnp.concatenate(weighted, axis=1),
        jnp.concatenate(rows_of),
        preferred_element_type=jnp.float32,
    )
    if blocks:
        acc += blocks[0][...]
    out_ref[...] = acc.astype(out_ref.dtype)


def per_device_by_target(
    query_res, target_res, target_len, hits, sharpness, query_pool, target_pool
):
    model_width = query_pool.shape[1]
    target_rows = target_res.shape[1]
    query = query_res[0]
    at_tgt, at_qry, at_rep = (lax.axis_index(name) for name in ("tgt", "qry", "rep"))

    def from_peer(array, k):
        return lax.ppermute(array, "tgt", [(i, i ^ k) for i in range(4)])

    def across(array, axis):
        return lax.ppermute(array, axis, [(0, 1), (1, 0)])

    def after(array, *done):
        return lax.optimization_barrier((array, *done))[0]

    split = [(2 * i + c, 2 * (i ^ (1 + c)) + c) for i in range(4) for c in range(2)]
    pool_split = lax.ppermute(target_pool, ("tgt", "rep"), split)
    pool_last = from_peer(target_pool, 3)
    pool_split = after(pool_split, pool_last)

    share = lax.dynamic_index_in_dim(target_res, at_qry, 0, keepdims=False)
    rest = lax.dynamic_index_in_dim(target_res, 1 - at_qry, 0, keepdims=False)
    far = from_peer(share, 2)
    near = from_peer(share, 1)

    bases = [2 * (at_tgt ^ k) for k in range(4)]
    slots = [bases[0], bases[0] + 1]
    for base in bases[1:]:
        slots += [base + at_qry, base + 1 - at_qry]
    owners = [at_tgt, at_tgt ^ (1 + at_rep), at_tgt ^ (2 - at_rep), at_tgt ^ 3]
    table = (len(target_len), target_rows)
    slots = jnp.broadcast_to(jnp.stack(slots)[:, None], table)
    owners = jnp.broadcast_to(jnp.stack(owners + owners)[:, None], table)
    named = slots[:, : table[0]] == jnp.arange(table[0])[None]
    lengths = jnp.sum(jnp.where(named, target_len[None], 0), axis=1, keepdims=True)
    lengths = jnp.broadcast_to(lengths.astype(jnp.float32), table)
    half_sharp = jnp.broadcast_to(0.5 * sharpness, (1, target_rows))

    def add_up(targets, out_shape, *operands):
        return call_kernel(
            functools.partial(profile_kernel, model_width, targets, isinstance(out_shape, tuple)),
            out_shape,
            weights,
            lengths,
            half_sharp,
            *operands,
        )

    acc_shape = jax.ShapeDtypeStruct(query.shape, jnp.float32)
    far = after(far, pool_split, pool_last, slots, owners, lengths, half_sharp)
    near = after(near, far)
    far = after(far, near)
    half = target_rows // 2
    last = [from_peer(far[:half], 1), from_peer(far[half:], 1)]
    pool_other = across(pool_split, "rep")
    near_rest = from_peer(after(rest, far), 1)

    one_blocks = [target_res[0], target_res[1], near, far]
    one = partial_similar(query, one_blocks)
    one_other = across(one, "rep")
    far_rest = across(after(far, one_other), "qry")
    last_rest = [across(piece, "qry") for piece in last]
    posterior, weights = call_kernel(
        weigh_kernel,
        (
            jax.ShapeDtypeStruct(table, jnp.float32),
            jax.ShapeDtypeStruct(table, jnp.float32),
        ),
        slots,
        after(hits, last[1]),
        query_pool,
        owners,
        target_pool,
        pool_split,
        pool_other,
        pool_last,
        flops=1_000_000_000,
    )
    far_rest = after(far_rest, weights)
    two_blocks = [far_rest, *last]
    two = partial_similar(query, two_blocks)
    two_other = across(two, "rep")

    acc = add_up(
        ((0, 1), (1, 1), (2, 1), (4, 1)), acc_shape, after(one, two), one_other, *one_blocks
    )

    three_blocks = [near_rest, *last_rest]
    three = partial_similar(after(query, acc), three_blocks)
    three_other = across(three, "rep")
    acc = add_up(((5, 1), (6, 2)), acc_shape, after(two, three), two_other, *two_blocks, acc)
    profile, posterior = add_up(
        ((3, 1), (7, 2)),
        (
            jax.ShapeDtypeStruct(query.shape, jnp.bfloat16),
            jax.ShapeDtypeStruct((1, table[0]), jnp.float32),
        ),
        three,
        three_other,
        *three_blocks,
        acc,
        posterior,
    )
    return (profile[None], posterior)


def solution(mesh):
    placed = (
        P(("grp", "tgt", "qry"), None, "rep"),
        P(("grp", "tgt"), None, "rep"),
        P("grp"),
        P(("grp", "tgt", "qry"), None),
        P(("grp", "tgt", "qry")),
        P(("grp", "tgt", "qry"), None),
        P(("grp", "tgt"), None),
    )
    groups = mesh.shape["tgt"]

    def per_device(*arrays):
        query_res, target_res, _, hits = arrays[:4]
        few = (
            query_res.shape[0] == 1
            and groups == 4 <= hits.shape[1] // target_res.shape[0]
            and target_res.shape[0] == mesh.shape["qry"] == 2
            and mesh.shape["rep"] == 2
        )
        return (per_device_by_target if few else per_device_by_hit)(*arrays)

    return jax.shard_map(
        per_device,
        mesh=mesh,
        in_specs=placed,
        out_specs=(P(("grp", "tgt", "qry"), None, "rep"), P(("grp", "tgt", "qry"), None)),
        check_vma=False,
    )
```

```python
import functools
import math

import jax
import jax.numpy as jnp
from jax import lax
from jax.experimental import pallas as pl
from jax.experimental.pallas import tpu as pltpu
from jax.sharding import PartitionSpec as P

VMEM_BYTES = 16 * 1024 * 1024


def softmax_rows(logits):
    highest = jnp.max(logits, axis=-1, keepdims=True)
    raised = jnp.exp(logits - highest)
    return raised / jnp.sum(raised, axis=-1, keepdims=True)


def weigh_alignment(similar, lengths, sharpness, hit_weight):
    target_rows = similar.shape[-1]
    inside = jnp.arange(target_rows)[None, None, None, :] < lengths[:, :, None, None]
    counted = lengths[:, :, None, None].astype(jnp.float32)
    row_mean = jnp.sum(jnp.where(inside, similar, 0.0), axis=-1, keepdims=True) / counted
    row_diff = similar - row_mean
    row_var = jnp.sum(jnp.where(inside, row_diff * row_diff, 0.0), axis=-1, keepdims=True) / counted
    row_score = row_diff / jnp.sqrt(row_var + 1e-05)
    column_mean = jnp.mean(similar, axis=2, keepdims=True)
    column_diff = similar - column_mean
    column_var = jnp.mean(column_diff * column_diff, axis=2, keepdims=True)
    column_score = column_diff / jnp.sqrt(column_var + 1e-05)
    scores = sharpness[:, None, None, None] * (0.5 * (row_score + column_score))
    scores = jnp.where(inside, scores, -jnp.inf)
    alignment = softmax_rows(scores)
    return (hit_weight[:, :, None, None] * alignment).astype(jnp.bfloat16)


def plan_slots(flat_hits, owned_targets, tgt_count, capacity):
    owners = flat_hits // owned_targets
    local_ids = flat_hits % owned_targets
    matched = owners[:, None] == jnp.arange(tgt_count)[None, :]
    earlier = jnp.cumsum(matched.astype(jnp.int32), axis=0) - 1
    rank_in = jnp.sum(jnp.where(matched, earlier, 0), axis=1)
    slot_of = owners * capacity + rank_in
    placed = slot_of[:, None] == jnp.arange(tgt_count * capacity)[None, :]
    wanted = jnp.sum(jnp.where(placed, local_ids[:, None], 0), axis=0).reshape(tgt_count, capacity)
    return (wanted, slot_of)


def fetch_shares(target_res, flat_hits, capacity):
    tgt_count = lax.axis_size("tgt")
    owned_targets, target_rows, width = target_res.shape
    wanted, slot_of = plan_slots(flat_hits, owned_targets, tgt_count, capacity)
    requested = lax.all_to_all(wanted, "tgt", split_axis=0, concat_axis=0, tiled=True)
    outgoing = jnp.take(target_res, requested.reshape(tgt_count * capacity), axis=0)
    outgoing = outgoing.reshape(tgt_count, capacity, target_rows, width)
    arrived = lax.all_to_all(outgoing, "tgt", split_axis=0, concat_axis=0, tiled=True)
    return jnp.take(arrived.reshape(tgt_count * capacity, target_rows, width), slot_of, axis=0)


def per_device_by_hit(query_res, target_res, target_len, hits, sharpness, query_pool, target_pool):
    tgt_count = lax.axis_size("tgt")
    query_count = query_res.shape[0]
    target_rows = target_res.shape[1]
    hit_count = hits.shape[1]
    pair_count = query_count * hit_count
    model_width = query_pool.shape[1]
    capacity = max(2, (2 * pair_count + tgt_count - 1) // tgt_count)
    library = lax.all_gather(target_pool, "tgt", axis=0, tiled=True)
    logits = jnp.dot(query_pool, library.T, precision=lax.Precision.HIGHEST) / math.sqrt(
        model_width
    )
    posterior = softmax_rows(logits)
    matches = hits[:, :, None] == jnp.arange(library.shape[0])[None, None, :]
    hit_weight = softmax_rows(jnp.sum(jnp.where(matches, logits[:, None, :], 0.0), axis=-1))
    lengths = jnp.sum(jnp.where(matches, target_len[None, None, :], 0), axis=-1)
    half_width = query_res.shape[2]
    chosen = fetch_shares(target_res, hits.reshape(pair_count), capacity)
    chosen = chosen.reshape(query_count, hit_count, target_rows, half_width)
    partial_sim = jnp.einsum(
        "qid,qhjd->qhij", query_res, chosen, preferred_element_type=jnp.float32
    ) / math.sqrt(model_width)
    similar = lax.psum(partial_sim, "rep")
    weighted = weigh_alignment(similar, lengths, sharpness, hit_weight)
    profile = jnp.einsum("qhij,qhjd->qid", weighted, chosen, preferred_element_type=jnp.float32)
    return (profile.astype(jnp.bfloat16), posterior)


VMEM = pl.BlockSpec(memory_space=pltpu.VMEM)


def call_kernel(kernel, out_shape, *operands, scratch=(), flops=0):
    return pl.pallas_call(
        kernel,
        out_shape=out_shape,
        in_specs=[VMEM] * len(operands),
        out_specs=jax.tree.map(lambda _: VMEM, out_shape),
        scratch_shapes=scratch,
        cost_estimate=pl.CostEstimate(flops=flops, bytes_accessed=0, transcendentals=0),
        compiler_params=pltpu.CompilerParams(vmem_limit_bytes=VMEM_BYTES),
    )(*operands)


def weigh_kernel(slot_ref, hits_ref, pool_ref, owner_ref, *refs):
    libs, (posterior_ref, weight_ref) = refs[:-2], refs[-2:]
    owned, width = libs[0].shape
    target_count = posterior_ref.shape[0]
    target = lax.broadcasted_iota(jnp.int32, (target_count, 1), 0)
    counts = jnp.sum(jnp.where(hits_ref[...] == target, 1.0, 0.0), axis=1, keepdims=True)
    logits = jnp.zeros((target_count, 1), jnp.float32)
    for at, lib in enumerate(libs):
        products = jnp.sum(lib[...] * pool_ref[...], axis=1, keepdims=True) / math.sqrt(width)
        first = owner_ref[at : at + 1, 0:1] * owned
        for a in range(owned):
            logits = jnp.where(target == first + a, products[a : a + 1, :], logits)
    raised = jnp.exp(logits - jnp.max(logits, axis=0, keepdims=True))
    posterior = raised / jnp.sum(raised, axis=0, keepdims=True)
    shown = jnp.where(counts > 0.0, logits, -jnp.inf)
    parts = counts * jnp.exp(shown - jnp.max(shown, axis=0, keepdims=True))
    weights = parts / jnp.sum(parts, axis=0, keepdims=True)
    lane = lax.broadcasted_iota(jnp.int32, (1, target_count), 1)
    posterior_ref[...] = jnp.broadcast_to(posterior, posterior_ref.shape)
    weights = jnp.sum(jnp.where(target == lane, weights, 0.0), axis=0, keepdims=True)
    weights = jnp.where(slot_ref[:, 0:1] == lane, weights, 0.0)
    weights = jnp.sum(weights, axis=1, keepdims=True)
    weight_ref[...] = jnp.broadcast_to(weights, weight_ref.shape)


def partial_kernel(*refs):
    query, blocks, out = refs[0], refs[1:-1], refs[-1]
    out[...] = lax.dot_general(
        query[...],
        jnp.concatenate([block[...] for block in blocks]),
        (((1,), (1,)), ((), ())),
        preferred_element_type=jnp.float32,
    )


def partial_similar(query, blocks):
    rows = sum(block.shape[0] for block in blocks)
    shape = jax.ShapeDtypeStruct((query.shape[0], rows), jnp.float32)
    return call_kernel(partial_kernel, shape, query, *blocks)


def align_block(similar, length, half_sharp, weight):
    column = lax.broadcasted_iota(jnp.int32, (1, similar.shape[1]), 1).astype(jnp.float32)
    inside = column < length
    fraction = 1.0 / length[:, 0:1]
    row_mean = jnp.sum(jnp.where(inside, similar, 0.0), axis=1, keepdims=True) * fraction
    row_diff = similar - row_mean
    row_var = (
        jnp.sum(jnp.where(inside, row_diff * row_diff, 0.0), axis=1, keepdims=True) * fraction
    )
    column_mean = jnp.mean(similar, axis=0, keepdims=True)
    column_diff = similar - column_mean
    column_var = jnp.mean(column_diff * column_diff, axis=0, keepdims=True)
    scores = row_diff * (half_sharp * lax.rsqrt(row_var + 1e-05)) + column_diff * (
        half_sharp * lax.rsqrt(column_var + 1e-05)
    )
    scores = jnp.where(inside, scores, -jnp.inf)
    raised = jnp.exp(scores - jnp.max(scores, axis=1, keepdims=True))
    return raised * (weight / jnp.sum(raised, axis=1, keepdims=True))


def profile_kernel(model_width, targets, last, weight_ref, len_ref, sharp_ref, mine, other, *refs):
    blocks, out_ref = list(refs[:-1]), refs[-1]
    if last:
        posterior_ref, out_ref, posterior_out = blocks[-2], blocks[-1], out_ref
        blocks = blocks[:-2]
        count = posterior_out.shape[1]
        row = lax.broadcasted_iota(jnp.int32, (count, 1), 0)
        lane = lax.broadcasted_iota(jnp.int32, (1, count), 1)
        chosen = jnp.where(row == lane, posterior_ref[:, 0:1], 0.0)
        posterior_out[...] = jnp.sum(chosen, axis=0, keepdims=True)
    rows = mine.shape[1] // len(targets)
    acc, weighted, rows_of = None, [], []
    for at, (slot, count) in enumerate(targets):
        part = pl.ds(at * rows, rows)
        similar = (mine[:, part] + other[:, part]) * (1.0 / math.sqrt(model_width))
        weight = weight_ref[slot : slot + 1, 0:1]
        aligned = align_block(similar, len_ref[slot : slot + 1, :rows], sharp_ref[:, 0:1], weight)
        weighted.append(aligned.astype(jnp.bfloat16))
        rows_of += [block[...] for block in blocks[:count]]
        blocks = blocks[count:]
        if at % 2 or at == len(targets) - 1:
            term = jnp.dot(
                jnp.concatenate(weighted, axis=1),
                jnp.concatenate(rows_of),
                preferred_element_type=jnp.float32,
            )
            acc = term if acc is None else acc + term
            weighted, rows_of = [], []
    if blocks:
        acc += blocks[0][...]
    out_ref[...] = acc.astype(out_ref.dtype)


def per_device_by_target(
    query_res, target_res, target_len, hits, sharpness, query_pool, target_pool
):
    model_width = query_pool.shape[1]
    target_rows = target_res.shape[1]
    query = query_res[0]
    at_tgt, at_qry, at_rep = (lax.axis_index(name) for name in ("tgt", "qry", "rep"))

    def from_peer(array, k):
        return lax.ppermute(array, "tgt", [(i, i ^ k) for i in range(4)])

    def across(array, axis):
        return lax.ppermute(array, axis, [(0, 1), (1, 0)])

    def after(array, *done):
        return lax.optimization_barrier((array, *done))[0]

    split = [(2 * i + c, 2 * (i ^ (1 + c)) + c) for i in range(4) for c in range(2)]
    pool_split = lax.ppermute(target_pool, ("tgt", "rep"), split)
    pool_last = from_peer(target_pool, 3)
    pool_split = after(pool_split, pool_last)

    share = lax.dynamic_index_in_dim(target_res, at_qry, 0, keepdims=False)
    rest = lax.dynamic_index_in_dim(target_res, 1 - at_qry, 0, keepdims=False)
    far = from_peer(share, 2)
    near = from_peer(share, 1)

    bases = [2 * (at_tgt ^ k) for k in range(4)]
    slots = [bases[0], bases[0] + 1]
    for base in bases[1:]:
        slots += [base + at_qry, base + 1 - at_qry]
    owners = [at_tgt, at_tgt ^ (1 + at_rep), at_tgt ^ (2 - at_rep), at_tgt ^ 3]
    table = (len(target_len), target_rows)
    slots = jnp.broadcast_to(jnp.stack(slots)[:, None], table)
    owners = jnp.broadcast_to(jnp.stack(owners + owners)[:, None], table)
    named = slots[:, : table[0]] == jnp.arange(table[0])[None]
    lengths = jnp.sum(jnp.where(named, target_len[None], 0), axis=1, keepdims=True)
    lengths = jnp.broadcast_to(lengths.astype(jnp.float32), table)
    half_sharp = jnp.broadcast_to(0.5 * sharpness, (1, target_rows))

    def add_up(targets, out_shape, *operands):
        return call_kernel(
            functools.partial(profile_kernel, model_width, targets, isinstance(out_shape, tuple)),
            out_shape,
            weights,
            lengths,
            half_sharp,
            *operands,
        )

    acc_shape = jax.ShapeDtypeStruct(query.shape, jnp.float32)
    far = after(far, pool_split, pool_last, slots, owners, lengths, half_sharp)
    near = after(near, far)
    far = after(far, near)
    half = target_rows // 2
    last = [from_peer(far[:half], 1), from_peer(far[half:], 1)]
    pool_other = across(pool_split, "rep")
    near_rest = from_peer(after(rest, far), 1)

    one_blocks = [target_res[0], target_res[1], near, far]
    one = partial_similar(query, one_blocks)
    one_other = across(one, "rep")
    far_rest = across(after(far, one_other), "qry")
    last_rest = [across(piece, "qry") for piece in last]
    posterior, weights = call_kernel(
        weigh_kernel,
        (
            jax.ShapeDtypeStruct(table, jnp.float32),
            jax.ShapeDtypeStruct(table, jnp.float32),
        ),
        slots,
        after(hits, last[1]),
        query_pool,
        owners,
        target_pool,
        pool_split,
        pool_other,
        pool_last,
        flops=1_000_000_000,
    )
    far_rest = after(far_rest, weights)
    two_blocks = [far_rest, *last]
    two = partial_similar(query, two_blocks)
    two_other = across(two, "rep")

    acc = add_up(
        ((0, 1), (1, 1), (2, 1), (4, 1)), acc_shape, after(one, two), one_other, *one_blocks
    )

    three_blocks = [near_rest, *last_rest]
    three = partial_similar(after(query, acc), three_blocks)
    three_other = across(three, "rep")
    acc = add_up(((5, 1), (6, 2)), acc_shape, after(two, three), two_other, *two_blocks, acc)
    profile, posterior = add_up(
        ((3, 1), (7, 2)),
        (
            jax.ShapeDtypeStruct(query.shape, jnp.bfloat16),
            jax.ShapeDtypeStruct((1, table[0]), jnp.float32),
        ),
        three,
        three_other,
        *three_blocks,
        acc,
        posterior,
    )
    return (profile[None], posterior)


def solution(mesh):
    placed = (
        P(("grp", "tgt", "qry"), None, "rep"),
        P(("grp", "tgt"), None, "rep"),
        P("grp"),
        P(("grp", "tgt", "qry"), None),
        P(("grp", "tgt", "qry")),
        P(("grp", "tgt", "qry"), None),
        P(("grp", "tgt"), None),
    )
    groups = mesh.shape["tgt"]

    def per_device(*arrays):
        query_res, target_res, _, hits = arrays[:4]
        few = (
            query_res.shape[0] == 1
            and groups == 4 <= hits.shape[1] // target_res.shape[0]
            and target_res.shape[0] == mesh.shape["qry"] == 2
            and mesh.shape["rep"] == 2
        )
        return (per_device_by_target if few else per_device_by_hit)(*arrays)

    return jax.shard_map(
        per_device,
        mesh=mesh,
        in_specs=placed,
        out_specs=(P(("grp", "tgt", "qry"), None, "rep"), P(("grp", "tgt", "qry"), None)),
        check_vma=False,
    )
```
